32 devices in a mesh: tower: 2 (over core), batch: 16 (over z, y, x).
Axes of the slice: x: 2, y: 2, z: 4, core: 2. Of those that a mesh axis runs over, the one named last changes fastest.
Arguments:
- states: bfloat16 [2, 96, 256, 768], P('tower', 'batch'), may hold values from -6 to 6
- q_lengths: int32 [96, 4], P('batch'), may hold values from 1 to 64, as said below
- dataset_ids: int32 [96], replicated, may hold values from 0 to 3
- positives: int32 [384], P('batch'), may hold values from 0 to 95
- w_qkv: bfloat16 [2, 768, 2304], P('tower', 'batch'), may hold values from -0.21875 to 0.21875
- w_out: bfloat16 [2, 768, 768], P('tower', 'batch'), may hold values from -1.75 to 1.75
- w_in: bfloat16 [2, 768, 3072], P('tower', 'batch'), may hold values from -0.21875 to 0.21875
- w_back: bfloat16 [2, 3072, 768], P('tower', 'batch'), may hold values from -0.109375 to 0.109375
- gain_first: bfloat16 [2, 768], P('tower', 'batch'), may hold values from 0.5 to 1.5
- bias_first: bfloat16 [2, 768], P('tower', 'batch'), may hold values from -1.5 to 1.5
- gain_second: bfloat16 [2, 768], P('tower', 'batch'), may hold values from 0.5 to 1.5
- bias_second: bfloat16 [2, 768], P('tower', 'batch'), may hold values from -1.5 to 1.5
Outputs:
- loss: float32 [], replicated
- encoded: bfloat16 [2, 96, 256, 768], P('tower', 'batch')
- states_grad: float32 [2, 96, 256, 768], P('tower', 'batch')
- grad_qkv: float32 [2, 768, 2304], P('tower', 'batch')
- grad_out: float32 [2, 768, 768], P('tower', 'batch')
- grad_in: float32 [2, 768, 3072], P('tower', 'batch')
- grad_back: float32 [2, 3072, 768], P('tower', 'batch')
- grad_gain_first: float32 [2, 768], P('tower', 'batch')
- grad_bias_first: float32 [2, 768], P('tower', 'batch')
- grad_gain_second: float32 [2, 768], P('tower', 'batch')
- grad_bias_second: float32 [2, 768], P('tower', 'batch')
The draws below stay inside these ranges and needn't reach their ends.
Inputs may be any that keep to these rules, and one draw needn't show every extreme that they name: `q_lengths`: every row of 4 questions holds one question of length 64.
All inputs are finite; a program needn't handle non-finite values.
Results may differ from the reference program's by a relative error of at most 0.017.
Values may be sent and summed in bfloat16 or wider, within the bound.
No kernel may reach another device: no remote copies, remote signals or barrier semaphores. Data moves between devices by JAX's collectives and lax.ppermute only.
A program may use at most 192 MiB of HBM per device.

```python
import math
import jax
import jax.numpy as jnp
from jax import lax

D = 768
HEADS = 12
HEAD = 64
FF = 3072
SEQ_LEN = 256
QLEN = 64
DATASETS = 4
SLOTS = 4
SEQS = 96
PASSAGES = 96
QUESTIONS = 384


def draw_q_lengths(key, part):
    key = jax.random.fold_in(key, 11)
    first_key, second_key = jax.random.split(key)
    drawn = jax.random.randint(first_key, (SEQS, SLOTS), 1, QLEN + 1)
    full_slot = jax.random.randint(second_key, (SEQS, 1), 0, SLOTS)
    slot_index = jnp.arange(SLOTS, dtype=jnp.int32)[None]
    return jnp.where(slot_index == full_slot, QLEN, drawn).astype(jnp.int32)


def with_ends(values, own_key, smallest, high):
    spot = [jax.random.randint(jax.random.fold_in(own_key, axis), (), 0, length) for axis, length in enumerate(values.shape)]
    widest = values.shape.index(max(values.shape))
    next_to = spot[:widest] + [(spot[widest] + 1) % values.shape[widest]] + spot[widest + 1:]
    return values.at[tuple(spot)].set(smallest).at[tuple(next_to)].set(high)


def steps_of(key, extent, cuts, low, largest):
    def one(axis_at, shards_of):
        steps = jax.random.uniform(jax.random.fold_in(jax.random.fold_in(key, 6), axis_at), (shards_of,), jnp.float32, low / len(cuts), largest / len(cuts))
        return jnp.repeat(jnp.exp(steps), extent[axis_at] // shards_of).reshape((-1,) + (1,) * (len(extent) - axis_at - 1))

    factor_of = one(*cuts[0])
    for cut in cuts[1:]:
        factor_of = factor_of * one(*cut)
    return factor_of


def centred(rng, dims, width, reach, shards=(), held_as=jnp.bfloat16):
    loudness = steps_of(rng, dims, shards, -0.22, 0.18) if shards else 1.0
    values = jax.random.normal(rng, dims, jnp.float32) * width * loudness
    return jnp.minimum(jnp.maximum(values, -reach), reach).astype(held_as)


def setup_inputs(seed: int = 0) -> dict:
    keys = jax.random.split(jax.random.key(seed), 13)
    states = centred(keys[0], (2, SEQS, SEQ_LEN, D), 1.0, 6.0, ((0, 2), (1, 16)))
    q_lengths = draw_q_lengths(jax.random.fold_in(keys[12], 71), 0)
    dataset_ids = with_ends(jax.random.randint(keys[2], (PASSAGES,), 0, DATASETS), jax.random.fold_in(keys[2], 1), 0, DATASETS - 1).astype(jnp.int32)
    positives = with_ends(jax.random.randint(keys[3], (QUESTIONS,), 0, PASSAGES), jax.random.fold_in(keys[3], 1), 0, PASSAGES - 1).astype(jnp.int32)
    w_qkv = centred(keys[4], (2, D, 3 * D), D ** -0.5, 0.21875, ((0, 2), (1, 16)))
    w_out = centred(keys[5], (2, D, D), (D // 64) ** -0.5, 1.75, ((0, 2), (1, 16)))
    w_in = centred(keys[6], (2, D, FF), D ** -0.5, 0.21875, ((0, 2), (1, 16)))
    w_back = centred(keys[7], (2, FF, D), FF ** -0.5, 0.109375, ((0, 2), (1, 16)))
    gain_first = jnp.clip(1.0 + 0.1 * jax.random.normal(keys[8], (2, D), jnp.float32), 0.5, 1.5).astype(jnp.bfloat16)
    bias_first = centred(keys[9], (2, D), 0.3, 1.5, ((0, 2), (1, 16)))
    gain_second = jnp.clip(1.0 + 0.1 * jax.random.normal(keys[10], (2, D), jnp.float32), 0.5, 1.5).astype(jnp.bfloat16)
    bias_second = centred(keys[11], (2, D), 0.3, 1.5, ((0, 2), (1, 16)))
    return {"states": states, "q_lengths": q_lengths, "dataset_ids": dataset_ids, "positives": positives, "w_qkv": w_qkv, "w_out": w_out, "w_in": w_in, "w_back": w_back, "gain_first": gain_first, "bias_first": bias_first, "gain_second": gain_second, "bias_second": bias_second}


exact_mode = lax.Precision.HIGHEST

@jax.custom_vjp
def low(v):
    return lax.optimization_barrier(v.astype(jnp.bfloat16)).astype(jnp.float32)

@jax.custom_vjp
def low_back(v):
    return v

def low_keep(v):
    return (low(v), None)

def low_pass(kept, grad):
    return (grad,)

def back_keep(v):
    return (v, None)

def back_low(kept, grad):
    return (low(grad),)
low.defvjp(low_keep, low_pass)
low_back.defvjp(back_keep, back_low)

def norm_rows(summed, gain, shift):
    center = summed - lax.optimization_barrier(jnp.mean(summed, axis=-1, keepdims=True))
    spread = lax.optimization_barrier(jnp.mean(center * center, axis=-1, keepdims=True))
    return center * lax.rsqrt(spread + 1e-05) * gain + shift

def gelu_exact(values):
    return jax.nn.gelu(values, approximate=False)

def key_valid(lengths, asking):
    position = jnp.arange(SEQ_LEN, dtype=jnp.int32)
    slot_of = position // QLEN
    within = position % QLEN
    hit = slot_of[None, :] == jnp.arange(SLOTS, dtype=jnp.int32)[:, None]
    limit = lax.optimization_barrier(jnp.sum(jnp.where(hit[None], lengths[:, :, None], 0), axis=1))
    open_key = within[None] < limit
    same_slot = slot_of[:, None] == slot_of[None]
    return same_slot[None] & open_key[:, None, :] | jnp.logical_not(asking)

def encoder(inputs, params, valid):
    w_qkv, w_out, w_in, w_back, gain_one, shift_one, gain_two, shift_two = params
    count = inputs.shape[0]
    mixed = jnp.einsum('gld,de->gle', inputs, w_qkv, precision=exact_mode)
    query = low_back(low(mixed[..., :D])).reshape(count, SEQ_LEN, HEADS, HEAD)
    keyset = low_back(low(mixed[..., D:2 * D])).reshape(count, SEQ_LEN, HEADS, HEAD)
    valset = low_back(low(mixed[..., 2 * D:])).reshape(count, SEQ_LEN, HEADS, HEAD)
    raw = jnp.einsum('gqhe,gkhe->ghqk', query, keyset, precision=exact_mode) * (1.0 / math.sqrt(HEAD))
    score = jnp.where(valid[:, None], low_back(raw), -1000000000.0)
    probs = jax.nn.softmax(score, axis=-1)
    context = low_back(low(jnp.einsum('ghqk,gkhe->gqhe', low(probs), valset, precision=exact_mode)))
    attended = low_back(jnp.einsum('gld,de->gle', context.reshape(count, SEQ_LEN, D), w_out, precision=exact_mode))
    first = norm_rows(inputs + attended, gain_one, shift_one)
    upward = low_back(jnp.einsum('gld,df->glf', low(first), w_in, precision=exact_mode))
    downward = low_back(jnp.einsum('glf,fd->gld', low(gelu_exact(upward)), w_back, precision=exact_mode))
    return norm_rows(first + downward, gain_two, shift_two)

def run_tower(tower_states, params, lengths, asking):
    group = math.gcd(SEQS, max(1, 4096 // SEQ_LEN))
    blocks = tower_states.reshape(SEQS // group, group, SEQ_LEN, D)
    length_blocks = lengths.reshape(SEQS // group, group, SLOTS)

    def one_block(pair):
        return encoder(pair[0], params, key_valid(pair[1], asking))
    return lax.map(jax.checkpoint(one_block), (blocks, length_blocks)).reshape(SEQS, SEQ_LEN, D)

def reference(states, q_lengths, dataset_ids, positives, w_qkv, w_out, w_in, w_back, gain_first, bias_first, gain_second, bias_second):
    inputs = states.astype(jnp.float32)
    params = tuple((item.astype(jnp.float32) for item in (w_qkv, w_out, w_in, w_back, gain_first, bias_first, gain_second, bias_second)))

    def objective(tower_inputs, weights):
        towers = []
        for tower in range(2):
            tower_params = tuple((item[tower] for item in weights))
            towers.append(run_tower(tower_inputs[tower], tower_params, q_lengths, tower == 0))
        asked = low(towers[0].reshape(SEQS, SLOTS, QLEN, D)[:, :, 0].reshape(QUESTIONS, D))
        passage_heads = low(towers[1][:, 0])
        logits = jnp.dot(asked, passage_heads.T, precision=exact_mode) * (2.0 / math.sqrt(D))
        chosen = positives[:, None] == jnp.arange(PASSAGES, dtype=jnp.int32)[None]
        asked_data = lax.optimization_barrier(jnp.sum(jnp.where(chosen, dataset_ids[None], 0), axis=1))
        same_data = asked_data[:, None] == dataset_ids[None]
        masked = jnp.where(same_data, logits, -1000000000.0)
        highest = lax.optimization_barrier(jnp.max(masked, axis=1, keepdims=True))
        log_total = highest[:, 0] + jnp.log(lax.optimization_barrier(jnp.sum(jnp.exp(masked - highest), axis=1)))
        target = lax.optimization_barrier(jnp.sum(jnp.where(chosen, logits, 0.0), axis=1))
        loss_value = jnp.mean(log_total - target)
        return (loss_value, jnp.stack(towers))
    loss_value, back_fn, final_states = jax.vjp(objective, inputs, params, has_aux=True)
    encoded = final_states.astype(jnp.bfloat16)
    grad_states, grad_params = back_fn(jnp.ones_like(loss_value))
    return (loss_value, encoded, grad_states, grad_params[0], grad_params[1], grad_params[2], grad_params[3], grad_params[4], grad_params[5], grad_params[6], grad_params[7])
```

```python
import functools
import math

import jax
import jax.numpy as jnp
from jax import lax
from jax.experimental import pallas as pl
from jax.experimental.pallas import tpu as pltpu
from jax.sharding import PartitionSpec as P

D = 768
HEADS = 12
HEAD = 64
FF = 3072
SEQ_LEN = 256
QLEN = 64
SLOTS = 4
EPS = 1e-05
NEG = -1000000000.0
BF = jnp.bfloat16
F32 = jnp.float32
MIB = 1 << 20
HEAD_SCALE = 1.0 / math.sqrt(HEAD)
LOGIT_SCALE = 2.0 / math.sqrt(D)
CHUNKS = FF // D
VMEM = pl.BlockSpec(memory_space=pltpu.VMEM)
SMEM = pl.BlockSpec(memory_space=pltpu.SMEM)
ANY = pl.BlockSpec(memory_space=pl.ANY)


def dot(a, b):
    return lax.dot_general(a, b, (((1,), (0,)), ((), ())), preferred_element_type=F32)


def dot_nt(a, b):
    return lax.dot_general(a, b, (((1,), (1,)), ((), ())), preferred_element_type=F32)


def dot_tn(a, b):
    return lax.dot_general(a, b, (((0,), (0,)), ((), ())), preferred_element_type=F32)


def iota(shape, axis):
    return lax.broadcasted_iota(jnp.int32, shape, axis)


def normalise(summed):
    center = summed - jnp.mean(summed, axis=-1, keepdims=True)
    spread = jnp.mean(center * center, axis=-1, keepdims=True)
    scale = lax.rsqrt(spread + EPS)
    return center * scale, scale


def normalise_back(grad, hat, scale, gain):
    d_hat = grad * gain
    mean_d = jnp.mean(d_hat, axis=-1, keepdims=True)
    mean_dh = jnp.mean(d_hat * hat, axis=-1, keepdims=True)
    d_gain = jnp.sum(grad * hat, axis=0, keepdims=True)
    d_shift = jnp.sum(grad, axis=0, keepdims=True)
    return scale * (d_hat - mean_d - hat * mean_dh), d_gain, d_shift


def normal_cdf(values):
    return 0.5 * (1.0 + lax.erf(values * math.sqrt(0.5)))


def gelu(values):
    return values * normal_cdf(values)


def gelu_pair(values):
    cdf = normal_cdf(values)
    bell = jnp.exp(-0.5 * values * values) * (1.0 / math.sqrt(2.0 * math.pi))
    return values * cdf, cdf + values * bell


class Links:
    def __init__(self):
        def table(move):
            at = lambda z, y, x: z * 4 + y * 2 + x
            return [
                (at(z, y, x), at(*move(z, y, x)))
                for z in range(4)
                for y in range(2)
                for x in range(2)
            ]

        self.x = table(lambda z, y, x: (z, y, 1 - x))
        self.y = table(lambda z, y, x: (z, 1 - y, x))
        self.z = [table(lambda z, y, x, c=c: ((z + c) % 4, y, x)) for c in range(4)]
        me = lax.axis_index("batch")
        self.at = (me // 4, me // 2 % 2, me % 2)


def move(value, pairs):
    return lax.ppermute(value, "batch", pairs)


def after(value, *earlier):
    late = sum(other[(0,) * other.ndim].astype(F32) for other in earlier) > 1e30
    return jnp.where(late, jnp.zeros_like(value), value)


ORDER = (0, 1, 3, 2)


def gather_line(links, shard):
    return [shard] + [move(shard, links.z[c]) for c in ORDER[1:]]


def gather_plane(links, line):
    near = [(block, move(block, links.x), move(block, links.y)) for block in line]
    pieces = []
    for k, (block, by_x, by_y) in enumerate(near):
        far = move(by_x, links.y) if k % 2 == 0 else move(by_y, links.x)
        pieces += [block, by_x, by_y, far]
    return pieces


def piece_places(links):
    z, y, x = links.at
    place = lambda c, dy, dx: (z - c + 4) % 4 * 4 + (y ^ dy) * 2 + (x ^ dx)
    order = [(c, dy, dx) for c in ORDER for dy in range(2) for dx in range(2)]
    return jnp.stack([place(*at) for at in order]).astype(jnp.int32)


class Gathered:
    def __init__(self, pieces, place):
        self.pieces = [piece[None] for piece in pieces]
        self.place = place
        self.blocks = place.shape[0]

    def whole(self):
        return self.pieces[0][0]


def gather_whole(shard):
    whole = lax.all_gather(shard, "batch", axis=0, tiled=True)
    return Gathered([whole], jnp.zeros((1,), jnp.int32))


def gather_rows(links, rows, cut):
    if links is None:
        full = lax.all_gather(rows, "batch", axis=0, tiled=True)
        return full[:, :cut], full[:, cut:]
    z, y, x = links.at
    count, width = rows.shape
    zs = [rows] + [move(rows, links.z[c]) for c in (1, 2, 3)]
    line = jnp.concatenate([zs[3], zs[2], zs[1], zs[0], zs[3], zs[2], zs[1]])
    line = lax.dynamic_slice(line, ((3 - z) * count, 0), (4 * count, width))
    left, right = line[:, :cut], line[:, cut:]

    def both(part, pairs, at):
        other = move(part, pairs)
        return jnp.where(at == 0, jnp.stack([part, other]), jnp.stack([other, part]))

    left = both(both(left, links.x, x), links.y, y)
    right = both(both(right, links.y, y), links.x, x)
    left = left.reshape(2, 2, 4, count, cut).transpose(2, 0, 1, 3, 4)
    right = right.reshape(2, 2, 4, count, width - cut).transpose(2, 1, 0, 3, 4)
    return left.reshape(16 * count, cut), right.reshape(16 * count, width - cut)


def low_sum(a, b):
    return (a.astype(F32) + b.astype(F32)).astype(BF)


def load(group, target, sems, low=0):
    place, pieces = group
    copies = []
    for piece in pieces:
        for c in range(piece.shape[0]):
            k = len(copies)
            unit = piece.shape[1]
            row = pl.multiple_of(place[k] * unit, unit)
            copies.append(
                pltpu.make_async_copy(
                    piece.at[c, :, pl.ds(low, target.shape[1])],
                    target.at[pl.ds(row, unit), :],
                    sems.at[k],
                )
            )
    for copy in copies:
        copy.start()
    return copies


def wait_all(copies):
    for copy in copies:
        copy.wait()


def launch(
    kernel, ins, weights, outs, scratch, room, grid=None, flops=0, moved=0, same=None, behind=()
):
    values = list(ins)
    for weight in weights:
        values += [(weight.place, SMEM)] + [(piece, ANY) for piece in weight.pieces]
    values += [(value, ANY) for value in behind]

    def run(*refs):
        at = len(ins)
        groups = []
        for weight in weights:
            end = at + 1 + len(weight.pieces)
            groups.append((refs[at], refs[at + 1 : end]))
            at = end
        at += len(behind)
        kernel(refs[: len(ins)], groups, refs[at : at + len(outs)], refs[at + len(outs) :])

    extra = {} if grid is None else {"grid": grid}
    return pl.pallas_call(
        run,
        name=getattr(kernel, "func", kernel).__name__,
        input_output_aliases=same or {},
        in_specs=[spec for _, spec in values],
        out_specs=[spec for _, _, spec in outs],
        out_shape=[jax.ShapeDtypeStruct(shape, dtype) for shape, dtype, _ in outs],
        scratch_shapes=scratch,
        compiler_params=pltpu.CompilerParams(vmem_limit_bytes=room * MIB),
        cost_estimate=pl.CostEstimate(
            flops=int(flops), bytes_accessed=int(moved), transcendentals=0
        ),
        **extra,
    )(*[value for value, _ in values])


def sems(*shape):
    return pltpu.SemaphoreType.DMA(shape)


def rows_spec(many, *tail, skip=0):
    return pl.BlockSpec((many,) + tail, lambda r: (r + skip,) + (0,) * len(tail))


def open_keys(shape, key_axis, row, slot_of_query, lens, ask):
    key_at = iota(shape, key_axis)
    slot = key_at >> 6
    limit = jnp.zeros(shape, jnp.int32)
    for s in range(SLOTS):
        limit = jnp.where(slot == s, lens[row, s] * ask + QLEN * (1 - ask), limit)
    return ((key_at & (QLEN - 1)) < limit) & (slot_of_query * ask == slot * ask)


def mix(skip, ins, groups, outs, scratch):
    lens, asking, x_ref = ins[:3]
    query_ref, key_ref, value_ref, context_ref = outs[:4]
    w, w_gain, w_turned, sem = scratch
    row = pl.program_id(0) + skip

    @pl.when(pl.program_id(0) == 0)
    def _():
        copies = load(groups[0], w, sem.at[0])
        if len(outs) > 4:
            wait_all(load(groups[0], w_gain, sem.at[1], 4 * D))
            outs[4][...] = w_gain[...].astype(F32).T[:8]
        wait_all(copies)
        for j in range(0, D, 128):
            part = w[:, 2 * D + j : 2 * D + j + 128].astype(F32)
            w_turned[j : j + 128, :] = part.T.astype(BF)

    x = x_ref[0]
    mixed = dot(x, w[:, : 2 * D])
    for s in range(SLOTS):
        query_ref[0, s : s + 1, :] = mixed[s * QLEN : s * QLEN + 1, :D]
    query = (mixed[:, :D] * HEAD_SCALE).astype(BF)
    keyset = mixed[:, D:].astype(BF)
    values = dot_nt(w_turned[...], x).astype(BF)
    key_ref[0] = keyset
    value_ref[0] = values
    shape = (SEQ_LEN, SEQ_LEN)
    closed = jnp.where(open_keys(shape, 0, row, iota(shape, 1) >> 6, lens, asking[0]), 0, 1) == 1
    ones = jnp.ones((16, SEQ_LEN), BF)
    nothing = jnp.zeros((SEQ_LEN, 128), BF)
    half_of = iota((SEQ_LEN, 128), 1) // HEAD
    scores = []
    for head in range(HEADS):
        low = head // 2 * 128
        mine = jnp.where(half_of == head % 2, query[:, low : low + 128], nothing)
        scores.append(dot_nt(keyset[:, low : low + 128], mine))
    expos = []
    for score in scores:
        score = jnp.where(closed, NEG, score)
        expos.append(jnp.exp(score - jnp.max(score, axis=0, keepdims=True)).astype(BF))
    parts = []
    for head, expo in enumerate(expos):
        mine = values[head * HEAD : head * HEAD + HEAD]
        summed = dot(jnp.concatenate([mine, ones], axis=0), expo)
        parts.append(summed[:HEAD] / summed[HEAD : HEAD + 1])
    context_ref[0] = jnp.concatenate(parts, axis=0).T.astype(BF)


def up(ins, groups, outs, scratch):
    x_ref, context_ref, gains = ins
    first_ref, act_ref = outs
    w_out, w_in, sem = scratch

    @pl.when(pl.program_id(0) == 0)
    def _():
        wait_all(load(groups[0], w_out, sem.at[0], 3 * D) + load(groups[1], w_in, sem.at[1]))

    many = x_ref.shape[0] * SEQ_LEN
    attended = dot(context_ref[...].reshape(many, D), w_out[...])
    summed = x_ref[...].reshape(many, D).astype(F32) + attended
    first = normalise(summed)[0] * gains[0:1] + gains[1:2]
    low = first.astype(BF)
    first_ref[...] = low.reshape(first_ref.shape)
    for j in range(CHUNKS):
        part = gelu(dot(low, w_in[:, j * D : j * D + D])).astype(BF)
        act_ref[:, :, j * D : j * D + D] = part.reshape(act_ref.shape[0], SEQ_LEN, D)


def down(ins, groups, outs, scratch):
    first_ref, act_ref, gains = ins
    (encoded_ref,) = outs
    w_back, sem = scratch

    @pl.when(pl.program_id(0) == 0)
    def _():
        wait_all(load(groups[0], w_back, sem))

    many = first_ref.shape[0] * SEQ_LEN
    summed = dot(act_ref[...].reshape(many, FF), w_back[...])
    hat = normalise(first_ref[...].reshape(many, D).astype(F32) + summed)[0]
    encoded_ref[...] = (hat * gains[2:3] + gains[3:4]).astype(BF).reshape(encoded_ref.shape)


def head_up_math(context, picked, gains, w_out, w_in, emit):
    hat, scale = normalise(picked.astype(F32) + dot(context, w_out))
    low = (hat * gains[0:1] + gains[1:2]).astype(BF)
    for j in range(CHUNKS):
        act, slope = gelu_pair(dot(low, w_in(j)))
        emit(j, act.astype(BF), slope.astype(BF))
    return hat, scale, low


def head_up(ins, groups, outs, scratch):
    context_ref, picked_ref, gains = ins
    hat_ref, scale_ref, low_ref, act_ref, slope_ref = outs
    w_out, w_in, sem = scratch
    wait_all(load(groups[0], w_out, sem.at[0], 3 * D) + load(groups[1], w_in, sem.at[1]))

    def emit(j, act, slope):
        act_ref[:, j * D : j * D + D] = act
        slope_ref[:, j * D : j * D + D] = slope

    hat, scale, low = head_up_math(
        context_ref[...],
        picked_ref[...],
        gains[...],
        w_out[...],
        lambda j: w_in[:, j * D : j * D + D],
        emit,
    )
    hat_ref[...] = hat
    scale_ref[...] = jnp.broadcast_to(scale, scale_ref.shape)
    low_ref[...] = low


def head_down_math(hat, gains, act, w_back):
    hat2, scale2 = normalise(hat * gains[0:1] + gains[1:2] + dot(act, w_back))
    return hat2, scale2, (hat2 * gains[2:3] + gains[3:4]).astype(BF)


def head_down(ins, groups, outs, scratch):
    hat_ref, act_ref, gains = ins
    hat2_ref, scale2_ref, final_ref = outs
    w_back, sem = scratch
    wait_all(load(groups[0], w_back, sem))
    hat2, scale2, final = head_down_math(hat_ref[...], gains[...], act_ref[...], w_back[...])
    hat2_ref[...] = hat2
    scale2_ref[...] = jnp.broadcast_to(scale2, scale2_ref.shape)
    final_ref[...] = final


def logit_back(asked, passages, positives, ids, place_of):
    logits = dot_nt(asked, passages) * LOGIT_SCALE
    chosen = positives == place_of
    asked_data = jnp.sum(jnp.where(chosen, ids, 0.0), axis=1, keepdims=True)
    open_to = (asked_data == ids) & (place_of >= 0)
    masked = jnp.where(open_to, logits, NEG)
    highest = jnp.max(masked, axis=1, keepdims=True)
    expo = jnp.exp(masked - highest)
    total = jnp.sum(expo, axis=1, keepdims=True)
    target = jnp.sum(jnp.where(chosen, logits, 0.0), axis=1, keepdims=True)
    loss = jnp.sum(highest + jnp.log(total) - target, axis=0, keepdims=True) / asked.shape[0]
    d_logits = (expo / total - jnp.where(chosen, 1.0, 0.0)) * (LOGIT_SCALE / asked.shape[0])
    return loss, d_logits


def dot_split(a, b):
    high = a.astype(BF)
    return dot(high, b) + dot((a - high.astype(F32)).astype(BF), b)


def back_math(d_final, hat2, scale2, hat, scale, gains, slope, w_out, w_in, w_back, emit):
    d_second, d_gain2, d_shift2 = normalise_back(d_final, hat2, scale2, gains[2:3])
    d_down = d_second.astype(BF)
    d_first = d_second
    for j in range(CHUNKS):
        d_up = (dot_nt(d_down, w_back(j)) * slope(j).astype(F32)).astype(BF)
        emit(j, d_up)
        d_first = d_first + dot_nt(d_up, w_in(j))
    d_sum, d_gain, d_shift = normalise_back(d_first, hat, scale, gains[0:1])
    d_att = d_sum.astype(BF)
    d_context = None if w_out is None else dot_nt(d_att, w_out())
    return d_down, d_sum, d_att, d_context, (d_gain, d_shift, d_gain2, d_shift2)


def head_back(ins, groups, outs, scratch):
    asking, own, mine_ref, other_ref, positives, ids, place_of, gains = ins[:8]
    hat2_ref, scale2_ref, hat_ref, scale_ref, slope_ref = ins[8:13]
    act_part, low_part, context_part = ins[13:]
    loss_ref, context_ref, sum_ref, gain_ref, grad_out, grad_in, grad_back = outs
    w_out, w_in, w_back, d_ups, keep_sum, keep_context, sem = scratch
    from_back = load(groups[2], w_back, sem.at[0])
    from_in = load(groups[1], w_in, sem.at[1])
    from_out = load(groups[0], w_out, sem.at[2], 3 * D)
    rows = mine_ref.shape[0]
    is_asking = jnp.full((rows, D), asking[0]) == 1
    mine, other = mine_ref[...], other_ref[...]
    loss, d_logits = logit_back(
        jnp.where(is_asking, mine, other),
        jnp.where(is_asking, other, mine),
        positives[...],
        ids[...],
        place_of[...],
    )
    loss_ref[...] = jnp.broadcast_to(loss, loss_ref.shape)
    square = jnp.full((rows, rows), asking[0]) == 1
    d_final = dot_split(jnp.where(square, d_logits, d_logits.T), other)
    wait_all(from_back)
    wait_all(from_in + from_out)

    def emit(j, d_up):
        d_ups[:, j * D : j * D + D] = d_up

    d_down, d_sum, d_att, d_context, d_gains = back_math(
        d_final,
        hat2_ref[...],
        scale2_ref[:, :1],
        hat_ref[...],
        scale_ref[:, :1],
        gains[...],
        lambda j: slope_ref[:, j * D : j * D + D],
        lambda: w_out[...],
        lambda j: w_in[:, j * D : j * D + D],
        lambda j: w_back[j * D : j * D + D, :],
        emit,
    )
    for i, d_gain in enumerate(d_gains):
        gain_ref[i : i + 1, :] = d_gain
    keep_sum[...] = d_sum
    keep_context[...] = d_context
    count = sum_ref.shape[0] * SLOTS
    at = pl.ds(pl.multiple_of(own[0] * count, 8), count)
    own_sum, own_context = keep_sum[at, :], keep_context[at, :]
    for r in range(sum_ref.shape[0]):
        sum_ref[r] = own_sum[r * SLOTS : r * SLOTS + SLOTS]
        context_ref[r] = own_context[r * SLOTS : r * SLOTS + SLOTS]
    grad_back[...] = dot_tn(act_part[...], d_down)
    grad_in[...] = dot_tn(low_part[...], d_ups[...])
    grad_out[...] = dot_tn(context_part[...], d_att)


WIDE = HEADS * SLOTS


def spread_heads(four):
    eight = jnp.concatenate([four, four], axis=0)
    tall = jnp.concatenate([eight] * (HEADS // 2), axis=0)
    return jnp.where(own_head(), tall, 0.0)


def own_head():
    shape = (WIDE, D)
    return iota(shape, 0) // SLOTS == iota(shape, 1) // HEAD


def attend_back(ins, groups, outs, scratch):
    source, lens, asking, x_ref, picked_ref, key_ref, value_ref, context_ref = ins
    probs_ref, score_ref, query_ref, wide_ref, d_query_ref = outs[:5]
    sum_refs = outs[5:]
    seen, full, total = scratch
    step = pl.program_id(0)
    many = x_ref.shape[0]
    shape = (WIDE, SEQ_LEN)
    every = range(many)
    slot_of = iota(shape, 0) & (SLOTS - 1)
    valid = [open_keys(shape, 1, step * many + i, slot_of, lens, asking[0]) for i in every]
    query = [spread_heads(picked_ref[i]).astype(BF) for i in every]
    d_context = [spread_heads(context_ref[i]).astype(BF) for i in every]
    score = [dot_nt(query[i], key_ref[i]) * HEAD_SCALE for i in every]
    d_probs = [dot(d_context[i], value_ref[i]) for i in every]
    probs, d_score = [], []
    for i in every:
        masked = jnp.where(valid[i], score[i], NEG)
        expo = jnp.exp(masked - jnp.max(masked, axis=-1, keepdims=True))
        prob = expo / jnp.sum(expo, axis=-1, keepdims=True)
        spread = jnp.sum(d_probs[i] * prob, axis=-1, keepdims=True)
        probs.append(prob.astype(BF))
        d_score.append((prob * (d_probs[i] - spread)).astype(BF))
    for i in every:
        probs_ref[i] = probs[i]
        score_ref[i] = d_score[i]
        query_ref[i] = query[i]
        wide_ref[i] = d_context[i]
    d_query = [dot(d_score[i], key_ref[i]) * HEAD_SCALE for i in every]
    by_key = [(dot(d_score[i], x_ref[i]) * HEAD_SCALE).astype(BF) for i in every]
    by_val = [dot(probs[i], x_ref[i]).astype(BF) for i in every]
    for i in every:
        kept = jnp.where(own_head(), d_query[i], 0.0)
        eight = kept[0:8]
        for j in range(8, WIDE, 8):
            eight = eight + kept[j : j + 8]
        d_query_ref[i] = (eight[:SLOTS] + eight[SLOTS:]).astype(BF)
        at = pl.ds(pl.multiple_of((step * many + i) * WIDE, 16), WIDE)
        seen[0, at, :] = by_key[i]
        seen[1, at, :] = by_val[i]
        full[0, at, :] = query[i]
        full[1, at, :] = d_context[i]

    @pl.when(step == pl.num_programs(0) - 1)
    def _():
        for which in range(2):
            total[...] = dot_tn(seen[which], full[which]).astype(BF)
            k = 0
            for out_ref in sum_refs[2 * which : 2 * which + 2]:
                blocks, unit = out_ref.shape[0], out_ref.shape[1]
                for i in range(blocks):
                    at = pl.multiple_of(source[which, k] * unit, unit)
                    out_ref[i] = total[pl.ds(at, unit), :]
                    k += 1


def states_back(ins, groups, outs, scratch):
    probs_ref, score_ref, query_ref, wide_ref, d_query_ref, d_sum_ref = ins
    (grad_ref,) = outs
    w, sem = scratch

    @pl.when(pl.program_id(0) == 0)
    def _():
        wait_all(load(groups[0], w, sem))

    many = grad_ref.shape[0]
    every = range(many)
    tall = many * WIDE
    by_key = (dot_nt(query_ref[...].reshape(tall, D), w[:, D : 2 * D]) * HEAD_SCALE).astype(BF)
    by_val = dot_nt(wide_ref[...].reshape(tall, D), w[:, 2 * D :]).astype(BF)
    fours = [d_query_ref[i].astype(F32) for i in every]
    extra = dot_nt(jnp.concatenate(fours, axis=0).astype(BF), w[:, :D])
    for i in every:
        rows = slice(i * WIDE, i * WIDE + WIDE)
        grad_ref[i] = dot_tn(score_ref[i], by_key[rows]) + dot_tn(probs_ref[i], by_val[rows])
        for s in range(SLOTS):
            at = slice(s * QLEN, s * QLEN + 1)
            add = extra[i * SLOTS + s : i * SLOTS + s + 1] + d_sum_ref[i, s : s + 1]
            grad_ref[i, at, :] = grad_ref[i, at, :] + add


def body(
    states,
    q_lengths,
    dataset_ids,
    positives,
    w_qkv,
    w_out,
    w_in,
    w_back,
    gain_first,
    bias_first,
    gain_second,
    bias_second,
):
    devices = lax.axis_size("batch")
    links = Links() if devices == 16 else None
    own = lax.axis_index("batch")
    is_asking = lax.axis_index("tower") == 0
    asking = is_asking.astype(jnp.int32).reshape(1)
    inputs = states[0]
    rows = inputs.shape[0]
    heads = rows * SLOTS
    every = heads * devices
    part = w_qkv.shape[1]
    back_part = w_back.shape[1]

    vectors = jnp.concatenate([gain_first, bias_first, gain_second, bias_second], axis=0)
    vectors = jnp.pad(vectors.T, ((0, 0), (0, 124)))
    first_needed = jnp.concatenate([w_qkv[0], w_out[0], vectors], axis=1)
    g_in = gather_whole(w_in[0])
    if links is not None:
        place = piece_places(links)
        mix_pieces = gather_plane(links, gather_line(links, first_needed))
        g_mix = Gathered(mix_pieces, place)
        back_line = gather_line(links, after(w_back[0], mix_pieces[12]))
        back_line[0] = after(w_back[0], mix_pieces[13], mix_pieces[14])
        back_pieces = gather_plane(links, back_line)
        g_back = Gathered(back_pieces, place)
    else:
        g_mix, g_back = gather_whole(first_needed), gather_whole(w_back[0])

    one = functools.partial(rows_spec, 1)
    two = functools.partial(rows_spec, 2)
    half = rows // 2
    mixed = []
    for skip in (0, half):
        at = functools.partial(rows_spec, 1, skip=skip)
        kept = [
            ((rows, SLOTS, D), F32, at(SLOTS, D)),
            ((rows, SEQ_LEN, D), BF, at(SEQ_LEN, D)),
            ((rows, D, SEQ_LEN), BF, at(D, SEQ_LEN)),
            ((rows, SEQ_LEN, D), BF, at(SEQ_LEN, D)),
        ]
        behind = []
        if links is not None:
            behind = [back_pieces[k] for k in ((1, 2, 5, 6, 9, 10) if skip else (4, 8, 12))]
        if skip:
            mixed, gains = mixed[:4], mixed[4]
        mixed = launch(
            functools.partial(mix, skip),
            [(q_lengths, SMEM), (asking, SMEM), (inputs, at(SEQ_LEN, D))]
            + [(value, ANY) for value in mixed],
            [g_mix],
            kept if skip else kept + [((8, D), F32, VMEM)],
            [
                pltpu.VMEM((D, 3 * D), BF),
                pltpu.VMEM((D, 128), BF),
                pltpu.VMEM((D, D), BF),
                sems(2, g_mix.blocks),
            ],
            room=60,
            grid=(half,),
            flops=2 * half * SEQ_LEN * D * (3 * D + 4 * SEQ_LEN),
            moved=10 * MIB,
            same={3 + k: k for k in range(4)} if skip else None,
            behind=behind,
        )
    query, key, value, context = mixed
    picked = inputs.reshape(rows, SLOTS, QLEN, D)[:, :, 0].reshape(heads, D)
    context_own = context.reshape(rows, SLOTS, QLEN, D)[:, :, 0].reshape(heads, D)
    index = positives[:, None]
    note = jnp.pad(jnp.concatenate([index // 256, index % 256], axis=1), ((0, 0), (0, 126)))
    parcel = jnp.concatenate([context_own, picked, note.astype(BF)], axis=1)
    context_all, shared = gather_rows(links, parcel, D)
    picked_all = shared[:, :D]
    noted = shared[:, D : D + 2].astype(jnp.int32)
    positives_all = noted[:, :1] * 256 + noted[:, 1:]

    if links is not None:
        first, act = launch(
            up,
            [(inputs, two(SEQ_LEN, D)), (context, two(SEQ_LEN, D)), (gains, VMEM)],
            [g_mix, g_in],
            [
                ((rows, SEQ_LEN, D), BF, two(SEQ_LEN, D)),
                ((rows, SEQ_LEN, FF), BF, two(SEQ_LEN, FF)),
            ],
            [pltpu.VMEM((D, D), BF), pltpu.VMEM((D, FF), BF), sems(2, g_mix.blocks)],
            room=40,
            grid=(rows // 2,),
            flops=2 * rows * SEQ_LEN * D * (D + FF),
            moved=30 * MIB,
        )

        hat, scale, low, head_act, slope = launch(
            head_up,
            [(context_all, VMEM), (picked_all, VMEM), (gains, VMEM)],
            [g_mix, g_in],
            [
                ((every, D), F32, VMEM),
                ((every, 128), F32, VMEM),
                ((every, D), BF, VMEM),
                ((every, FF), BF, VMEM),
                ((every, FF), BF, VMEM),
            ],
            [pltpu.VMEM((D, D), BF), pltpu.VMEM((D, FF), BF), sems(2, g_mix.blocks)],
            room=36,
            flops=2 * every * D * (D + FF),
            moved=14 * MIB,
            behind=[act],
        )
        hat2, scale2, final = launch(
            head_down,
            [(hat, VMEM), (head_act, VMEM), (gains, VMEM)],
            [g_back],
            [((every, D), F32, VMEM), ((every, 128), F32, VMEM), ((every, D), BF, VMEM)],
            [pltpu.VMEM((FF, D), BF), sems(g_back.blocks)],
            room=24,
            flops=2 * every * D * FF,
            moved=10 * MIB,
        )
    else:
        first, act = launch(
            up,
            [(inputs, two(SEQ_LEN, D)), (context, two(SEQ_LEN, D)), (gains, VMEM)],
            [g_mix, g_in],
            [
                ((rows, SEQ_LEN, D), BF, two(SEQ_LEN, D)),
                ((rows, SEQ_LEN, FF), BF, two(SEQ_LEN, FF)),
            ],
            [pltpu.VMEM((D, D), BF), pltpu.VMEM((D, FF), BF), sems(2, g_mix.blocks)],
            room=40,
            grid=(rows // 2,),
            flops=2 * rows * SEQ_LEN * D * (D + FF),
            moved=30 * MIB,
        )

        out_full = g_mix.whole()[:, 3 * D : 4 * D]
        in_full, back_full = g_in.whole(), g_back.whole()
        acts, slopes = [], []

        def emit(j, act_part, slope_part):
            acts.append(act_part)
            slopes.append(slope_part)

        hat, scale, low = head_up_math(
            context_all,
            picked_all,
            gains,
            out_full,
            lambda j: in_full[:, j * D : j * D + D],
            emit,
        )
        head_act = jnp.concatenate(acts, axis=1)
        hat2, scale2, final = head_down_math(hat, gains, head_act, back_full)

    other = lax.ppermute(final, "tower", [(0, 1), (1, 0)])
    if links is not None:
        column = jnp.arange(every, dtype=jnp.int32)[None]
        place_of = jnp.where(column % SLOTS == 0, column // SLOTS, -1)
        ids = jnp.repeat(dataset_ids.astype(F32), SLOTS)[None]
        columns = lambda a, width: lax.dynamic_slice(a, (0, own * width), (every, width))
        loss, d_context, d_sum, d_gains, grad_out, grad_in, grad_back = launch(
            head_back,
            [
                (asking, SMEM),
                (own.astype(jnp.int32).reshape(1), SMEM),
                (final, VMEM),
                (other, VMEM),
                (positives_all, VMEM),
                (ids, VMEM),
                (place_of, VMEM),
                (gains, VMEM),
                (hat2, VMEM),
                (scale2, VMEM),
                (hat, VMEM),
                (scale, VMEM),
                (slope, VMEM),
                (columns(head_act, back_part), VMEM),
                (columns(low, part), VMEM),
                (columns(context_all, part), VMEM),
            ],
            [g_mix, g_in, g_back],
            [
                ((8, 128), F32, VMEM),
                ((rows, SLOTS, D), F32, VMEM),
                ((rows, SLOTS, D), F32, VMEM),
                ((8, D), F32, VMEM),
                ((part, D), F32, VMEM),
                ((part, FF), F32, VMEM),
                ((back_part, D), F32, VMEM),
            ],
            [
                pltpu.VMEM((D, D), BF),
                pltpu.VMEM((D, FF), BF),
                pltpu.VMEM((FF, D), BF),
                pltpu.VMEM((every, FF), BF),
                pltpu.VMEM((every, D), F32),
                pltpu.VMEM((every, D), F32),
                sems(3, g_back.blocks),
            ],
            room=48,
            flops=2 * every * D * (2 * FF + 3 * D),
            moved=20 * MIB,
        )
        loss = loss[0, 0]
    else:
        passages = jnp.where(is_asking, other, final)[::SLOTS]
        asked = jnp.where(is_asking, final, other)
        loss, d_logits = logit_back(
            asked,
            passages,
            positives_all,
            dataset_ids.astype(F32)[None],
            jnp.arange(passages.shape[0], dtype=jnp.int32)[None],
        )
        loss = loss[0, 0]
        d_asked = dot_split(d_logits, passages)
        d_passages = dot_split(d_logits.T, asked)
        spaced = jnp.pad(d_passages[:, None], ((0, 0), (0, SLOTS - 1), (0, 0)))
        d_ups = []
        d_down, d_sum, d_att, d_context, d_gains = back_math(
            jnp.where(is_asking, d_asked, spaced.reshape(every, D)),
            hat2,
            scale2,
            hat,
            scale,
            gains,
            lambda j: slopes[j],
            lambda: out_full,
            lambda j: in_full[:, j * D : j * D + D],
            lambda j: back_full[j * D : j * D + D],
            lambda j, d_up_part: d_ups.append(d_up_part),
        )
        d_up = jnp.concatenate(d_ups, axis=1)
        d_gains = jnp.concatenate(d_gains, axis=0)
        own_rows = lambda a: lax.dynamic_slice(a, (own * heads, 0), (heads, D))
        d_sum = own_rows(d_sum).reshape(rows, SLOTS, D)
        d_context = own_rows(d_context).reshape(rows, SLOTS, D)

    if links is not None:
        z, y, x = links.at
        block = jnp.arange(devices, dtype=jnp.int32)
        far, near, line = block // 8, block // 4 % 2, (z + block) % 4 * 4
        source = jnp.stack(
            [line + (y ^ near) * 2 + (x ^ far), line + (y ^ far) * 2 + (x ^ near)]
        ).astype(jnp.int32)
        sums = [((8, part, D), BF, VMEM)] * 4
    else:
        source = jnp.zeros((2, 2), jnp.int32)
        sums = [((1, D, D), BF, VMEM)] * 4
    outs = launch(
        attend_back,
        [
            (source, SMEM),
            (q_lengths, SMEM),
            (asking, SMEM),
            (inputs, two(SEQ_LEN, D)),
            (query, two(SLOTS, D)),
            (key, two(SEQ_LEN, D)),
            (value, two(D, SEQ_LEN)),
            (d_context, two(SLOTS, D)),
        ],
        [],
        [
            ((rows, WIDE, SEQ_LEN), BF, two(WIDE, SEQ_LEN)),
            ((rows, WIDE, SEQ_LEN), BF, two(WIDE, SEQ_LEN)),
            ((rows, WIDE, D), BF, two(WIDE, D)),
            ((rows, WIDE, D), BF, two(WIDE, D)),
            ((rows, SLOTS, D), BF, two(SLOTS, D)),
        ]
        + sums,
        [
            pltpu.VMEM((2, rows * WIDE, D), BF),
            pltpu.VMEM((2, rows * WIDE, D), BF),
            pltpu.VMEM((D, D), BF),
        ],
        room=60,
        grid=(rows // 2,),
        flops=2 * rows * WIDE * D * (5 * SEQ_LEN + 2 * D),
        moved=16 * MIB,
    )
    low_probs, low_score, wide_query, wide_context, d_query = outs[:5]
    keys, keys_away, vals, vals_away = outs[5:]
    d_query_all = jnp.concatenate(gather_rows(links, d_query.reshape(heads, D), D // 2), axis=1)
    (states_grad,) = launch(
        states_back,
        [
            (low_probs, two(WIDE, SEQ_LEN)),
            (low_score, two(WIDE, SEQ_LEN)),
            (wide_query, two(WIDE, D)),
            (wide_context, two(WIDE, D)),
            (d_query, two(SLOTS, D)),
            (d_sum, two(SLOTS, D)),
        ],
        [g_mix],
        [((rows, SEQ_LEN, D), F32, two(SEQ_LEN, D))],
        [pltpu.VMEM((D, 3 * D), BF), sems(g_mix.blocks)],
        room=60,
        grid=(rows // 2,),
        flops=2 * rows * WIDE * D * (3 * D + 2 * SEQ_LEN),
        moved=12 * MIB,
    )
    if links is not None:
        key_in, val_in = move(keys_away, links.x), move(vals_away, links.y)
        keys_away, vals_away = low_sum(keys[4:], key_in[4:]), low_sum(vals[4:], val_in[4:])
        keys, vals = low_sum(keys[:4], key_in[:4]), low_sum(vals[:4], val_in[:4])
        key_in, val_in = move(keys_away, links.y), move(vals_away, links.x)
        both = jnp.stack([low_sum(keys, key_in), low_sum(vals, val_in)], axis=1)
        behind = [both]
        total = both[0].astype(F32)
        for c in (1, 2, 3):
            total = total + move(both[c], links.z[c]).astype(F32)
        grad_key, grad_val = total[0], total[1]
    else:
        grad_key = lax.psum_scatter(keys[0], "batch", scatter_dimension=0, tiled=True).astype(F32)
        grad_val = lax.psum_scatter(vals[0], "batch", scatter_dimension=0, tiled=True).astype(F32)
    (encoded,) = launch(
        down,
        [(first, two(SEQ_LEN, D)), (act, two(SEQ_LEN, FF)), (gains, VMEM)],
        [g_back],
        [((rows, SEQ_LEN, D), BF, two(SEQ_LEN, D))],
        [pltpu.VMEM((FF, D), BF), sems(g_back.blocks)],
        room=32,
        grid=(rows // 2,),
        flops=2 * rows * SEQ_LEN * D * FF,
        moved=24 * MIB,
        behind=behind,
    )
    columns = lambda a, width: lax.dynamic_slice(a, (0, own * width), (every, width))
    if links is None:
        grad_back = dot_tn(columns(head_act, back_part), d_down)
        grad_in = dot_tn(columns(low, part), d_up)
        grad_out = dot_tn(columns(context_all, part), d_att)
    grad_query = dot_tn(columns(picked_all, part), d_query_all)
    grad_qkv = jnp.concatenate([grad_query, grad_key, grad_val], axis=1)
    gain_own = lax.dynamic_slice(d_gains, (0, own * part), (4, part))
    return (
        loss,
        encoded[None],
        states_grad[None],
        grad_qkv[None],
        grad_out[None],
        grad_in[None],
        grad_back[None],
        gain_own[0:1],
        gain_own[1:2],
        gain_own[2:3],
        gain_own[3:4],
    )


def solution(mesh):
    rows = P("tower", "batch", None, None)
    matrix = P("tower", "batch", None)
    vector = P("tower", "batch")
    return jax.shard_map(
        body,
        mesh=mesh,
        in_specs=(rows, P("batch", None), P(), P("batch"))
        + (matrix,) * 4
        + (vector,) * 4,
        out_specs=(P(), rows, rows) + (matrix,) * 4 + (vector,) * 4,
        check_vma=False,
    )
```

```python
import functools
import math

import jax
import jax.numpy as jnp
from jax import lax
from jax.experimental import pallas as pl
from jax.experimental.pallas import tpu as pltpu
from jax.sharding import PartitionSpec as P

D = 768
HEADS = 12
HEAD = 64
FF = 3072
SEQ_LEN = 256
QLEN = 64
SLOTS = 4
EPS = 1e-05
NEG = -1000000000.0
BF = jnp.bfloat16
F32 = jnp.float32
MIB = 1 << 20
HEAD_SCALE = 1.0 / math.sqrt(HEAD)
LOGIT_SCALE = 2.0 / math.sqrt(D)
CHUNKS = FF // D
VMEM = pl.BlockSpec(memory_space=pltpu.VMEM)
SMEM = pl.BlockSpec(memory_space=pltpu.SMEM)
ANY = pl.BlockSpec(memory_space=pl.ANY)


def dot(a, b):
    return lax.dot_general(a, b, (((1,), (0,)), ((), ())), preferred_element_type=F32)


def dot_nt(a, b):
    return lax.dot_general(a, b, (((1,), (1,)), ((), ())), preferred_element_type=F32)


def dot_tn(a, b):
    return lax.dot_general(a, b, (((0,), (0,)), ((), ())), preferred_element_type=F32)


def iota(shape, axis):
    return lax.broadcasted_iota(jnp.int32, shape, axis)


def normalise(summed):
    center = summed - jnp.mean(summed, axis=-1, keepdims=True)
    spread = jnp.mean(center * center, axis=-1, keepdims=True)
    scale = lax.rsqrt(spread + EPS)
    return center * scale, scale


def normalise_back(grad, hat, scale, gain):
    d_hat = grad * gain
    mean_d = jnp.mean(d_hat, axis=-1, keepdims=True)
    mean_dh = jnp.mean(d_hat * hat, axis=-1, keepdims=True)
    d_gain = jnp.sum(grad * hat, axis=0, keepdims=True)
    d_shift = jnp.sum(grad, axis=0, keepdims=True)
    return scale * (d_hat - mean_d - hat * mean_dh), d_gain, d_shift


def normal_cdf(values):
    return 0.5 * (1.0 + lax.erf(values * math.sqrt(0.5)))


def gelu(values):
    return values * normal_cdf(values)


def gelu_pair(values):
    cdf = normal_cdf(values)
    bell = jnp.exp(-0.5 * values * values) * (1.0 / math.sqrt(2.0 * math.pi))
    return values * cdf, cdf + values * bell


class Links:
    def __init__(self):
        def table(move):
            at = lambda z, y, x: z * 4 + y * 2 + x
            return [
                (at(z, y, x), at(*move(z, y, x)))
                for z in range(4)
                for y in range(2)
                for x in range(2)
            ]

        by_x = table(lambda z, y, x: (z, y, 1 - x))
        by_y = table(lambda z, y, x: (z, 1 - y, x))
        self.z = [table(lambda z, y, x, c=c: ((z + c) % 4, y, x)) for c in range(4)]
        shifted = lambda pairs: [(a + 16, b + 16) for a, b in pairs]
        self.x, self.y = by_x, by_y
        self.first = by_x + shifted(by_y)
        self.second = by_y + shifted(by_x)
        me = lax.axis_index("batch")
        self.at = (me // 4, me // 2 % 2, me % 2)
        self.question = lax.axis_index("tower") == 0

    def place(self, c, first, second):
        z, y, x = self.at
        dx = jnp.where(self.question, first, second)
        dy = jnp.where(self.question, second, first)
        return (z + c + 4) % 4 * 4 + (y ^ dy) * 2 + (x ^ dx)


def move(value, pairs):
    return lax.ppermute(value, "batch", pairs)


def move_plane(value, pairs):
    return lax.ppermute(value, ("tower", "batch"), pairs)


def after(value, *earlier):
    late = sum(other[(0,) * other.ndim].astype(F32) for other in earlier) > 1e30
    return jnp.where(late, jnp.zeros_like(value), value)


def gather_line(links, shard):
    return jnp.stack([move(shard, links.z[c]) for c in (1, 2, 3)])


def gather_plane(links, line):
    near = move_plane(line, links.first)
    side = move_plane(line, links.second)
    return [line, near, side, move_plane(near, links.second)]


CORNERS = ((0, 0), (1, 0), (0, 1), (1, 1))


class Gathered:
    def __init__(self, pieces, place, bases=None, folds=1):
        self.pieces = pieces
        self.place = place
        self.bases = bases or [0] * len(pieces)
        self.folds = folds
        self.copies = place.shape[0] * folds

    def whole(self):
        return self.pieces[0][0]


def gather_whole(shard):
    whole = lax.all_gather(shard, "batch", axis=0, tiled=True)
    return Gathered([whole[None]], jnp.zeros((1,), jnp.int32))


def gather_pieces(links, own, line, base, folds=1):
    order = [(0, f, s) for f, s in CORNERS] + [(-c, f, s) for f, s in CORNERS for c in (1, 2, 3)]
    place = jnp.stack([links.place(*at) for at in order]).astype(jnp.int32)
    return Gathered([piece[None] for piece in own] + line, place, [base] * 4 + [0] * 4, folds)


def gather_rows(links, rows, behind=None):
    if links is None:
        return lax.all_gather(rows, "batch", axis=0, tiled=True)
    z, y, x = links.at
    count, width = rows.shape
    zs = [rows] + [move(rows, links.z[c]) for c in (1, 2, 3)]
    line = jnp.concatenate([zs[3], zs[2], zs[1], zs[0], zs[3], zs[2], zs[1]])
    line = lax.dynamic_slice(line, ((3 - z) * count, 0), (4 * count, width))
    if behind is not None:
        line = after(line, behind)
    line, near, side, far = gather_plane(links, line)
    by_x, by_y = (jnp.where(links.question, *pair) for pair in ((near, side), (side, near)))
    flip = lambda at, a, b: jnp.where(at == 0, jnp.stack([a, b]), jnp.stack([b, a]))
    full = flip(y, flip(x, line, by_x), flip(x, by_y, far))
    return full.reshape(4, 4, count, width).transpose(1, 0, 2, 3).reshape(16 * count, width)


def low_sum(a, b):
    return (a.astype(F32) + b.astype(F32)).astype(BF)


def load(group, target, sems, low=0):
    place, pieces, weight = group
    width = target.shape[1]
    copies = []
    k = 0
    for piece, base in zip(pieces, weight.bases):
        for c in range(piece.shape[0]):
            unit = piece.shape[1]
            for fold in range(weight.folds):
                row = pl.multiple_of((place[k] * weight.folds + fold) * unit, unit)
                copies.append(
                    pltpu.make_async_copy(
                        piece.at[c, :, pl.ds(base + low + fold * width, width)],
                        target.at[pl.ds(row, unit), :],
                        sems.at[len(copies)],
                    )
                )
            k += 1
    for copy in copies:
        copy.start()
    return copies


def wait_all(copies):
    for copy in copies:
        copy.wait()


def launch(
    kernel, ins, weights, outs, scratch, room, grid=None, flops=0, moved=0, same=None, behind=()
):
    values = list(ins)
    for weight in weights:
        values += [(weight.place, SMEM)] + [(piece, ANY) for piece in weight.pieces]
    values += [(value, ANY) for value in behind]

    def run(*refs):
        at = len(ins)
        groups = []
        for weight in weights:
            end = at + 1 + len(weight.pieces)
            groups.append((refs[at], refs[at + 1 : end], weight))
            at = end
        at += len(behind)
        kernel(refs[: len(ins)], groups, refs[at : at + len(outs)], refs[at + len(outs) :])

    extra = {} if grid is None else {"grid": grid}
    return pl.pallas_call(
        run,
        name=getattr(kernel, "func", kernel).__name__,
        input_output_aliases=same or {},
        in_specs=[spec for _, spec in values],
        out_specs=[spec for _, _, spec in outs],
        out_shape=[jax.ShapeDtypeStruct(shape, dtype) for shape, dtype, _ in outs],
        scratch_shapes=scratch,
        compiler_params=pltpu.CompilerParams(vmem_limit_bytes=room * MIB),
        cost_estimate=pl.CostEstimate(
            flops=int(flops), bytes_accessed=int(moved), transcendentals=0
        ),
        **extra,
    )(*[value for value, _ in values])


def sems(*shape):
    return pltpu.SemaphoreType.DMA(shape)


def rows_spec(many, *tail, skip=0):
    return pl.BlockSpec((many,) + tail, lambda r: (r + skip,) + (0,) * len(tail))


def open_keys(shape, key_axis, row, slot_of_query, lens, ask):
    key_at = iota(shape, key_axis)
    slot = key_at >> 6
    limit = jnp.zeros(shape, jnp.int32)
    for s in range(SLOTS):
        limit = jnp.where(slot == s, lens[row, s] * ask + QLEN * (1 - ask), limit)
    return ((key_at & (QLEN - 1)) < limit) & (slot_of_query * ask == slot * ask)


def mix(skip, ins, groups, outs, scratch):
    lens, asking, x_ref = ins[:3]
    query_ref, key_ref, value_ref, context_ref = outs[:4]
    w, w_gain, w_turned, sem = scratch
    row = pl.program_id(0) + skip

    @pl.when(pl.program_id(0) == 0)
    def _():
        copies = load(groups[0], w, sem.at[0])
        if len(outs) > 4:
            wait_all(load(groups[0], w_gain, sem.at[1], 4 * D))
            outs[4][...] = w_gain[...].astype(F32).T[:8]
        wait_all(copies)
        for j in range(0, D, 128):
            part = w[:, 2 * D + j : 2 * D + j + 128].astype(F32)
            w_turned[j : j + 128, :] = part.T.astype(BF)

    x = x_ref[0]
    mixed = dot(x, w[:, : 2 * D])
    for s in range(SLOTS):
        query_ref[0, s : s + 1, :] = mixed[s * QLEN : s * QLEN + 1, :D]
    query = (mixed[:, :D] * HEAD_SCALE).astype(BF)
    keyset = mixed[:, D:].astype(BF)
    values = dot_nt(w_turned[...], x).astype(BF)
    key_ref[0] = keyset
    value_ref[0] = values
    shape = (SEQ_LEN, SEQ_LEN)
    closed = jnp.where(open_keys(shape, 0, row, iota(shape, 1) >> 6, lens, asking[0]), 0, 1) == 1
    ones = jnp.ones((16, SEQ_LEN), BF)
    nothing = jnp.zeros((SEQ_LEN, 128), BF)
    half_of = iota((SEQ_LEN, 128), 1) // HEAD
    scores = []
    for head in range(HEADS):
        low = head // 2 * 128
        mine = jnp.where(half_of == head % 2, query[:, low : low + 128], nothing)
        scores.append(dot_nt(keyset[:, low : low + 128], mine))
    expos = []
    for score in scores:
        score = jnp.where(closed, NEG, score)
        expos.append(jnp.exp(score - jnp.max(score, axis=0, keepdims=True)).astype(BF))
    parts = []
    for head, expo in enumerate(expos):
        mine = values[head * HEAD : head * HEAD + HEAD]
        summed = dot(jnp.concatenate([mine, ones], axis=0), expo)
        parts.append(summed[:HEAD] / summed[HEAD : HEAD + 1])
    context_ref[0] = jnp.concatenate(parts, axis=0).T.astype(BF)


def up(ins, groups, outs, scratch):
    x_ref, context_ref, gains = ins
    first_ref, act_ref = outs
    w_out, w_in, sem = scratch

    @pl.when(pl.program_id(0) == 0)
    def _():
        wait_all(load(groups[0], w_out, sem.at[0], 3 * D) + load(groups[1], w_in, sem.at[1]))

    many = x_ref.shape[0] * SEQ_LEN
    attended = dot(context_ref[...].reshape(many, D), w_out[...])
    summed = x_ref[...].reshape(many, D).astype(F32) + attended
    first = normalise(summed)[0] * gains[0:1] + gains[1:2]
    low = first.astype(BF)
    first_ref[...] = low.reshape(first_ref.shape)
    for j in range(CHUNKS):
        part = gelu(dot(low, w_in[:, j * D : j * D + D])).astype(BF)
        act_ref[:, :, j * D : j * D + D] = part.reshape(act_ref.shape[0], SEQ_LEN, D)


def down(ins, groups, outs, scratch):
    first_ref, act_ref, gains = ins
    (encoded_ref,) = outs
    w_back, sem = scratch

    @pl.when(pl.program_id(0) == 0)
    def _():
        wait_all(load(groups[0], w_back, sem))

    many = first_ref.shape[0] * SEQ_LEN
    summed = dot(act_ref[...].reshape(many, FF), w_back[...])
    hat = normalise(first_ref[...].reshape(many, D).astype(F32) + summed)[0]
    encoded_ref[...] = (hat * gains[2:3] + gains[3:4]).astype(BF).reshape(encoded_ref.shape)


def head_up_math(context, picked, gains, w_out, w_in, emit):
    hat, scale = normalise(picked.astype(F32) + dot(context, w_out))
    low = (hat * gains[0:1] + gains[1:2]).astype(BF)
    for j in range(CHUNKS):
        act, slope = gelu_pair(dot(low, w_in(j)))
        emit(j, act.astype(BF), slope.astype(BF))
    return hat, scale, low


def head_up(ins, groups, outs, scratch):
    context_ref, picked_ref, gains = ins
    hat_ref, scale_ref, low_ref, act_ref, slope_ref = outs
    w_out, w_in, sem = scratch
    wait_all(load(groups[0], w_out, sem.at[0], 3 * D) + load(groups[1], w_in, sem.at[1]))

    def emit(j, act, slope):
        act_ref[:, j * D : j * D + D] = act
        slope_ref[:, j * D : j * D + D] = slope

    hat, scale, low = head_up_math(
        context_ref[...],
        picked_ref[...],
        gains[...],
        w_out[...],
        lambda j: w_in[:, j * D : j * D + D],
        emit,
    )
    hat_ref[...] = hat
    scale_ref[...] = jnp.broadcast_to(scale, scale_ref.shape)
    low_ref[...] = low


def head_down_math(hat, gains, act, w_back):
    hat2, scale2 = normalise(hat * gains[0:1] + gains[1:2] + dot(act, w_back))
    return hat2, scale2, (hat2 * gains[2:3] + gains[3:4]).astype(BF)


def head_down(ins, groups, outs, scratch):
    hat_ref, act_ref, gains = ins
    hat2_ref, scale2_ref, final_ref = outs
    w_back, sem = scratch
    wait_all(load(groups[0], w_back, sem))
    hat2, scale2, final = head_down_math(hat_ref[...], gains[...], act_ref[...], w_back[...])
    hat2_ref[...] = hat2
    scale2_ref[...] = jnp.broadcast_to(scale2, scale2_ref.shape)
    final_ref[...] = final


def logit_back(asked, passages, positives, ids, place_of):
    logits = dot_nt(asked, passages) * LOGIT_SCALE
    chosen = positives == place_of
    asked_data = jnp.sum(jnp.where(chosen, ids, 0.0), axis=1, keepdims=True)
    open_to = (asked_data == ids) & (place_of >= 0)
    masked = jnp.where(open_to, logits, NEG)
    highest = jnp.max(masked, axis=1, keepdims=True)
    expo = jnp.exp(masked - highest)
    total = jnp.sum(expo, axis=1, keepdims=True)
    target = jnp.sum(jnp.where(chosen, logits, 0.0), axis=1, keepdims=True)
    loss = jnp.sum(highest + jnp.log(total) - target, axis=0, keepdims=True) / asked.shape[0]
    d_logits = (expo / total - jnp.where(chosen, 1.0, 0.0)) * (LOGIT_SCALE / asked.shape[0])
    return loss, d_logits


def dot_split(a, b):
    high = a.astype(BF)
    return dot(high, b) + dot((a - high.astype(F32)).astype(BF), b)


def back_math(d_final, hat2, scale2, hat, scale, gains, slope, w_out, w_in, w_back, emit):
    d_second, d_gain2, d_shift2 = normalise_back(d_final, hat2, scale2, gains[2:3])
    d_down = d_second.astype(BF)
    d_first = d_second
    for j in range(CHUNKS):
        d_up = (dot_nt(d_down, w_back(j)) * slope(j).astype(F32)).astype(BF)
        emit(j, d_up)
        d_first = d_first + dot_nt(d_up, w_in(j))
    d_sum, d_gain, d_shift = normalise_back(d_first, hat, scale, gains[0:1])
    d_att = d_sum.astype(BF)
    d_context = None if w_out is None else dot_nt(d_att, w_out())
    return d_down, d_sum, d_att, d_context, (d_gain, d_shift, d_gain2, d_shift2)


def head_back(ins, groups, outs, scratch):
    asking, own, mine_ref, other_ref, positives, ids, place_of, gains = ins[:8]
    hat2_ref, scale2_ref, hat_ref, scale_ref, slope_ref = ins[8:13]
    act_part, low_part, context_part = ins[13:]
    loss_ref, context_ref, sum_ref, gain_ref, grad_out, grad_in, grad_back = outs
    w_out, w_in, w_back, d_ups, keep_sum, keep_context, sem = scratch
    from_back = load(groups[2], w_back, sem.at[0])
    from_in = load(groups[1], w_in, sem.at[1])
    from_out = load(groups[0], w_out, sem.at[2], 3 * D)
    rows = mine_ref.shape[0]
    is_asking = jnp.full((rows, D), asking[0]) == 1
    mine, other = mine_ref[...], other_ref[...]
    loss, d_logits = logit_back(
        jnp.where(is_asking, mine, other),
        jnp.where(is_asking, other, mine),
        positives[...],
        ids[...],
        place_of[...],
    )
    loss_ref[...] = jnp.broadcast_to(loss, loss_ref.shape)
    square = jnp.full((rows, rows), asking[0]) == 1
    d_final = dot_split(jnp.where(square, d_logits, d_logits.T), other)
    wait_all(from_back)
    wait_all(from_in + from_out)

    def emit(j, d_up):
        d_ups[:, j * D : j * D + D] = d_up

    d_down, d_sum, d_att, d_context, d_gains = back_math(
        d_final,
        hat2_ref[...],
        scale2_ref[:, :1],
        hat_ref[...],
        scale_ref[:, :1],
        gains[...],
        lambda j: slope_ref[:, j * D : j * D + D],
        lambda: w_out[...],
        lambda j: w_in[:, j * D : j * D + D],
        lambda j: w_back[j * D : j * D + D, :],
        emit,
    )
    for i, d_gain in enumerate(d_gains):
        gain_ref[i : i + 1, :] = d_gain
    keep_sum[...] = d_sum
    keep_context[...] = d_context
    count = sum_ref.shape[0] * SLOTS
    at = pl.ds(pl.multiple_of(own[0] * count, 8), count)
    own_sum, own_context = keep_sum[at, :], keep_context[at, :]
    for r in range(sum_ref.shape[0]):
        sum_ref[r] = own_sum[r * SLOTS : r * SLOTS + SLOTS]
        context_ref[r] = own_context[r * SLOTS : r * SLOTS + SLOTS]
    grad_back[...] = dot_tn(act_part[...], d_down)
    grad_in[...] = dot_tn(low_part[...], d_ups[...])
    grad_out[...] = dot_tn(context_part[...], d_att)


WIDE = HEADS * SLOTS


def spread_heads(four):
    eight = jnp.concatenate([four, four], axis=0)
    tall = jnp.concatenate([eight] * (HEADS // 2), axis=0)
    return jnp.where(own_head(), tall, 0.0)


def own_head():
    shape = (WIDE, D)
    return iota(shape, 0) // SLOTS == iota(shape, 1) // HEAD


def attend_back(ins, groups, outs, scratch):
    source, lens, asking, x_ref, picked_ref, key_ref, value_ref, context_ref = ins
    probs_ref, score_ref, query_ref, wide_ref, d_query_ref = outs[:5]
    sum_refs = outs[5:]
    seen, full, total = scratch
    step = pl.program_id(0)
    many = x_ref.shape[0]
    shape = (WIDE, SEQ_LEN)
    every = range(many)
    slot_of = iota(shape, 0) & (SLOTS - 1)
    valid = [open_keys(shape, 1, step * many + i, slot_of, lens, asking[0]) for i in every]
    query = [spread_heads(picked_ref[i]).astype(BF) for i in every]
    d_context = [spread_heads(context_ref[i]).astype(BF) for i in every]
    score = [dot_nt(query[i], key_ref[i]) * HEAD_SCALE for i in every]
    d_probs = [dot(d_context[i], value_ref[i]) for i in every]
    probs, d_score = [], []
    for i in every:
        masked = jnp.where(valid[i], score[i], NEG)
        expo = jnp.exp(masked - jnp.max(masked, axis=-1, keepdims=True))
        prob = expo / jnp.sum(expo, axis=-1, keepdims=True)
        spread = jnp.sum(d_probs[i] * prob, axis=-1, keepdims=True)
        probs.append(prob.astype(BF))
        d_score.append((prob * (d_probs[i] - spread)).astype(BF))
    for i in every:
        probs_ref[i] = probs[i]
        score_ref[i] = d_score[i]
        query_ref[i] = query[i]
        wide_ref[i] = d_context[i]
    d_query = [dot(d_score[i], key_ref[i]) * HEAD_SCALE for i in every]
    by_key = [(dot(d_score[i], x_ref[i]) * HEAD_SCALE).astype(BF) for i in every]
    by_val = [dot(probs[i], x_ref[i]).astype(BF) for i in every]
    for i in every:
        kept = jnp.where(own_head(), d_query[i], 0.0)
        eight = kept[0:8]
        for j in range(8, WIDE, 8):
            eight = eight + kept[j : j + 8]
        d_query_ref[i] = (eight[:SLOTS] + eight[SLOTS:]).astype(BF)
        at = pl.ds(pl.multiple_of((step * many + i) * WIDE, 16), WIDE)
        seen[0, at, :] = by_key[i]
        seen[1, at, :] = by_val[i]
        full[0, at, :] = query[i]
        full[1, at, :] = d_context[i]

    @pl.when(step == pl.num_programs(0) - 1)
    def _():
        for which in range(2):
            total[...] = dot_tn(seen[which], full[which]).astype(BF)
            k = 0
            for out_ref in sum_refs[which::2]:
                blocks, unit = out_ref.shape[0], out_ref.shape[1]
                for i in range(blocks):
                    at = pl.multiple_of(source[which, k] * unit, unit)
                    out_ref[i] = total[pl.ds(at, unit), :]
                    k += 1


def states_back(ins, groups, outs, scratch):
    probs_ref, score_ref, query_ref, wide_ref, d_query_ref, d_sum_ref = ins
    (grad_ref,) = outs
    w, sem = scratch

    @pl.when(pl.program_id(0) == 0)
    def _():
        wait_all(load(groups[0], w, sem))

    many = grad_ref.shape[0]
    every = range(many)
    tall = many * WIDE
    by_key = (dot_nt(query_ref[...].reshape(tall, D), w[:, D : 2 * D]) * HEAD_SCALE).astype(BF)
    by_val = dot_nt(wide_ref[...].reshape(tall, D), w[:, 2 * D :]).astype(BF)
    fours = [d_query_ref[i].astype(F32) for i in every]
    extra = dot_nt(jnp.concatenate(fours, axis=0).astype(BF), w[:, :D])
    for i in every:
        rows = slice(i * WIDE, i * WIDE + WIDE)
        grad_ref[i] = dot_tn(score_ref[i], by_key[rows]) + dot_tn(probs_ref[i], by_val[rows])
        for s in range(SLOTS):
            at = slice(s * QLEN, s * QLEN + 1)
            add = extra[i * SLOTS + s : i * SLOTS + s + 1] + d_sum_ref[i, s : s + 1]
            grad_ref[i, at, :] = grad_ref[i, at, :] + add


def body(
    states,
    q_lengths,
    dataset_ids,
    positives,
    w_qkv,
    w_out,
    w_in,
    w_back,
    gain_first,
    bias_first,
    gain_second,
    bias_second,
):
    devices = lax.axis_size("batch")
    links = Links() if devices == 16 else None
    own = lax.axis_index("batch")
    is_asking = lax.axis_index("tower") == 0
    asking = is_asking.astype(jnp.int32).reshape(1)
    inputs = states[0]
    rows = inputs.shape[0]
    heads = rows * SLOTS
    every = heads * devices
    part = w_qkv.shape[1]
    back_part = w_back.shape[1]

    vectors = jnp.concatenate([gain_first, bias_first, gain_second, bias_second], axis=0)
    vectors = jnp.pad(vectors.T, ((0, 0), (0, 124)))
    first_needed = jnp.concatenate([w_qkv[0], w_out[0], vectors], axis=1)
    if links is not None:
        folded = jnp.concatenate(jnp.split(w_back[0], CHUNKS, axis=0), axis=1)
        mix_line = gather_line(links, first_needed)
        mix_own = gather_plane(links, first_needed)
        later = jnp.concatenate([w_in[0], folded], axis=1)
        later_own = gather_plane(links, after(later, mix_own[1], mix_own[2]))
        mix_pieces = gather_plane(links, mix_line)
        in_line = gather_line(links, after(w_in[0], mix_line))
        in_pieces = gather_plane(links, after(in_line, mix_pieces[3]))
        g_mix = gather_pieces(links, mix_own, mix_pieces, 0)
        g_in = gather_pieces(links, later_own, in_pieces, 0)
    else:
        g_mix, g_in, g_back = (
            gather_whole(weight) for weight in (first_needed, w_in[0], w_back[0])
        )

    two = functools.partial(rows_spec, 2)
    half = rows // 2
    mixed = []
    for skip in (0, half):
        at = functools.partial(rows_spec, 1, skip=skip)
        kept = [
            ((rows, SLOTS, D), F32, at(SLOTS, D)),
            ((rows, SEQ_LEN, D), BF, at(SEQ_LEN, D)),
            ((rows, D, SEQ_LEN), BF, at(D, SEQ_LEN)),
            ((rows, SEQ_LEN, D), BF, at(SEQ_LEN, D)),
        ]
        behind = []
        if links is not None:
            behind = in_pieces[1:3] if skip else []
        if skip:
            mixed, gains = mixed[:4], mixed[4]
            if links is not None:
                back_line = gather_line(links, after(folded, gains))
        mixed = launch(
            functools.partial(mix, skip),
            [(q_lengths, SMEM), (asking, SMEM), (inputs, at(SEQ_LEN, D))]
            + [(value, ANY) for value in mixed],
            [g_mix],
            kept if skip else kept + [((8, D), F32, VMEM)],
            [
                pltpu.VMEM((D, 3 * D), BF),
                pltpu.VMEM((D, 128), BF),
                pltpu.VMEM((D, D), BF),
                sems(2, g_mix.copies),
            ],
            room=60,
            grid=(half,),
            flops=2 * half * SEQ_LEN * D * (3 * D + 4 * SEQ_LEN),
            moved=10 * MIB,
            same={3 + k: k for k in range(4)} if skip else None,
            behind=behind,
        )
    query, key, value, context = mixed
    picked = inputs.reshape(rows, SLOTS, QLEN, D)[:, :, 0].reshape(heads, D)
    context_own = context.reshape(rows, SLOTS, QLEN, D)[:, :, 0].reshape(heads, D)
    index = positives[:, None]
    note = jnp.pad(jnp.concatenate([index // 256, index % 256], axis=1), ((0, 0), (0, 126)))
    parcel = jnp.concatenate([context_own, picked, note.astype(BF)], axis=1)
    if links is not None:
        parcel = after(parcel, in_pieces[3])
        back_pieces = gather_plane(links, back_line)
        g_back = gather_pieces(links, later_own, back_pieces, FF, CHUNKS)
    shared = gather_rows(links, parcel)
    context_all, picked_all = shared[:, :D], shared[:, D : 2 * D]
    noted = shared[:, 2 * D : 2 * D + 2].astype(jnp.int32)
    positives_all = noted[:, :1] * 256 + noted[:, 1:]

    def finish(first, act, behind):
        (encoded,) = launch(
            down,
            [(first, two(SEQ_LEN, D)), (act, two(SEQ_LEN, FF)), (gains, VMEM)],
            [g_back],
            [((rows, SEQ_LEN, D), BF, two(SEQ_LEN, D))],
            [pltpu.VMEM((FF, D), BF), sems(g_back.copies)],
            room=60,
            grid=(rows // 2,),
            flops=2 * rows * SEQ_LEN * D * FF,
            moved=24 * MIB,
            behind=behind,
        )
        return encoded

    if links is not None:
        first, act = launch(
            up,
            [(inputs, two(SEQ_LEN, D)), (context, two(SEQ_LEN, D)), (gains, VMEM)],
            [g_mix, g_in],
            [
                ((rows, SEQ_LEN, D), BF, two(SEQ_LEN, D)),
                ((rows, SEQ_LEN, FF), BF, two(SEQ_LEN, FF)),
            ],
            [pltpu.VMEM((D, D), BF), pltpu.VMEM((D, FF), BF), sems(2, g_mix.copies)],
            room=40,
            grid=(rows // 2,),
            flops=2 * rows * SEQ_LEN * D * (D + FF),
            moved=30 * MIB,
        )

        hat, scale, low, head_act, slope = launch(
            head_up,
            [(context_all, VMEM), (picked_all, VMEM), (gains, VMEM)],
            [g_mix, g_in],
            [
                ((every, D), F32, VMEM),
                ((every, 128), F32, VMEM),
                ((every, D), BF, VMEM),
                ((every, FF), BF, VMEM),
                ((every, FF), BF, VMEM),
            ],
            [pltpu.VMEM((D, D), BF), pltpu.VMEM((D, FF), BF), sems(2, g_mix.copies)],
            room=36,
            flops=2 * every * D * (D + FF),
            moved=14 * MIB,
            behind=[act],
        )
        hat2, scale2, final = launch(
            head_down,
            [(hat, VMEM), (head_act, VMEM), (gains, VMEM)],
            [g_back],
            [((every, D), F32, VMEM), ((every, 128), F32, VMEM), ((every, D), BF, VMEM)],
            [pltpu.VMEM((FF, D), BF), sems(g_back.copies)],
            room=24,
            flops=2 * every * D * FF,
            moved=10 * MIB,
        )
    else:
        first, act = launch(
            up,
            [(inputs, two(SEQ_LEN, D)), (context, two(SEQ_LEN, D)), (gains, VMEM)],
            [g_mix, g_in],
            [
                ((rows, SEQ_LEN, D), BF, two(SEQ_LEN, D)),
                ((rows, SEQ_LEN, FF), BF, two(SEQ_LEN, FF)),
            ],
            [pltpu.VMEM((D, D), BF), pltpu.VMEM((D, FF), BF), sems(2, g_mix.copies)],
            room=40,
            grid=(rows // 2,),
            flops=2 * rows * SEQ_LEN * D * (D + FF),
            moved=30 * MIB,
        )

        encoded = finish(first, act, [])
        context_all = after(context_all, encoded)
        out_full = g_mix.whole()[:, 3 * D : 4 * D]
        in_full, back_full = g_in.whole(), g_back.whole()
        acts, slopes = [], []

        def emit(j, act_part, slope_part):
            acts.append(act_part)
            slopes.append(slope_part)

        hat, scale, low = head_up_math(
            context_all,
            picked_all,
            gains,
            out_full,
            lambda j: in_full[:, j * D : j * D + D],
            emit,
        )
        head_act = jnp.concatenate(acts, axis=1)
        hat2, scale2, final = head_down_math(hat, gains, head_act, back_full)

    other = lax.ppermute(final, "tower", [(0, 1), (1, 0)])
    if links is not None:
        column = jnp.arange(every, dtype=jnp.int32)[None]
        place_of = jnp.where(column % SLOTS == 0, column // SLOTS, -1)
        ids = jnp.repeat(dataset_ids.astype(F32), SLOTS)[None]
        columns = lambda a, width: lax.dynamic_slice(a, (0, own * width), (every, width))
        loss, d_context, d_sum, d_gains, grad_out, grad_in, grad_back = launch(
            head_back,
            [
                (asking, SMEM),
                (own.astype(jnp.int32).reshape(1), SMEM),
                (final, VMEM),
                (other, VMEM),
                (positives_all, VMEM),
                (ids, VMEM),
                (place_of, VMEM),
                (gains, VMEM),
                (hat2, VMEM),
                (scale2, VMEM),
                (hat, VMEM),
                (scale, VMEM),
                (slope, VMEM),
                (columns(head_act, back_part), VMEM),
                (columns(low, part), VMEM),
                (columns(context_all, part), VMEM),
            ],
            [g_mix, g_in, g_back],
            [
                ((8, 128), F32, VMEM),
                ((rows, SLOTS, D), F32, VMEM),
                ((rows, SLOTS, D), F32, VMEM),
                ((8, D), F32, VMEM),
                ((part, D), F32, VMEM),
                ((part, FF), F32, VMEM),
                ((back_part, D), F32, VMEM),
            ],
            [
                pltpu.VMEM((D, D), BF),
                pltpu.VMEM((D, FF), BF),
                pltpu.VMEM((FF, D), BF),
                pltpu.VMEM((every, FF), BF),
                pltpu.VMEM((every, D), F32),
                pltpu.VMEM((every, D), F32),
                sems(3, g_back.copies),
            ],
            room=48,
            flops=2 * every * D * (2 * FF + 3 * D),
            moved=20 * MIB,
        )
        loss = loss[0, 0]
    else:
        passages = jnp.where(is_asking, other, final)[::SLOTS]
        asked = jnp.where(is_asking, final, other)
        loss, d_logits = logit_back(
            asked,
            passages,
            positives_all,
            dataset_ids.astype(F32)[None],
            jnp.arange(passages.shape[0], dtype=jnp.int32)[None],
        )
        loss = loss[0, 0]
        d_asked = dot_split(d_logits, passages)
        d_passages = dot_split(d_logits.T, asked)
        spaced = jnp.pad(d_passages[:, None], ((0, 0), (0, SLOTS - 1), (0, 0)))
        d_ups = []
        d_down, d_sum, d_att, d_context, d_gains = back_math(
            jnp.where(is_asking, d_asked, spaced.reshape(every, D)),
            hat2,
            scale2,
            hat,
            scale,
            gains,
            lambda j: slopes[j],
            lambda: out_full,
            lambda j: in_full[:, j * D : j * D + D],
            lambda j: back_full[j * D : j * D + D],
            lambda j, d_up_part: d_ups.append(d_up_part),
        )
        d_up = jnp.concatenate(d_ups, axis=1)
        d_gains = jnp.concatenate(d_gains, axis=0)
        columns = lambda a, width: lax.dynamic_slice(a, (0, own * width), (every, width))
        grad_back = dot_tn(columns(head_act, back_part), d_down)
        grad_in = dot_tn(columns(low, part), d_up)
        grad_out = dot_tn(columns(context_all, part), d_att)
        d_context = after(d_context, grad_back, grad_in, grad_out)
        own_rows = lambda a: lax.dynamic_slice(a, (own * heads, 0), (heads, D))
        d_sum = own_rows(d_sum).reshape(rows, SLOTS, D)
        d_context = own_rows(d_context).reshape(rows, SLOTS, D)

    if links is not None:
        z, y, x = links.at
        where = lambda c, dx, dy: (z + c) % 4 * 4 + (y ^ dy) * 2 + (x ^ dx)
        order = [(c, far, near) for far in range(2) for near in range(2) for c in range(4)]
        source = [[where(c, a, b) for c, a, b in order], [where(c, b, a) for c, a, b in order]]
        source = jnp.stack([jnp.stack(row) for row in source]).astype(jnp.int32)
        sums = [((8, part, D), BF, VMEM)] * 4
    else:
        source = jnp.zeros((2, 1), jnp.int32)
        sums = [((1, D, D), BF, VMEM)] * 2
    outs = launch(
        attend_back,
        [
            (source, SMEM),
            (q_lengths, SMEM),
            (asking, SMEM),
            (inputs, two(SEQ_LEN, D)),
            (query, two(SLOTS, D)),
            (key, two(SEQ_LEN, D)),
            (value, two(D, SEQ_LEN)),
            (d_context, two(SLOTS, D)),
        ],
        [],
        [
            ((rows, WIDE, SEQ_LEN), BF, two(WIDE, SEQ_LEN)),
            ((rows, WIDE, SEQ_LEN), BF, two(WIDE, SEQ_LEN)),
            ((rows, WIDE, D), BF, two(WIDE, D)),
            ((rows, WIDE, D), BF, two(WIDE, D)),
            ((rows, SLOTS, D), BF, two(SLOTS, D)),
        ]
        + sums,
        [
            pltpu.VMEM((2, rows * WIDE, D), BF),
            pltpu.VMEM((2, rows * WIDE, D), BF),
            pltpu.VMEM((D, D), BF),
        ],
        room=60,
        grid=(rows // 2,),
        flops=2 * rows * WIDE * D * (5 * SEQ_LEN + 2 * D),
        moved=16 * MIB,
    )
    low_probs, low_score, wide_query, wide_context, d_query = outs[:5]
    (states_grad,) = launch(
        states_back,
        [
            (low_probs, two(WIDE, SEQ_LEN)),
            (low_score, two(WIDE, SEQ_LEN)),
            (wide_query, two(WIDE, D)),
            (wide_context, two(WIDE, D)),
            (d_query, two(SLOTS, D)),
            (d_sum, two(SLOTS, D)),
        ],
        [g_mix],
        [((rows, SEQ_LEN, D), F32, two(SEQ_LEN, D))],
        [pltpu.VMEM((D, 3 * D), BF), sems(g_mix.copies)],
        room=60,
        grid=(rows // 2,),
        flops=2 * rows * WIDE * D * (3 * D + 2 * SEQ_LEN),
        moved=12 * MIB,
    )
    if links is not None:
        keys, vals, keys_away, vals_away = outs[5:]
        key_in, val_in = move(keys_away, links.x), move(vals_away, links.y)
        keys_away, vals_away = low_sum(keys[4:], key_in[4:]), low_sum(vals[4:], val_in[4:])
        keys, vals = low_sum(keys[:4], key_in[:4]), low_sum(vals[:4], val_in[:4])
        d_query_all = gather_rows(links, d_query.reshape(heads, D), keys)
        key_in, val_in = move(keys_away, links.y), move(vals_away, links.x)
        keep = jnp.concatenate([low_sum(keys, key_in), low_sum(vals, val_in)], axis=2)
        behind = [keep]
        total = keep[0].astype(F32)
        for c in (1, 2, 3):
            total = total + move(keep[c], links.z[c]).astype(F32)
    else:
        behind = []
        d_query_all = gather_rows(links, d_query.reshape(heads, D))
        sums = jnp.concatenate([outs[5][0], outs[6][0]], axis=1)
        total = lax.psum_scatter(sums, "batch", scatter_dimension=0, tiled=True).astype(F32)
    if links is not None:
        encoded = finish(first, act, behind)
    columns = lambda a, width: lax.dynamic_slice(a, (0, own * width), (every, width))
    grad_query = dot_tn(columns(picked_all, part), d_query_all)
    grad_qkv = jnp.concatenate([grad_query, total], axis=1)
    gain_own = lax.dynamic_slice(d_gains, (0, own * part), (4, part))
    return (
        loss,
        encoded[None],
        states_grad[None],
        grad_qkv[None],
        grad_out[None],
        grad_in[None],
        grad_back[None],
        gain_own[0:1],
        gain_own[1:2],
        gain_own[2:3],
        gain_own[3:4],
    )


def solution(mesh):
    rows = P("tower", "batch", None, None)
    matrix = P("tower", "batch", None)
    vector = P("tower", "batch")
    return jax.shard_map(
        body,
        mesh=mesh,
        in_specs=(rows, P("batch", None), P(), P("batch"))
        + (matrix,) * 4
        + (vector,) * 4,
        out_specs=(P(), rows, rows) + (matrix,) * 4 + (vector,) * 4,
        check_vma=False,
    )
```

```python
import functools
import math

import jax
import jax.numpy as jnp
from jax import lax
from jax.experimental import pallas as pl
from jax.experimental.pallas import tpu as pltpu
from jax.sharding import PartitionSpec as P

D = 768
HEADS = 12
HEAD = 64
FF = 3072
SEQ_LEN = 256
QLEN = 64
SLOTS = 4
EPS = 1e-05
NEG = -1000000000.0
BF = jnp.bfloat16
F32 = jnp.float32
MIB = 1 << 20
HEAD_SCALE = 1.0 / math.sqrt(HEAD)
LOGIT_SCALE = 2.0 / math.sqrt(D)
CHUNKS = FF // D
VMEM = pl.BlockSpec(memory_space=pltpu.VMEM)
SMEM = pl.BlockSpec(memory_space=pltpu.SMEM)
ANY = pl.BlockSpec(memory_space=pl.ANY)


def dot(a, b):
    return lax.dot_general(a, b, (((1,), (0,)), ((), ())), preferred_element_type=F32)


def dot_nt(a, b):
    return lax.dot_general(a, b, (((1,), (1,)), ((), ())), preferred_element_type=F32)


def dot_tn(a, b):
    return lax.dot_general(a, b, (((0,), (0,)), ((), ())), preferred_element_type=F32)


def iota(shape, axis):
    return lax.broadcasted_iota(jnp.int32, shape, axis)


def normalise(summed):
    center = summed - jnp.mean(summed, axis=-1, keepdims=True)
    spread = jnp.mean(center * center, axis=-1, keepdims=True)
    scale = lax.rsqrt(spread + EPS)
    return center * scale, scale


def normalise_back(grad, hat, scale, gain):
    d_hat = grad * gain
    mean_d = jnp.mean(d_hat, axis=-1, keepdims=True)
    mean_dh = jnp.mean(d_hat * hat, axis=-1, keepdims=True)
    d_gain = jnp.sum(grad * hat, axis=0, keepdims=True)
    d_shift = jnp.sum(grad, axis=0, keepdims=True)
    return scale * (d_hat - mean_d - hat * mean_dh), d_gain, d_shift


def normal_cdf(values):
    return 0.5 * (1.0 + lax.erf(values * math.sqrt(0.5)))


def gelu(values):
    return values * normal_cdf(values)


def gelu_pair(values):
    cdf = normal_cdf(values)
    bell = jnp.exp(-0.5 * values * values) * (1.0 / math.sqrt(2.0 * math.pi))
    return values * cdf, cdf + values * bell


class Links:
    def __init__(self):
        def table(move):
            at = lambda z, y, x: z * 4 + y * 2 + x
            return [
                (at(z, y, x), at(*move(z, y, x)))
                for z in range(4)
                for y in range(2)
                for x in range(2)
            ]

        by_x = table(lambda z, y, x: (z, y, 1 - x))
        by_y = table(lambda z, y, x: (z, 1 - y, x))
        self.z = [table(lambda z, y, x, c=c: ((z + c) % 4, y, x)) for c in range(4)]
        shifted = lambda pairs: [(a + 16, b + 16) for a, b in pairs]
        self.x, self.y = by_x, by_y
        self.first = by_x + shifted(by_y)
        self.second = by_y + shifted(by_x)
        me = lax.axis_index("batch")
        self.at = (me // 4, me // 2 % 2, me % 2)
        self.question = lax.axis_index("tower") == 0

    def place(self, c, first, second):
        z, y, x = self.at
        dx = jnp.where(self.question, first, second)
        dy = jnp.where(self.question, second, first)
        return (z + c + 4) % 4 * 4 + (y ^ dy) * 2 + (x ^ dx)


def move(value, pairs):
    return lax.ppermute(value, "batch", pairs)


def move_plane(value, pairs):
    return lax.ppermute(value, ("tower", "batch"), pairs)


def after(value, *earlier):
    late = sum(other[(0,) * other.ndim].astype(F32) for other in earlier) > 1e30
    return jnp.where(late, jnp.zeros_like(value), value)


def gather_line(links, shard):
    return jnp.stack([move(shard, links.z[c]) for c in (1, 2, 3)])


def gather_plane(links, line):
    near = move_plane(line, links.first)
    side = move_plane(line, links.second)
    return [line, near, side, move_plane(near, links.second)]


CORNERS = ((0, 0), (1, 0), (0, 1), (1, 1))


class Gathered:
    def __init__(self, pieces, place, bases=None, folds=1):
        self.pieces = pieces
        self.place = place
        self.bases = bases or [0] * len(pieces)
        self.folds = folds
        self.copies = place.shape[0] * folds

    def whole(self):
        return self.pieces[0][0]


def gather_whole(shard):
    whole = lax.all_gather(shard, "batch", axis=0, tiled=True)
    return Gathered([whole[None]], jnp.zeros((1,), jnp.int32))


def gather_pieces(links, own, line, base, folds=1):
    order = [(0, f, s) for f, s in CORNERS] + [(-c, f, s) for f, s in CORNERS for c in (1, 2, 3)]
    place = jnp.stack([links.place(*at) for at in order]).astype(jnp.int32)
    return Gathered([piece[None] for piece in own] + line, place, [base] * 4 + [0] * 4, folds)


def gather_rows(links, rows, behind=None):
    if links is None:
        return lax.all_gather(rows, "batch", axis=0, tiled=True)
    z, y, x = links.at
    count, width = rows.shape
    zs = [rows] + [move(rows, links.z[c]) for c in (1, 2, 3)]
    line = jnp.concatenate([zs[3], zs[2], zs[1], zs[0], zs[3], zs[2], zs[1]])
    line = lax.dynamic_slice(line, ((3 - z) * count, 0), (4 * count, width))
    if behind is not None:
        line = after(line, behind)
    line, near, side, far = gather_plane(links, line)
    by_x, by_y = (jnp.where(links.question, *pair) for pair in ((near, side), (side, near)))
    flip = lambda at, a, b: jnp.where(at == 0, jnp.stack([a, b]), jnp.stack([b, a]))
    full = flip(y, flip(x, line, by_x), flip(x, by_y, far))
    return full.reshape(4, 4, count, width).transpose(1, 0, 2, 3).reshape(16 * count, width)


def low_sum(a, b):
    return (a.astype(F32) + b.astype(F32)).astype(BF)


def load(group, target, sems, low=0):
    place, pieces, weight = group
    width = target.shape[1]
    copies = []
    k = 0
    for piece, base in zip(pieces, weight.bases):
        for c in range(piece.shape[0]):
            unit = piece.shape[1]
            for fold in range(weight.folds):
                row = pl.multiple_of((place[k] * weight.folds + fold) * unit, unit)
                copies.append(
                    pltpu.make_async_copy(
                        piece.at[c, :, pl.ds(base + low + fold * width, width)],
                        target.at[pl.ds(row, unit), :],
                        sems.at[len(copies)],
                    )
                )
            k += 1
    for copy in copies:
        copy.start()
    return copies


def wait_all(copies):
    for copy in copies:
        copy.wait()


def launch(
    kernel, ins, weights, outs, scratch, room, grid=None, flops=0, moved=0, same=None, behind=()
):
    values = list(ins)
    for weight in weights:
        values += [(weight.place, SMEM)] + [(piece, ANY) for piece in weight.pieces]
    values += [(value, ANY) for value in behind]

    def run(*refs):
        at = len(ins)
        groups = []
        for weight in weights:
            end = at + 1 + len(weight.pieces)
            groups.append((refs[at], refs[at + 1 : end], weight))
            at = end
        at += len(behind)
        kernel(refs[: len(ins)], groups, refs[at : at + len(outs)], refs[at + len(outs) :])

    extra = {} if grid is None else {"grid": grid}
    return pl.pallas_call(
        run,
        name=getattr(kernel, "func", kernel).__name__,
        input_output_aliases=same or {},
        in_specs=[spec for _, spec in values],
        out_specs=[spec for _, _, spec in outs],
        out_shape=[jax.ShapeDtypeStruct(shape, dtype) for shape, dtype, _ in outs],
        scratch_shapes=scratch,
        compiler_params=pltpu.CompilerParams(vmem_limit_bytes=room * MIB),
        cost_estimate=pl.CostEstimate(
            flops=int(flops), bytes_accessed=int(moved), transcendentals=0
        ),
        **extra,
    )(*[value for value, _ in values])


def sems(*shape):
    return pltpu.SemaphoreType.DMA(shape)


def rows_spec(many, *tail, skip=0):
    return pl.BlockSpec((many,) + tail, lambda r: (r + skip,) + (0,) * len(tail))


def open_keys(shape, key_axis, row, slot_of_query, lens, ask):
    key_at = iota(shape, key_axis)
    slot = key_at >> 6
    limit = jnp.zeros(shape, jnp.int32)
    for s in range(SLOTS):
        limit = jnp.where(slot == s, lens[row, s] * ask + QLEN * (1 - ask), limit)
    return ((key_at & (QLEN - 1)) < limit) & (slot_of_query * ask == slot * ask)


def mix(skip, ins, groups, outs, scratch):
    lens, asking, x_ref = ins[:3]
    query_ref, key_ref, value_ref, context_ref = outs[:4]
    w, w_gain, w_turned, sem = scratch
    row = pl.program_id(0) + skip

    @pl.when(pl.program_id(0) == 0)
    def _():
        copies = load(groups[0], w, sem.at[0])
        if len(outs) > 4:
            wait_all(load(groups[0], w_gain, sem.at[1], 4 * D))
            outs[4][...] = w_gain[...].astype(F32).T[:8]
        wait_all(copies)
        for j in range(0, D, 128):
            part = w[:, 2 * D + j : 2 * D + j + 128].astype(F32)
            w_turned[j : j + 128, :] = part.T.astype(BF)

    x = x_ref[0]
    mixed = dot(x, w[:, : 2 * D])
    for s in range(SLOTS):
        query_ref[0, s : s + 1, :] = mixed[s * QLEN : s * QLEN + 1, :D]
    query = (mixed[:, :D] * HEAD_SCALE).astype(BF)
    keyset = mixed[:, D:].astype(BF)
    values = dot_nt(w_turned[...], x).astype(BF)
    key_ref[0] = keyset
    value_ref[0] = values
    shape = (SEQ_LEN, SEQ_LEN)
    closed = jnp.where(open_keys(shape, 0, row, iota(shape, 1) >> 6, lens, asking[0]), 0, 1) == 1
    ones = jnp.ones((16, SEQ_LEN), BF)
    nothing = jnp.zeros((SEQ_LEN, 128), BF)
    half_of = iota((SEQ_LEN, 128), 1) // HEAD
    scores = []
    for head in range(HEADS):
        low = head // 2 * 128
        mine = jnp.where(half_of == head % 2, query[:, low : low + 128], nothing)
        scores.append(dot_nt(keyset[:, low : low + 128], mine))
    expos = []
    for score in scores:
        score = jnp.where(closed, NEG, score)
        expos.append(jnp.exp(score - jnp.max(score, axis=0, keepdims=True)).astype(BF))
    parts = []
    for head, expo in enumerate(expos):
        mine = values[head * HEAD : head * HEAD + HEAD]
        summed = dot(jnp.concatenate([mine, ones], axis=0), expo)
        parts.append(summed[:HEAD] / summed[HEAD : HEAD + 1])
    context_ref[0] = jnp.concatenate(parts, axis=0).T.astype(BF)


def up(ins, groups, outs, scratch):
    x_ref, context_ref, gains = ins
    first_ref, act_ref = outs
    w_out, w_in, sem = scratch

    @pl.when(pl.program_id(0) == 0)
    def _():
        wait_all(load(groups[0], w_out, sem.at[0], 3 * D) + load(groups[1], w_in, sem.at[1]))

    many = x_ref.shape[0] * SEQ_LEN
    attended = dot(context_ref[...].reshape(many, D), w_out[...])
    summed = x_ref[...].reshape(many, D).astype(F32) + attended
    first = normalise(summed)[0] * gains[0:1] + gains[1:2]
    low = first.astype(BF)
    first_ref[...] = low.reshape(first_ref.shape)
    for j in range(CHUNKS):
        part = gelu(dot(low, w_in[:, j * D : j * D + D])).astype(BF)
        act_ref[:, :, j * D : j * D + D] = part.reshape(act_ref.shape[0], SEQ_LEN, D)


def down(ins, groups, outs, scratch):
    first_ref, act_ref, gains = ins
    (encoded_ref,) = outs
    w_back, sem = scratch

    @pl.when(pl.program_id(0) == 0)
    def _():
        wait_all(load(groups[0], w_back, sem))

    many = first_ref.shape[0] * SEQ_LEN
    summed = dot(act_ref[...].reshape(many, FF), w_back[...])
    hat = normalise(first_ref[...].reshape(many, D).astype(F32) + summed)[0]
    encoded_ref[...] = (hat * gains[2:3] + gains[3:4]).astype(BF).reshape(encoded_ref.shape)


def head_up_math(context, picked, gains, w_out, w_in, emit):
    hat, scale = normalise(picked.astype(F32) + dot(context, w_out))
    low = (hat * gains[0:1] + gains[1:2]).astype(BF)
    for j in range(CHUNKS):
        act, slope = gelu_pair(dot(low, w_in(j)))
        emit(j, act.astype(BF), slope.astype(BF))
    return hat, scale, low


def head_up(ins, groups, outs, scratch):
    context_ref, picked_ref, gains = ins
    hat_ref, scale_ref, low_ref, act_ref, slope_ref = outs
    w_out, w_in, sem = scratch
    wait_all(load(groups[0], w_out, sem.at[0], 3 * D) + load(groups[1], w_in, sem.at[1]))

    def emit(j, act, slope):
        act_ref[:, j * D : j * D + D] = act
        slope_ref[:, j * D : j * D + D] = slope

    hat, scale, low = head_up_math(
        context_ref[...],
        picked_ref[...],
        gains[...],
        w_out[...],
        lambda j: w_in[:, j * D : j * D + D],
        emit,
    )
    hat_ref[...] = hat
    scale_ref[...] = jnp.broadcast_to(scale, scale_ref.shape)
    low_ref[...] = low


def head_down_math(hat, gains, act, w_back):
    hat2, scale2 = normalise(hat * gains[0:1] + gains[1:2] + dot(act, w_back))
    return hat2, scale2, (hat2 * gains[2:3] + gains[3:4]).astype(BF)


def head_down(ins, groups, outs, scratch):
    hat_ref, act_ref, gains = ins
    hat2_ref, scale2_ref, final_ref = outs
    w_back, sem = scratch
    wait_all(load(groups[0], w_back, sem))
    hat2, scale2, final = head_down_math(hat_ref[...], gains[...], act_ref[...], w_back[...])
    hat2_ref[...] = hat2
    scale2_ref[...] = jnp.broadcast_to(scale2, scale2_ref.shape)
    final_ref[...] = final


def logit_back(asked, passages, positives, ids, place_of):
    logits = dot_nt(asked, passages) * LOGIT_SCALE
    chosen = positives == place_of
    asked_data = jnp.sum(jnp.where(chosen, ids, 0.0), axis=1, keepdims=True)
    open_to = (asked_data == ids) & (place_of >= 0)
    masked = jnp.where(open_to, logits, NEG)
    highest = jnp.max(masked, axis=1, keepdims=True)
    expo = jnp.exp(masked - highest)
    total = jnp.sum(expo, axis=1, keepdims=True)
    target = jnp.sum(jnp.where(chosen, logits, 0.0), axis=1, keepdims=True)
    loss = jnp.sum(highest + jnp.log(total) - target, axis=0, keepdims=True) / asked.shape[0]
    d_logits = (expo / total - jnp.where(chosen, 1.0, 0.0)) * (LOGIT_SCALE / asked.shape[0])
    return loss, d_logits


def dot_split(a, b):
    high = a.astype(BF)
    return dot(high, b) + dot((a - high.astype(F32)).astype(BF), b)


def back_math(d_final, hat2, scale2, hat, scale, gains, slope, w_out, w_in, w_back, emit):
    d_second, d_gain2, d_shift2 = normalise_back(d_final, hat2, scale2, gains[2:3])
    d_down = d_second.astype(BF)
    d_first = d_second
    for j in range(CHUNKS):
        d_up = (dot_nt(d_down, w_back(j)) * slope(j).astype(F32)).astype(BF)
        emit(j, d_up)
        d_first = d_first + dot_nt(d_up, w_in(j))
    d_sum, d_gain, d_shift = normalise_back(d_first, hat, scale, gains[0:1])
    d_att = d_sum.astype(BF)
    d_context = None if w_out is None else dot_nt(d_att, w_out())
    return d_down, d_sum, d_att, d_context, (d_gain, d_shift, d_gain2, d_shift2)


def head_back(ins, groups, outs, scratch):
    asking, own, mine_ref, other_ref, positives, ids, place_of, gains = ins[:8]
    hat2_ref, scale2_ref, hat_ref, scale_ref, slope_ref = ins[8:13]
    act_part, low_part, context_part = ins[13:]
    loss_ref, context_ref, sum_ref, gain_ref, grad_out, grad_in, grad_back = outs
    w_out, w_in, w_back, d_ups, keep_sum, keep_context, sem = scratch
    from_back = load(groups[2], w_back, sem.at[0])
    from_in = load(groups[1], w_in, sem.at[1])
    from_out = load(groups[0], w_out, sem.at[2], 3 * D)
    rows = mine_ref.shape[0]
    is_asking = jnp.full((rows, D), asking[0]) == 1
    mine, other = mine_ref[...], other_ref[...]
    loss, d_logits = logit_back(
        jnp.where(is_asking, mine, other),
        jnp.where(is_asking, other, mine),
        positives[...],
        ids[...],
        place_of[...],
    )
    loss_ref[...] = jnp.broadcast_to(loss, loss_ref.shape)
    square = jnp.full((rows, rows), asking[0]) == 1
    d_final = dot_split(jnp.where(square, d_logits, d_logits.T), other)
    wait_all(from_back)
    wait_all(from_in + from_out)

    def emit(j, d_up):
        d_ups[:, j * D : j * D + D] = d_up

    d_down, d_sum, d_att, d_context, d_gains = back_math(
        d_final,
        hat2_ref[...],
        scale2_ref[:, :1],
        hat_ref[...],
        scale_ref[:, :1],
        gains[...],
        lambda j: slope_ref[:, j * D : j * D + D],
        lambda: w_out[...],
        lambda j: w_in[:, j * D : j * D + D],
        lambda j: w_back[j * D : j * D + D, :],
        emit,
    )
    for i, d_gain in enumerate(d_gains):
        gain_ref[i : i + 1, :] = d_gain
    keep_sum[...] = d_sum
    keep_context[...] = d_context
    count = sum_ref.shape[0] * SLOTS
    at = pl.ds(pl.multiple_of(own[0] * count, 8), count)
    own_sum, own_context = keep_sum[at, :], keep_context[at, :]
    for r in range(sum_ref.shape[0]):
        sum_ref[r] = own_sum[r * SLOTS : r * SLOTS + SLOTS]
        context_ref[r] = own_context[r * SLOTS : r * SLOTS + SLOTS]
    grad_back[...] = dot_tn(act_part[...], d_down)
    grad_in[...] = dot_tn(low_part[...], d_ups[...])
    grad_out[...] = dot_tn(context_part[...], d_att)


WIDE = HEADS * SLOTS


def spread_heads(four):
    eight = jnp.concatenate([four, four], axis=0)
    tall = jnp.concatenate([eight] * (HEADS // 2), axis=0)
    return jnp.where(own_head(), tall, 0.0)


def own_head():
    shape = (WIDE, D)
    return iota(shape, 0) // SLOTS == iota(shape, 1) // HEAD


def attend_back(ins, groups, outs, scratch):
    source, lens, asking, x_ref, picked_ref, key_ref, value_ref, context_ref = ins
    probs_ref, score_ref, query_ref, wide_ref, d_query_ref = outs[:5]
    sum_refs = outs[5:]
    seen, full, total, asked = scratch
    step = pl.program_id(0)
    many = x_ref.shape[0]
    shape = (WIDE, SEQ_LEN)
    every = range(many)
    slot_of = iota(shape, 0) & (SLOTS - 1)
    valid = [open_keys(shape, 1, step * many + i, slot_of, lens, asking[0]) for i in every]
    query = [spread_heads(picked_ref[i]).astype(BF) for i in every]
    d_context = [spread_heads(context_ref[i]).astype(BF) for i in every]
    score = [dot_nt(query[i], key_ref[i]) * HEAD_SCALE for i in every]
    d_probs = [dot(d_context[i], value_ref[i]) for i in every]
    probs, d_score = [], []
    for i in every:
        masked = jnp.where(valid[i], score[i], NEG)
        expo = jnp.exp(masked - jnp.max(masked, axis=-1, keepdims=True))
        prob = expo / jnp.sum(expo, axis=-1, keepdims=True)
        spread = jnp.sum(d_probs[i] * prob, axis=-1, keepdims=True)
        probs.append(prob.astype(BF))
        d_score.append((prob * (d_probs[i] - spread)).astype(BF))
    for i in every:
        probs_ref[i] = probs[i]
        score_ref[i] = d_score[i]
        query_ref[i] = query[i]
        wide_ref[i] = d_context[i]
    d_query = [dot(d_score[i], key_ref[i]) * HEAD_SCALE for i in every]
    by_key = [(dot(d_score[i], x_ref[i]) * HEAD_SCALE).astype(BF) for i in every]
    by_val = [dot(probs[i], x_ref[i]).astype(BF) for i in every]
    fours = []
    for i in every:
        kept = jnp.where(own_head(), d_query[i], 0.0)
        eight = kept[0:8]
        for j in range(8, WIDE, 8):
            eight = eight + kept[j : j + 8]
        fours.append(eight[:SLOTS] + eight[SLOTS:])
        d_query_ref[i] = fours[i].astype(BF)
        at = pl.ds(pl.multiple_of((step * many + i) * WIDE, 16), WIDE)
        seen[0, at, :] = by_key[i]
        seen[1, at, :] = by_val[i]
        full[0, at, :] = query[i]
        full[1, at, :] = d_context[i]

    asked[pl.ds(pl.multiple_of(step * 8, 8), 8), :] = jnp.concatenate(fours, axis=0)

    @pl.when(step == pl.num_programs(0) - 1)
    def _():
        for which in range(2):
            total[...] = dot_tn(seen[which], full[which]).astype(BF)
            k = 0
            for out_ref in sum_refs[which::2]:
                blocks, unit = out_ref.shape[0], out_ref.shape[1]
                for i in range(min(blocks, 8)):
                    at = pl.multiple_of(source[which, k] * unit, unit)
                    out_ref[i] = total[pl.ds(at, unit), :]
                    k += 1
        if len(sum_refs) > 2:
            spare = jnp.zeros((sum_refs[2].shape[1] - asked.shape[0], D), F32)
            sum_refs[2][8] = jnp.concatenate([asked[...], spare], axis=0).astype(BF)


def states_back(ins, groups, outs, scratch):
    probs_ref, score_ref, query_ref, wide_ref, d_query_ref, d_sum_ref = ins
    (grad_ref,) = outs
    w, sem = scratch

    @pl.when(pl.program_id(0) == 0)
    def _():
        wait_all(load(groups[0], w, sem))

    many = grad_ref.shape[0]
    every = range(many)
    tall = many * WIDE
    by_key = (dot_nt(query_ref[...].reshape(tall, D), w[:, D : 2 * D]) * HEAD_SCALE).astype(BF)
    by_val = dot_nt(wide_ref[...].reshape(tall, D), w[:, 2 * D :]).astype(BF)
    fours = [d_query_ref[i].astype(F32) for i in every]
    extra = dot_nt(jnp.concatenate(fours, axis=0).astype(BF), w[:, :D])
    for i in every:
        rows = slice(i * WIDE, i * WIDE + WIDE)
        grad_ref[i] = dot_tn(score_ref[i], by_key[rows]) + dot_tn(probs_ref[i], by_val[rows])
        for s in range(SLOTS):
            at = slice(s * QLEN, s * QLEN + 1)
            add = extra[i * SLOTS + s : i * SLOTS + s + 1] + d_sum_ref[i, s : s + 1]
            grad_ref[i, at, :] = grad_ref[i, at, :] + add


def body(
    states,
    q_lengths,
    dataset_ids,
    positives,
    w_qkv,
    w_out,
    w_in,
    w_back,
    gain_first,
    bias_first,
    gain_second,
    bias_second,
):
    devices = lax.axis_size("batch")
    links = Links() if devices == 16 else None
    own = lax.axis_index("batch")
    is_asking = lax.axis_index("tower") == 0
    asking = is_asking.astype(jnp.int32).reshape(1)
    inputs = states[0]
    rows = inputs.shape[0]
    heads = rows * SLOTS
    every = heads * devices
    part = w_qkv.shape[1]
    back_part = w_back.shape[1]

    vectors = jnp.concatenate([gain_first, bias_first, gain_second, bias_second], axis=0)
    vectors = jnp.pad(vectors.T, ((0, 0), (0, 124)))
    first_needed = jnp.concatenate([w_qkv[0], w_out[0], vectors], axis=1)
    if links is not None:
        folded = jnp.concatenate(jnp.split(w_back[0], CHUNKS, axis=0), axis=1)
        mix_line = gather_line(links, first_needed)
        mix_own = gather_plane(links, first_needed)
        later = jnp.concatenate([w_in[0], folded], axis=1)
        later_own = gather_plane(links, after(later, mix_own[1], mix_own[2]))
        mix_pieces = gather_plane(links, mix_line)
        in_line = gather_line(links, after(w_in[0], mix_line))
        in_pieces = gather_plane(links, after(in_line, mix_pieces[3]))
        g_mix = gather_pieces(links, mix_own, mix_pieces, 0)
        g_in = gather_pieces(links, later_own, in_pieces, 0)
    else:
        g_mix, g_in, g_back = (
            gather_whole(weight) for weight in (first_needed, w_in[0], w_back[0])
        )

    two = functools.partial(rows_spec, 2)
    half = rows // 2
    mixed = []
    for skip in (0, half):
        at = functools.partial(rows_spec, 1, skip=skip)
        kept = [
            ((rows, SLOTS, D), F32, at(SLOTS, D)),
            ((rows, SEQ_LEN, D), BF, at(SEQ_LEN, D)),
            ((rows, D, SEQ_LEN), BF, at(D, SEQ_LEN)),
            ((rows, SEQ_LEN, D), BF, at(SEQ_LEN, D)),
        ]
        behind = []
        if links is not None:
            behind = in_pieces[1:3] if skip else []
        if skip:
            mixed, gains = mixed[:4], mixed[4]
            if links is not None:
                back_line = gather_line(links, after(folded, gains))
        mixed = launch(
            functools.partial(mix, skip),
            [(q_lengths, SMEM), (asking, SMEM), (inputs, at(SEQ_LEN, D))]
            + [(value, ANY) for value in mixed],
            [g_mix],
            kept if skip else kept + [((8, D), F32, VMEM)],
            [
                pltpu.VMEM((D, 3 * D), BF),
                pltpu.VMEM((D, 128), BF),
                pltpu.VMEM((D, D), BF),
                sems(2, g_mix.copies),
            ],
            room=60,
            grid=(half,),
            flops=2 * half * SEQ_LEN * D * (3 * D + 4 * SEQ_LEN),
            moved=10 * MIB,
            same={3 + k: k for k in range(4)} if skip else None,
            behind=behind,
        )
    query, key, value, context = mixed
    picked = inputs.reshape(rows, SLOTS, QLEN, D)[:, :, 0].reshape(heads, D)
    context_own = context.reshape(rows, SLOTS, QLEN, D)[:, :, 0].reshape(heads, D)
    index = positives[:, None]
    note = jnp.pad(jnp.concatenate([index // 256, index % 256], axis=1), ((0, 0), (0, 126)))
    parcel = jnp.concatenate([context_own, picked, note.astype(BF)], axis=1)
    if links is not None:
        parcel = after(parcel, in_pieces[3])
        back_pieces = gather_plane(links, after(back_line, context))
        g_back = gather_pieces(links, later_own, back_pieces, FF, CHUNKS)
    shared = gather_rows(links, parcel)
    context_all, picked_all = shared[:, :D], shared[:, D : 2 * D]
    if links is not None:
        z, y, x = links.at
        plane = lax.dynamic_slice(picked_all, (z * 4 * heads, 0), (4 * heads, D))
        plane = plane.reshape(2, 2, heads, D)
        plane = jnp.where(y == 0, plane, plane[::-1])
        plane = jnp.where(x == 0, plane, plane[:, ::-1]).reshape(4 * heads, 4, 4, part)
        plane = lax.dynamic_slice(plane, (0, 0, own % 4, 0), (4 * heads, 4, 1, part))
        plane = jnp.concatenate([plane, plane], axis=1)
        plane = lax.dynamic_slice(plane, (0, z, 0, 0), (4 * heads, 4, 1, part))
        picked_plane = plane.reshape(4 * heads, 4 * part)
    noted = shared[:, 2 * D : 2 * D + 2].astype(jnp.int32)
    positives_all = noted[:, :1] * 256 + noted[:, 1:]

    def finish(first, act, behind):
        (encoded,) = launch(
            down,
            [(first, two(SEQ_LEN, D)), (act, two(SEQ_LEN, FF)), (gains, VMEM)],
            [g_back],
            [((rows, SEQ_LEN, D), BF, two(SEQ_LEN, D))],
            [pltpu.VMEM((FF, D), BF), sems(g_back.copies)],
            room=60,
            grid=(rows // 2,),
            flops=2 * rows * SEQ_LEN * D * FF,
            moved=24 * MIB,
            behind=behind,
        )
        return encoded

    if links is not None:
        first, act = launch(
            up,
            [(inputs, two(SEQ_LEN, D)), (context, two(SEQ_LEN, D)), (gains, VMEM)],
            [g_mix, g_in],
            [
                ((rows, SEQ_LEN, D), BF, two(SEQ_LEN, D)),
                ((rows, SEQ_LEN, FF), BF, two(SEQ_LEN, FF)),
            ],
            [pltpu.VMEM((D, D), BF), pltpu.VMEM((D, FF), BF), sems(2, g_mix.copies)],
            room=40,
            grid=(rows // 2,),
            flops=2 * rows * SEQ_LEN * D * (D + FF),
            moved=30 * MIB,
        )

        hat, scale, low, head_act, slope = launch(
            head_up,
            [(context_all, VMEM), (picked_all, VMEM), (gains, VMEM)],
            [g_mix, g_in],
            [
                ((every, D), F32, VMEM),
                ((every, 128), F32, VMEM),
                ((every, D), BF, VMEM),
                ((every, FF), BF, VMEM),
                ((every, FF), BF, VMEM),
            ],
            [pltpu.VMEM((D, D), BF), pltpu.VMEM((D, FF), BF), sems(2, g_mix.copies)],
            room=36,
            flops=2 * every * D * (D + FF),
            moved=14 * MIB,
            behind=[act],
        )
        hat2, scale2, final = launch(
            head_down,
            [(hat, VMEM), (head_act, VMEM), (gains, VMEM)],
            [g_back],
            [((every, D), F32, VMEM), ((every, 128), F32, VMEM), ((every, D), BF, VMEM)],
            [pltpu.VMEM((FF, D), BF), sems(g_back.copies)],
            room=24,
            flops=2 * every * D * FF,
            moved=10 * MIB,
        )
    else:
        first, act = launch(
            up,
            [(inputs, two(SEQ_LEN, D)), (context, two(SEQ_LEN, D)), (gains, VMEM)],
            [g_mix, g_in],
            [
                ((rows, SEQ_LEN, D), BF, two(SEQ_LEN, D)),
                ((rows, SEQ_LEN, FF), BF, two(SEQ_LEN, FF)),
            ],
            [pltpu.VMEM((D, D), BF), pltpu.VMEM((D, FF), BF), sems(2, g_mix.copies)],
            room=40,
            grid=(rows // 2,),
            flops=2 * rows * SEQ_LEN * D * (D + FF),
            moved=30 * MIB,
        )

        encoded = finish(first, act, [])
        context_all = after(context_all, encoded)
        out_full = g_mix.whole()[:, 3 * D : 4 * D]
        in_full, back_full = g_in.whole(), g_back.whole()
        acts, slopes = [], []

        def emit(j, act_part, slope_part):
            acts.append(act_part)
            slopes.append(slope_part)

        hat, scale, low = head_up_math(
            context_all,
            picked_all,
            gains,
            out_full,
            lambda j: in_full[:, j * D : j * D + D],
            emit,
        )
        head_act = jnp.concatenate(acts, axis=1)
        hat2, scale2, final = head_down_math(hat, gains, head_act, back_full)

    other = lax.ppermute(final, "tower", [(0, 1), (1, 0)])
    if links is not None:
        column = jnp.arange(every, dtype=jnp.int32)[None]
        place_of = jnp.where(column % SLOTS == 0, column // SLOTS, -1)
        ids = jnp.repeat(dataset_ids.astype(F32), SLOTS)[None]
        columns = lambda a, width: lax.dynamic_slice(a, (0, own * width), (every, width))
        loss, d_context, d_sum, d_gains, grad_out, grad_in, grad_back = launch(
            head_back,
            [
                (asking, SMEM),
                (own.astype(jnp.int32).reshape(1), SMEM),
                (final, VMEM),
                (other, VMEM),
                (positives_all, VMEM),
                (ids, VMEM),
                (place_of, VMEM),
                (gains, VMEM),
                (hat2, VMEM),
                (scale2, VMEM),
                (hat, VMEM),
                (scale, VMEM),
                (slope, VMEM),
                (columns(head_act, back_part), VMEM),
                (columns(low, part), VMEM),
                (columns(context_all, part), VMEM),
            ],
            [g_mix, g_in, g_back],
            [
                ((8, 128), F32, VMEM),
                ((rows, SLOTS, D), F32, VMEM),
                ((rows, SLOTS, D), F32, VMEM),
                ((8, D), F32, VMEM),
                ((part, D), F32, VMEM),
                ((part, FF), F32, VMEM),
                ((back_part, D), F32, VMEM),
            ],
            [
                pltpu.VMEM((D, D), BF),
                pltpu.VMEM((D, FF), BF),
                pltpu.VMEM((FF, D), BF),
                pltpu.VMEM((every, FF), BF),
                pltpu.VMEM((every, D), F32),
                pltpu.VMEM((every, D), F32),
                sems(3, g_back.copies),
            ],
            room=48,
            flops=2 * every * D * (2 * FF + 3 * D),
            moved=20 * MIB,
        )
        loss = loss[0, 0]
    else:
        passages = jnp.where(is_asking, other, final)[::SLOTS]
        asked = jnp.where(is_asking, final, other)
        loss, d_logits = logit_back(
            asked,
            passages,
            positives_all,
            dataset_ids.astype(F32)[None],
            jnp.arange(passages.shape[0], dtype=jnp.int32)[None],
        )
        loss = loss[0, 0]
        d_asked = dot_split(d_logits, passages)
        d_passages = dot_split(d_logits.T, asked)
        spaced = jnp.pad(d_passages[:, None], ((0, 0), (0, SLOTS - 1), (0, 0)))
        d_ups = []
        d_down, d_sum, d_att, d_context, d_gains = back_math(
            jnp.where(is_asking, d_asked, spaced.reshape(every, D)),
            hat2,
            scale2,
            hat,
            scale,
            gains,
            lambda j: slopes[j],
            lambda: out_full,
            lambda j: in_full[:, j * D : j * D + D],
            lambda j: back_full[j * D : j * D + D],
            lambda j, d_up_part: d_ups.append(d_up_part),
        )
        d_up = jnp.concatenate(d_ups, axis=1)
        d_gains = jnp.concatenate(d_gains, axis=0)
        columns = lambda a, width: lax.dynamic_slice(a, (0, own * width), (every, width))
        grad_back = dot_tn(columns(head_act, back_part), d_down)
        grad_in = dot_tn(columns(low, part), d_up)
        grad_out = dot_tn(columns(context_all, part), d_att)
        d_context = after(d_context, grad_back, grad_in, grad_out)
        own_rows = lambda a: lax.dynamic_slice(a, (own * heads, 0), (heads, D))
        d_sum = own_rows(d_sum).reshape(rows, SLOTS, D)
        d_context = own_rows(d_context).reshape(rows, SLOTS, D)

    if links is not None:
        z, y, x = links.at
        where = lambda c, dx, dy: (z + c) % 4 * 4 + (y ^ dy) * 2 + (x ^ dx)
        order = [(c, far, near) for far in range(2) for near in range(2) for c in range(4)]
        source = [[where(c, a, b) for c, a, b in order], [where(c, b, a) for c, a, b in order]]
        source = jnp.stack([jnp.stack(row) for row in source]).astype(jnp.int32)
        sums = [((8, part, D), BF, VMEM)] * 4
        sums[2] = ((9, part, D), BF, VMEM)
    else:
        source = jnp.zeros((2, 1), jnp.int32)
        sums = [((1, D, D), BF, VMEM)] * 2
    outs = launch(
        attend_back,
        [
            (source, SMEM),
            (q_lengths, SMEM),
            (asking, SMEM),
            (inputs, two(SEQ_LEN, D)),
            (query, two(SLOTS, D)),
            (key, two(SEQ_LEN, D)),
            (value, two(D, SEQ_LEN)),
            (d_context, two(SLOTS, D)),
        ],
        [],
        [
            ((rows, WIDE, SEQ_LEN), BF, two(WIDE, SEQ_LEN)),
            ((rows, WIDE, SEQ_LEN), BF, two(WIDE, SEQ_LEN)),
            ((rows, WIDE, D), BF, two(WIDE, D)),
            ((rows, WIDE, D), BF, two(WIDE, D)),
            ((rows, SLOTS, D), BF, two(SLOTS, D)),
        ]
        + sums,
        [
            pltpu.VMEM((2, rows * WIDE, D), BF),
            pltpu.VMEM((2, rows * WIDE, D), BF),
            pltpu.VMEM((D, D), BF),
            pltpu.VMEM((heads, D), F32),
        ],
        room=60,
        grid=(rows // 2,),
        flops=2 * rows * WIDE * D * (5 * SEQ_LEN + 2 * D),
        moved=16 * MIB,
    )
    low_probs, low_score, wide_query, wide_context, d_query = outs[:5]
    (states_grad,) = launch(
        states_back,
        [
            (low_probs, two(WIDE, SEQ_LEN)),
            (low_score, two(WIDE, SEQ_LEN)),
            (wide_query, two(WIDE, D)),
            (wide_context, two(WIDE, D)),
            (d_query, two(SLOTS, D)),
            (d_sum, two(SLOTS, D)),
        ],
        [g_mix],
        [((rows, SEQ_LEN, D), F32, two(SEQ_LEN, D))],
        [pltpu.VMEM((D, 3 * D), BF), sems(g_mix.copies)],
        room=60,
        grid=(rows // 2,),
        flops=2 * rows * WIDE * D * (3 * D + 2 * SEQ_LEN),
        moved=12 * MIB,
    )
    if links is not None:
        keys, vals, keys_away, vals_away = outs[5:]
        key_in, val_in = move(keys_away, links.x), move(vals_away, links.y)
        key_in, val_in = after(key_in, states_grad), after(val_in, states_grad)
        asked = jnp.concatenate([d_query.reshape(heads, D), key_in[8, :heads]])
        keys_away, vals_away = low_sum(keys[4:], key_in[4:8]), low_sum(vals[4:], val_in[4:])
        keys, vals = low_sum(keys[:4], key_in[:4]), low_sum(vals[:4], val_in[:4])
        key_in = move(jnp.concatenate([keys_away, asked[None]]), links.y)
        val_in = move(vals_away, links.x)
        asked = jnp.concatenate([asked, key_in[4]])
        queries = dot_tn(picked_plane, asked).astype(BF).reshape(4, part, D)
        keys, vals = low_sum(keys, key_in[:4]), low_sum(vals, val_in)
        keep = jnp.concatenate([queries, keys, vals], axis=2)
        behind = [keep]
        grad_qkv = keep[0].astype(F32)
        for c in (1, 2, 3):
            grad_qkv = grad_qkv + move(keep[c], links.z[c]).astype(F32)
    else:
        behind = []
        d_query_all = gather_rows(links, d_query.reshape(heads, D))
        sums = jnp.concatenate([outs[5][0], outs[6][0]], axis=1)
        total = lax.psum_scatter(sums, "batch", scatter_dimension=0, tiled=True).astype(F32)
    if links is not None:
        encoded = finish(first, act, behind)
    columns = lambda a, width: lax.dynamic_slice(a, (0, own * width), (every, width))
    if links is None:
        grad_query = dot_tn(columns(picked_all, part), d_query_all)
        grad_qkv = jnp.concatenate([grad_query, total], axis=1)
    gain_own = lax.dynamic_slice(d_gains, (0, own * part), (4, part))
    return (
        loss,
        encoded[None],
        states_grad[None],
        grad_qkv[None],
        grad_out[None],
        grad_in[None],
        grad_back[None],
        gain_own[0:1],
        gain_own[1:2],
        gain_own[2:3],
        gain_own[3:4],
    )


def solution(mesh):
    rows = P("tower", "batch", None, None)
    matrix = P("tower", "batch", None)
    vector = P("tower", "batch")
    return jax.shard_map(
        body,
        mesh=mesh,
        in_specs=(rows, P("batch", None), P(), P("batch"))
        + (matrix,) * 4
        + (vector,) * 4,
        out_specs=(P(), rows, rows) + (matrix,) * 4 + (vector,) * 4,
        check_vma=False,
    )
```

```python
import functools
import math

import jax
import jax.numpy as jnp
from jax import lax
from jax.experimental import pallas as pl
from jax.experimental.pallas import tpu as pltpu
from jax.sharding import PartitionSpec as P

D = 768
HEADS = 12
HEAD = 64
FF = 3072
SEQ_LEN = 256
QLEN = 64
SLOTS = 4
EPS = 1e-05
NEG = -1000000000.0
BF = jnp.bfloat16
F32 = jnp.float32
MIB = 1 << 20
HEAD_SCALE = 1.0 / math.sqrt(HEAD)
LOGIT_SCALE = 2.0 / math.sqrt(D)
CHUNKS = FF // D
VMEM = pl.BlockSpec(memory_space=pltpu.VMEM)
SMEM = pl.BlockSpec(memory_space=pltpu.SMEM)
ANY = pl.BlockSpec(memory_space=pl.ANY)


def dot(a, b):
    return lax.dot_general(a, b, (((1,), (0,)), ((), ())), preferred_element_type=F32)


def dot_nt(a, b):
    return lax.dot_general(a, b, (((1,), (1,)), ((), ())), preferred_element_type=F32)


def dot_tn(a, b):
    return lax.dot_general(a, b, (((0,), (0,)), ((), ())), preferred_element_type=F32)


def iota(shape, axis):
    return lax.broadcasted_iota(jnp.int32, shape, axis)


def normalise(summed):
    center = summed - jnp.mean(summed, axis=-1, keepdims=True)
    spread = jnp.mean(center * center, axis=-1, keepdims=True)
    scale = lax.rsqrt(spread + EPS)
    return center * scale, scale


def normalise_back(grad, hat, scale, gain):
    d_hat = grad * gain
    mean_d = jnp.mean(d_hat, axis=-1, keepdims=True)
    mean_dh = jnp.mean(d_hat * hat, axis=-1, keepdims=True)
    d_gain = jnp.sum(grad * hat, axis=0, keepdims=True)
    d_shift = jnp.sum(grad, axis=0, keepdims=True)
    return scale * (d_hat - mean_d - hat * mean_dh), d_gain, d_shift


def normal_cdf(values):
    return 0.5 * (1.0 + lax.erf(values * math.sqrt(0.5)))


def gelu(values):
    return values * normal_cdf(values)


def gelu_pair(values):
    cdf = normal_cdf(values)
    bell = jnp.exp(-0.5 * values * values) * (1.0 / math.sqrt(2.0 * math.pi))
    return values * cdf, cdf + values * bell


class Links:
    def __init__(self):
        def table(move):
            at = lambda z, y, x: z * 4 + y * 2 + x
            return [
                (at(z, y, x), at(*move(z, y, x)))
                for z in range(4)
                for y in range(2)
                for x in range(2)
            ]

        by_x = table(lambda z, y, x: (z, y, 1 - x))
        by_y = table(lambda z, y, x: (z, 1 - y, x))
        self.z = [table(lambda z, y, x, c=c: ((z + c) % 4, y, x)) for c in range(4)]
        shifted = lambda pairs: [(a + 16, b + 16) for a, b in pairs]
        self.x, self.y = by_x, by_y
        self.first = by_x + shifted(by_y)
        self.second = by_y + shifted(by_x)
        me = lax.axis_index("batch")
        self.at = (me // 4, me // 2 % 2, me % 2)
        self.question = lax.axis_index("tower") == 0

    def place(self, c, first, second):
        z, y, x = self.at
        dx = jnp.where(self.question, first, second)
        dy = jnp.where(self.question, second, first)
        return (z + c + 4) % 4 * 4 + (y ^ dy) * 2 + (x ^ dx)


def move(value, pairs):
    return lax.ppermute(value, "batch", pairs)


def move_plane(value, pairs):
    return lax.ppermute(value, ("tower", "batch"), pairs)


def after(value, *earlier):
    late = sum(other[(0,) * other.ndim].astype(F32) for other in earlier) > 1e30
    return jnp.where(late, jnp.zeros_like(value), value)


def gather_line(links, shard):
    return jnp.stack([move(shard, links.z[c]) for c in (1, 2, 3)])


def gather_plane(links, line):
    near = move_plane(line, links.first)
    side = move_plane(line, links.second)
    return [line, near, side, move_plane(near, links.second)]


CORNERS = ((0, 0), (1, 0), (0, 1), (1, 1))


class Gathered:
    def __init__(self, pieces, place, bases=None, folds=1):
        self.pieces = pieces
        self.place = place
        self.bases = bases or [0] * len(pieces)
        self.folds = folds
        self.copies = place.shape[0] * folds

    def whole(self):
        return self.pieces[0][0]


def gather_whole(shard):
    whole = lax.all_gather(shard, "batch", axis=0, tiled=True)
    return Gathered([whole[None]], jnp.zeros((1,), jnp.int32))


def gather_pieces(links, own, line, base, folds=1):
    order = [(0, f, s) for f, s in CORNERS] + [(-c, f, s) for f, s in CORNERS for c in (1, 2, 3)]
    place = jnp.stack([links.place(*at) for at in order]).astype(jnp.int32)
    return Gathered([piece[None] for piece in own] + line, place, [base] * 4 + [0] * 4, folds)


def gather_rows(links, rows, behind=None):
    if links is None:
        return lax.all_gather(rows, "batch", axis=0, tiled=True)
    z, y, x = links.at
    count, width = rows.shape
    zs = [rows] + [move(rows, links.z[c]) for c in (1, 2, 3)]
    line = jnp.concatenate([zs[3], zs[2], zs[1], zs[0], zs[3], zs[2], zs[1]])
    line = lax.dynamic_slice(line, ((3 - z) * count, 0), (4 * count, width))
    if behind is not None:
        line = after(line, behind)
    line, near, side, far = gather_plane(links, line)
    by_x, by_y = (jnp.where(links.question, *pair) for pair in ((near, side), (side, near)))
    flip = lambda at, a, b: jnp.where(at == 0, jnp.stack([a, b]), jnp.stack([b, a]))
    full = flip(y, flip(x, line, by_x), flip(x, by_y, far))
    return full.reshape(4, 4, count, width).transpose(1, 0, 2, 3).reshape(16 * count, width)


def low_sum(a, b):
    return (a.astype(F32) + b.astype(F32)).astype(BF)


def load(group, target, sems, low=0):
    place, pieces, weight = group
    width = target.shape[1]
    copies = []
    k = 0
    for piece, base in zip(pieces, weight.bases):
        for c in range(piece.shape[0]):
            unit = piece.shape[1]
            for fold in range(weight.folds):
                row = pl.multiple_of((place[k] * weight.folds + fold) * unit, unit)
                copies.append(
                    pltpu.make_async_copy(
                        piece.at[c, :, pl.ds(base + low + fold * width, width)],
                        target.at[pl.ds(row, unit), :],
                        sems.at[len(copies)],
                    )
                )
            k += 1
    for copy in copies:
        copy.start()
    return copies


def wait_all(copies):
    for copy in copies:
        copy.wait()


def launch(
    kernel, ins, weights, outs, scratch, room, grid=None, flops=0, moved=0, same=None, behind=()
):
    values = list(ins)
    for weight in weights:
        values += [(weight.place, SMEM)] + [(piece, ANY) for piece in weight.pieces]
    values += [(value, ANY) for value in behind]

    def run(*refs):
        at = len(ins)
        groups = []
        for weight in weights:
            end = at + 1 + len(weight.pieces)
            groups.append((refs[at], refs[at + 1 : end], weight))
            at = end
        at += len(behind)
        kernel(refs[: len(ins)], groups, refs[at : at + len(outs)], refs[at + len(outs) :])

    extra = {} if grid is None else {"grid": grid}
    return pl.pallas_call(
        run,
        name=getattr(kernel, "func", kernel).__name__,
        input_output_aliases=same or {},
        in_specs=[spec for _, spec in values],
        out_specs=[spec for _, _, spec in outs],
        out_shape=[jax.ShapeDtypeStruct(shape, dtype) for shape, dtype, _ in outs],
        scratch_shapes=scratch,
        compiler_params=pltpu.CompilerParams(vmem_limit_bytes=room * MIB),
        cost_estimate=pl.CostEstimate(
            flops=int(flops), bytes_accessed=int(moved), transcendentals=0
        ),
        **extra,
    )(*[value for value, _ in values])


def sems(*shape):
    return pltpu.SemaphoreType.DMA(shape)


def rows_spec(many, *tail, skip=0):
    return pl.BlockSpec((many,) + tail, lambda r: (r + skip,) + (0,) * len(tail))


def open_keys(shape, key_axis, row, slot_of_query, lens, ask):
    key_at = iota(shape, key_axis)
    slot = key_at >> 6
    limit = jnp.zeros(shape, jnp.int32)
    for s in range(SLOTS):
        limit = jnp.where(slot == s, lens[row, s] * ask + QLEN * (1 - ask), limit)
    return ((key_at & (QLEN - 1)) < limit) & (slot_of_query * ask == slot * ask)


def mix(skip, ins, groups, outs, scratch):
    lens, asking, x_ref = ins[:3]
    query_ref, key_ref, value_ref, context_ref = outs[:4]
    w, w_gain, w_turned, sem = scratch
    row = pl.program_id(0) + skip

    @pl.when(pl.program_id(0) == 0)
    def _():
        copies = load(groups[0], w, sem.at[0])
        if len(outs) > 4:
            wait_all(load(groups[0], w_gain, sem.at[1], 4 * D))
            outs[4][...] = w_gain[...].astype(F32).T[:8]
        wait_all(copies)
        for j in range(0, D, 128):
            part = w[:, 2 * D + j : 2 * D + j + 128].astype(F32)
            w_turned[j : j + 128, :] = part.T.astype(BF)

    x = x_ref[0]
    mixed = dot(x, w[:, : 2 * D])
    for s in range(SLOTS):
        query_ref[0, s : s + 1, :] = mixed[s * QLEN : s * QLEN + 1, :D]
    query = (mixed[:, :D] * HEAD_SCALE).astype(BF)
    keyset = mixed[:, D:].astype(BF)
    values = dot_nt(w_turned[...], x).astype(BF)
    key_ref[0] = keyset
    value_ref[0] = values
    shape = (SEQ_LEN, SEQ_LEN)
    closed = jnp.where(open_keys(shape, 0, row, iota(shape, 1) >> 6, lens, asking[0]), 0, 1) == 1
    ones = jnp.ones((16, SEQ_LEN), BF)
    nothing = jnp.zeros((SEQ_LEN, 128), BF)
    half_of = iota((SEQ_LEN, 128), 1) // HEAD
    scores = []
    for head in range(HEADS):
        low = head // 2 * 128
        mine = jnp.where(half_of == head % 2, query[:, low : low + 128], nothing)
        scores.append(dot_nt(keyset[:, low : low + 128], mine))
    expos = []
    for score in scores:
        score = jnp.where(closed, NEG, score)
        expos.append(jnp.exp(score - jnp.max(score, axis=0, keepdims=True)).astype(BF))
    parts = []
    for head, expo in enumerate(expos):
        mine = values[head * HEAD : head * HEAD + HEAD]
        summed = dot(jnp.concatenate([mine, ones], axis=0), expo)
        parts.append(summed[:HEAD] / summed[HEAD : HEAD + 1])
    context_ref[0] = jnp.concatenate(parts, axis=0).T.astype(BF)


def up(ins, groups, outs, scratch):
    x_ref, context_ref, gains = ins
    first_ref, act_ref = outs
    w_out, w_in, sem = scratch

    @pl.when(pl.program_id(0) == 0)
    def _():
        wait_all(load(groups[0], w_out, sem.at[0], 3 * D) + load(groups[1], w_in, sem.at[1]))

    many = x_ref.shape[0] * SEQ_LEN
    attended = dot(context_ref[...].reshape(many, D), w_out[...])
    summed = x_ref[...].reshape(many, D).astype(F32) + attended
    first = normalise(summed)[0] * gains[0:1] + gains[1:2]
    low = first.astype(BF)
    first_ref[...] = low.reshape(first_ref.shape)
    for j in range(CHUNKS):
        part = gelu(dot(low, w_in[:, j * D : j * D + D])).astype(BF)
        act_ref[:, :, j * D : j * D + D] = part.reshape(act_ref.shape[0], SEQ_LEN, D)


def down(ins, groups, outs, scratch):
    first_ref, act_ref, gains = ins
    (encoded_ref,) = outs
    w_back, sem = scratch

    @pl.when(pl.program_id(0) == 0)
    def _():
        wait_all(load(groups[0], w_back, sem))

    many = first_ref.shape[0] * SEQ_LEN
    summed = dot(act_ref[...].reshape(many, FF), w_back[...])
    hat = normalise(first_ref[...].reshape(many, D).astype(F32) + summed)[0]
    encoded_ref[...] = (hat * gains[2:3] + gains[3:4]).astype(BF).reshape(encoded_ref.shape)


def head_up_math(context, picked, gains, w_out, w_in, emit):
    hat, scale = normalise(picked.astype(F32) + dot(context, w_out))
    low = (hat * gains[0:1] + gains[1:2]).astype(BF)
    for j in range(CHUNKS):
        act, slope = gelu_pair(dot(low, w_in(j)))
        emit(j, act.astype(BF), slope.astype(BF))
    return hat, scale, low


def head_up(ins, groups, outs, scratch):
    context_ref, picked_ref, gains = ins
    hat_ref, scale_ref, low_ref, act_ref, slope_ref = outs
    w_out, w_in, sem = scratch
    wait_all(load(groups[0], w_out, sem.at[0], 3 * D) + load(groups[1], w_in, sem.at[1]))

    def emit(j, act, slope):
        act_ref[:, j * D : j * D + D] = act
        slope_ref[:, j * D : j * D + D] = slope

    hat, scale, low = head_up_math(
        context_ref[...],
        picked_ref[...],
        gains[...],
        w_out[...],
        lambda j: w_in[:, j * D : j * D + D],
        emit,
    )
    hat_ref[...] = hat
    scale_ref[...] = jnp.broadcast_to(scale, scale_ref.shape)
    low_ref[...] = low


def head_down_math(hat, gains, act, w_back):
    hat2, scale2 = normalise(hat * gains[0:1] + gains[1:2] + dot(act, w_back))
    return hat2, scale2, (hat2 * gains[2:3] + gains[3:4]).astype(BF)


def head_down(ins, groups, outs, scratch):
    hat_ref, act_ref, gains = ins
    hat2_ref, scale2_ref, final_ref = outs
    w_back, sem = scratch
    wait_all(load(groups[0], w_back, sem))
    hat2, scale2, final = head_down_math(hat_ref[...], gains[...], act_ref[...], w_back[...])
    hat2_ref[...] = hat2
    scale2_ref[...] = jnp.broadcast_to(scale2, scale2_ref.shape)
    final_ref[...] = final


def logit_back(asked, passages, positives, ids, place_of):
    logits = dot_nt(asked, passages) * LOGIT_SCALE
    chosen = positives == place_of
    asked_data = jnp.sum(jnp.where(chosen, ids, 0.0), axis=1, keepdims=True)
    open_to = (asked_data == ids) & (place_of >= 0)
    masked = jnp.where(open_to, logits, NEG)
    highest = jnp.max(masked, axis=1, keepdims=True)
    expo = jnp.exp(masked - highest)
    total = jnp.sum(expo, axis=1, keepdims=True)
    target = jnp.sum(jnp.where(chosen, logits, 0.0), axis=1, keepdims=True)
    loss = jnp.sum(highest + jnp.log(total) - target, axis=0, keepdims=True) / asked.shape[0]
    d_logits = (expo / total - jnp.where(chosen, 1.0, 0.0)) * (LOGIT_SCALE / asked.shape[0])
    return loss, d_logits


def dot_split(a, b):
    high = a.astype(BF)
    return dot(high, b) + dot((a - high.astype(F32)).astype(BF), b)


def back_math(d_final, hat2, scale2, hat, scale, gains, slope, w_out, w_in, w_back, emit):
    d_second, d_gain2, d_shift2 = normalise_back(d_final, hat2, scale2, gains[2:3])
    d_down = d_second.astype(BF)
    d_first = d_second
    for j in range(CHUNKS):
        d_up = (dot_nt(d_down, w_back(j)) * slope(j).astype(F32)).astype(BF)
        emit(j, d_up)
        d_first = d_first + dot_nt(d_up, w_in(j))
    d_sum, d_gain, d_shift = normalise_back(d_first, hat, scale, gains[0:1])
    d_att = d_sum.astype(BF)
    d_context = None if w_out is None else dot_nt(d_att, w_out())
    return d_down, d_sum, d_att, d_context, (d_gain, d_shift, d_gain2, d_shift2)


def head_back(ins, groups, outs, scratch):
    asking, own, mine_ref, other_ref, positives, ids, place_of, gains = ins[:8]
    hat2_ref, scale2_ref, hat_ref, scale_ref, slope_ref = ins[8:13]
    act_part, low_part, context_part = ins[13:]
    loss_ref, context_ref, sum_ref, gain_ref, grad_out, grad_in, grad_back = outs
    w_out, w_in, w_back, d_ups, keep_sum, keep_context, near, slopes, near_sem, sem = scratch
    from_near = [
        pltpu.make_async_copy(ref, near.at[k, :, pl.ds(0, ref.shape[1])], near_sem.at[k])
        for k, ref in enumerate((hat2_ref, scale2_ref, hat_ref, scale_ref))
    ]
    from_near.append(pltpu.make_async_copy(slope_ref, slopes, near_sem.at[4]))
    for copy in from_near:
        copy.start()
    from_back = load(groups[2], w_back, sem.at[0])
    from_in = load(groups[1], w_in, sem.at[1])
    from_out = load(groups[0], w_out, sem.at[2], 3 * D)
    rows = mine_ref.shape[0]
    is_asking = jnp.full((rows, D), asking[0]) == 1
    mine, other = mine_ref[...], other_ref[...]
    loss, d_logits = logit_back(
        jnp.where(is_asking, mine, other),
        jnp.where(is_asking, other, mine),
        positives[...],
        ids[...],
        place_of[...],
    )
    loss_ref[...] = jnp.broadcast_to(loss, loss_ref.shape)
    square = jnp.full((rows, rows), asking[0]) == 1
    d_final = dot_split(jnp.where(square, d_logits, d_logits.T), other)
    wait_all(from_near + from_back)

    def in_part(j):
        if j == 0:
            wait_all(from_in)
        return w_in[:, j * D : j * D + D]

    def out_whole():
        wait_all(from_out)
        return w_out[...]

    def emit(j, d_up):
        d_ups[:, j * D : j * D + D] = d_up

    d_down, d_sum, d_att, d_context, d_gains = back_math(
        d_final,
        near[0],
        near[1, :, :1],
        near[2],
        near[3, :, :1],
        gains[...],
        lambda j: slopes[:, j * D : j * D + D],
        out_whole,
        in_part,
        lambda j: w_back[j * D : j * D + D, :],
        emit,
    )
    for i, d_gain in enumerate(d_gains):
        gain_ref[i : i + 1, :] = d_gain
    keep_sum[...] = d_sum
    keep_context[...] = d_context
    count = sum_ref.shape[0] * SLOTS
    at = pl.ds(pl.multiple_of(own[0] * count, 8), count)
    own_sum, own_context = keep_sum[at, :], keep_context[at, :]
    for r in range(sum_ref.shape[0]):
        sum_ref[r] = own_sum[r * SLOTS : r * SLOTS + SLOTS]
        context_ref[r] = own_context[r * SLOTS : r * SLOTS + SLOTS]
    grad_back[...] = dot_tn(act_part[...], d_down)
    grad_in[...] = dot_tn(low_part[...], d_ups[...])
    grad_out[...] = dot_tn(context_part[...], d_att)


WIDE = HEADS * SLOTS


def spread_heads(four):
    eight = jnp.concatenate([four, four], axis=0)
    tall = jnp.concatenate([eight] * (HEADS // 2), axis=0)
    return jnp.where(own_head(), tall, 0.0)


def own_head():
    shape = (WIDE, D)
    return iota(shape, 0) // SLOTS == iota(shape, 1) // HEAD


def attend_back(ins, groups, outs, scratch):
    source, lens, asking, x_ref, picked_ref, key_ref, value_ref, context_ref = ins
    probs_ref, score_ref, query_ref, wide_ref, d_query_ref = outs[:5]
    sum_refs = outs[5:]
    seen, full, total, asked = scratch
    step = pl.program_id(0)
    many = x_ref.shape[0]
    shape = (WIDE, SEQ_LEN)
    every = range(many)
    slot_of = iota(shape, 0) & (SLOTS - 1)
    valid = [open_keys(shape, 1, step * many + i, slot_of, lens, asking[0]) for i in every]
    query = [spread_heads(picked_ref[i]).astype(BF) for i in every]
    d_context = [spread_heads(context_ref[i]).astype(BF) for i in every]
    score = [dot_nt(query[i], key_ref[i]) * HEAD_SCALE for i in every]
    d_probs = [dot(d_context[i], value_ref[i]) for i in every]
    probs, d_score = [], []
    for i in every:
        masked = jnp.where(valid[i], score[i], NEG)
        expo = jnp.exp(masked - jnp.max(masked, axis=-1, keepdims=True))
        prob = expo / jnp.sum(expo, axis=-1, keepdims=True)
        spread = jnp.sum(d_probs[i] * prob, axis=-1, keepdims=True)
        probs.append(prob.astype(BF))
        d_score.append((prob * (d_probs[i] - spread)).astype(BF))
    for i in every:
        probs_ref[i] = probs[i]
        score_ref[i] = d_score[i]
        query_ref[i] = query[i]
        wide_ref[i] = d_context[i]
    d_query = [dot(d_score[i], key_ref[i]) * HEAD_SCALE for i in every]
    by_key = [(dot(d_score[i], x_ref[i]) * HEAD_SCALE).astype(BF) for i in every]
    by_val = [dot(probs[i], x_ref[i]).astype(BF) for i in every]
    fours = []
    for i in every:
        kept = jnp.where(own_head(), d_query[i], 0.0)
        eight = kept[0:8]
        for j in range(8, WIDE, 8):
            eight = eight + kept[j : j + 8]
        fours.append(eight[:SLOTS] + eight[SLOTS:])
        d_query_ref[i] = fours[i].astype(BF)
        at = pl.ds(pl.multiple_of((step * many + i) * WIDE, 16), WIDE)
        seen[0, at, :] = by_key[i]
        seen[1, at, :] = by_val[i]
        full[0, at, :] = query[i]
        full[1, at, :] = d_context[i]

    asked[pl.ds(pl.multiple_of(step * 8, 8), 8), :] = jnp.concatenate(fours, axis=0)

    @pl.when(step == pl.num_programs(0) - 1)
    def _():
        for which in range(2):
            total[...] = dot_tn(seen[which], full[which]).astype(BF)
            k = 0
            for out_ref in sum_refs[which::2]:
                blocks, unit = out_ref.shape[0], out_ref.shape[1]
                for i in range(min(blocks, 8)):
                    at = pl.multiple_of(source[which, k] * unit, unit)
                    out_ref[i] = total[pl.ds(at, unit), :]
                    k += 1
        if len(sum_refs) > 2:
            spare = jnp.zeros((sum_refs[2].shape[1] - asked.shape[0], D), F32)
            sum_refs[2][8] = jnp.concatenate([asked[...], spare], axis=0).astype(BF)


def states_back(ins, groups, outs, scratch):
    probs_ref, score_ref, query_ref, wide_ref, d_query_ref, d_sum_ref = ins
    (grad_ref,) = outs
    w, sem = scratch

    @pl.when(pl.program_id(0) == 0)
    def _():
        wait_all(load(groups[0], w, sem))

    many = grad_ref.shape[0]
    every = range(many)
    tall = many * WIDE
    by_key = (dot_nt(query_ref[...].reshape(tall, D), w[:, D : 2 * D]) * HEAD_SCALE).astype(BF)
    by_val = dot_nt(wide_ref[...].reshape(tall, D), w[:, 2 * D :]).astype(BF)
    fours = [d_query_ref[i].astype(F32) for i in every]
    extra = dot_nt(jnp.concatenate(fours, axis=0).astype(BF), w[:, :D])
    for i in every:
        rows = slice(i * WIDE, i * WIDE + WIDE)
        grad_ref[i] = dot_tn(score_ref[i], by_key[rows]) + dot_tn(probs_ref[i], by_val[rows])
        for s in range(SLOTS):
            at = slice(s * QLEN, s * QLEN + 1)
            add = extra[i * SLOTS + s : i * SLOTS + s + 1] + d_sum_ref[i, s : s + 1]
            grad_ref[i, at, :] = grad_ref[i, at, :] + add


def body(
    states,
    q_lengths,
    dataset_ids,
    positives,
    w_qkv,
    w_out,
    w_in,
    w_back,
    gain_first,
    bias_first,
    gain_second,
    bias_second,
):
    devices = lax.axis_size("batch")
    links = Links() if devices == 16 else None
    own = lax.axis_index("batch")
    is_asking = lax.axis_index("tower") == 0
    asking = is_asking.astype(jnp.int32).reshape(1)
    inputs = states[0]
    rows = inputs.shape[0]
    heads = rows * SLOTS
    every = heads * devices
    part = w_qkv.shape[1]
    back_part = w_back.shape[1]

    vectors = jnp.concatenate([gain_first, bias_first, gain_second, bias_second], axis=0)
    vectors = jnp.pad(vectors.T, ((0, 0), (0, 124)))
    first_needed = jnp.concatenate([w_qkv[0], w_out[0], vectors], axis=1)
    if links is not None:
        folded = jnp.concatenate(jnp.split(w_back[0], CHUNKS, axis=0), axis=1)
        mix_line = gather_line(links, first_needed)
        mix_own = gather_plane(links, first_needed)
        later = jnp.concatenate([w_in[0], folded], axis=1)
        later_own = gather_plane(links, after(later, mix_own[1], mix_own[2]))
        mix_pieces = gather_plane(links, mix_line)
        in_line = gather_line(links, after(w_in[0], mix_line))
        in_pieces = gather_plane(links, after(in_line, mix_pieces[3]))
        g_mix = gather_pieces(links, mix_own, mix_pieces, 0)
        g_in = gather_pieces(links, later_own, in_pieces, 0)
    else:
        g_mix, g_in, g_back = (
            gather_whole(weight) for weight in (first_needed, w_in[0], w_back[0])
        )

    two = functools.partial(rows_spec, 2)
    half = rows // 2
    mixed = []
    for skip in (0, half):
        at = functools.partial(rows_spec, 1, skip=skip)
        kept = [
            ((rows, SLOTS, D), F32, at(SLOTS, D)),
            ((rows, SEQ_LEN, D), BF, at(SEQ_LEN, D)),
            ((rows, D, SEQ_LEN), BF, at(D, SEQ_LEN)),
            ((rows, SEQ_LEN, D), BF, at(SEQ_LEN, D)),
        ]
        behind = []
        if links is not None:
            behind = in_pieces[1:3] if skip else []
        if skip:
            mixed, gains = mixed[:4], mixed[4]
            if links is not None:
                back_line = gather_line(links, after(folded, gains))
        mixed = launch(
            functools.partial(mix, skip),
            [(q_lengths, SMEM), (asking, SMEM), (inputs, at(SEQ_LEN, D))]
            + [(value, ANY) for value in mixed],
            [g_mix],
            kept if skip else kept + [((8, D), F32, VMEM)],
            [
                pltpu.VMEM((D, 3 * D), BF),
                pltpu.VMEM((D, 128), BF),
                pltpu.VMEM((D, D), BF),
                sems(2, g_mix.copies),
            ],
            room=60,
            grid=(half,),
            flops=2 * half * SEQ_LEN * D * (3 * D + 4 * SEQ_LEN),
            moved=10 * MIB,
            same={3 + k: k for k in range(4)} if skip else None,
            behind=behind,
        )
    query, key, value, context = mixed
    picked = inputs.reshape(rows, SLOTS, QLEN, D)[:, :, 0].reshape(heads, D)
    context_own = context.reshape(rows, SLOTS, QLEN, D)[:, :, 0].reshape(heads, D)
    index = positives[:, None]
    note = jnp.pad(jnp.concatenate([index // 256, index % 256], axis=1), ((0, 0), (0, 126)))
    parcel = jnp.concatenate([context_own, picked, note.astype(BF)], axis=1)
    if links is not None:
        parcel = after(parcel, in_pieces[3])
        back_pieces = gather_plane(links, after(back_line, context))
        g_back = gather_pieces(links, later_own, back_pieces, FF, CHUNKS)
    shared = gather_rows(links, parcel)
    context_all, picked_all = shared[:, :D], shared[:, D : 2 * D]
    if links is not None:
        z, y, x = links.at
        plane = lax.dynamic_slice(picked_all, (z * 4 * heads, 0), (4 * heads, D))
        plane = plane.reshape(2, 2, heads, D)
        plane = jnp.where(y == 0, plane, plane[::-1])
        plane = jnp.where(x == 0, plane, plane[:, ::-1]).reshape(4 * heads, 4, 4, part)
        plane = lax.dynamic_slice(plane, (0, 0, own % 4, 0), (4 * heads, 4, 1, part))
        plane = jnp.concatenate([plane, plane], axis=1)
        plane = lax.dynamic_slice(plane, (0, z, 0, 0), (4 * heads, 4, 1, part))
        picked_plane = plane.reshape(4 * heads, 4 * part)
    noted = shared[:, 2 * D : 2 * D + 2].astype(jnp.int32)
    positives_all = noted[:, :1] * 256 + noted[:, 1:]

    def finish(first, act, behind):
        (encoded,) = launch(
            down,
            [(first, two(SEQ_LEN, D)), (act, two(SEQ_LEN, FF)), (gains, VMEM)],
            [g_back],
            [((rows, SEQ_LEN, D), BF, two(SEQ_LEN, D))],
            [pltpu.VMEM((FF, D), BF), sems(g_back.copies)],
            room=60,
            grid=(rows // 2,),
            flops=2 * rows * SEQ_LEN * D * FF,
            moved=24 * MIB,
            behind=behind,
        )
        return encoded

    if links is not None:
        first, act = launch(
            up,
            [(inputs, two(SEQ_LEN, D)), (context, two(SEQ_LEN, D)), (gains, VMEM)],
            [g_mix, g_in],
            [
                ((rows, SEQ_LEN, D), BF, two(SEQ_LEN, D)),
                ((rows, SEQ_LEN, FF), BF, two(SEQ_LEN, FF)),
            ],
            [pltpu.VMEM((D, D), BF), pltpu.VMEM((D, FF), BF), sems(2, g_mix.copies)],
            room=40,
            grid=(rows // 2,),
            flops=2 * rows * SEQ_LEN * D * (D + FF),
            moved=30 * MIB,
        )

        hat, scale, low, head_act, slope = launch(
            head_up,
            [(context_all, VMEM), (picked_all, VMEM), (gains, VMEM)],
            [g_mix, g_in],
            [
                ((every, D), F32, VMEM),
                ((every, 128), F32, VMEM),
                ((every, D), BF, VMEM),
                ((every, FF), BF, VMEM),
                ((every, FF), BF, VMEM),
            ],
            [pltpu.VMEM((D, D), BF), pltpu.VMEM((D, FF), BF), sems(2, g_mix.copies)],
            room=36,
            flops=2 * every * D * (D + FF),
            moved=14 * MIB,
            behind=[act],
        )
        hat2, scale2, final = launch(
            head_down,
            [(hat, VMEM), (head_act, VMEM), (gains, VMEM)],
            [g_back],
            [((every, D), F32, VMEM), ((every, 128), F32, VMEM), ((every, D), BF, VMEM)],
            [pltpu.VMEM((FF, D), BF), sems(g_back.copies)],
            room=24,
            flops=2 * every * D * FF,
            moved=10 * MIB,
        )
    else:
        first, act = launch(
            up,
            [(inputs, two(SEQ_LEN, D)), (context, two(SEQ_LEN, D)), (gains, VMEM)],
            [g_mix, g_in],
            [
                ((rows, SEQ_LEN, D), BF, two(SEQ_LEN, D)),
                ((rows, SEQ_LEN, FF), BF, two(SEQ_LEN, FF)),
            ],
            [pltpu.VMEM((D, D), BF), pltpu.VMEM((D, FF), BF), sems(2, g_mix.copies)],
            room=40,
            grid=(rows // 2,),
            flops=2 * rows * SEQ_LEN * D * (D + FF),
            moved=30 * MIB,
        )

        encoded = finish(first, act, [])
        context_all = after(context_all, encoded)
        out_full = g_mix.whole()[:, 3 * D : 4 * D]
        in_full, back_full = g_in.whole(), g_back.whole()
        acts, slopes = [], []

        def emit(j, act_part, slope_part):
            acts.append(act_part)
            slopes.append(slope_part)

        hat, scale, low = head_up_math(
            context_all,
            picked_all,
            gains,
            out_full,
            lambda j: in_full[:, j * D : j * D + D],
            emit,
        )
        head_act = jnp.concatenate(acts, axis=1)
        hat2, scale2, final = head_down_math(hat, gains, head_act, back_full)

    other = lax.ppermute(final, "tower", [(0, 1), (1, 0)])
    if links is not None:
        column = jnp.arange(every, dtype=jnp.int32)[None]
        place_of = jnp.where(column % SLOTS == 0, column // SLOTS, -1)
        ids = jnp.repeat(dataset_ids.astype(F32), SLOTS)[None]
        columns = lambda a, width: lax.dynamic_slice(a, (0, own * width), (every, width))
        loss, d_context, d_sum, d_gains, grad_out, grad_in, grad_back = launch(
            head_back,
            [
                (asking, SMEM),
                (own.astype(jnp.int32).reshape(1), SMEM),
                (final, VMEM),
                (other, VMEM),
                (positives_all, VMEM),
                (ids, VMEM),
                (place_of, VMEM),
                (gains, VMEM),
                (hat2, ANY),
                (scale2, ANY),
                (hat, ANY),
                (scale, ANY),
                (slope, ANY),
                (columns(head_act, back_part), VMEM),
                (columns(low, part), VMEM),
                (columns(context_all, part), VMEM),
            ],
            [g_mix, g_in, g_back],
            [
                ((8, 128), F32, VMEM),
                ((rows, SLOTS, D), F32, VMEM),
                ((rows, SLOTS, D), F32, VMEM),
                ((8, D), F32, VMEM),
                ((part, D), F32, VMEM),
                ((part, FF), F32, VMEM),
                ((back_part, D), F32, VMEM),
            ],
            [
                pltpu.VMEM((D, D), BF),
                pltpu.VMEM((D, FF), BF),
                pltpu.VMEM((FF, D), BF),
                pltpu.VMEM((every, FF), BF),
                pltpu.VMEM((every, D), F32),
                pltpu.VMEM((every, D), F32),
                pltpu.VMEM((4, every, D), F32),
                pltpu.VMEM((every, FF), BF),
                sems(5),
                sems(3, g_back.copies),
            ],
            room=48,
            flops=2 * every * D * (2 * FF + 3 * D),
            moved=20 * MIB,
        )
        loss = loss[0, 0]
    else:
        passages = jnp.where(is_asking, other, final)[::SLOTS]
        asked = jnp.where(is_asking, final, other)
        loss, d_logits = logit_back(
            asked,
            passages,
            positives_all,
            dataset_ids.astype(F32)[None],
            jnp.arange(passages.shape[0], dtype=jnp.int32)[None],
        )
        loss = loss[0, 0]
        d_asked = dot_split(d_logits, passages)
        d_passages = dot_split(d_logits.T, asked)
        spaced = jnp.pad(d_passages[:, None], ((0, 0), (0, SLOTS - 1), (0, 0)))
        d_ups = []
        d_down, d_sum, d_att, d_context, d_gains = back_math(
            jnp.where(is_asking, d_asked, spaced.reshape(every, D)),
            hat2,
            scale2,
            hat,
            scale,
            gains,
            lambda j: slopes[j],
            lambda: out_full,
            lambda j: in_full[:, j * D : j * D + D],
            lambda j: back_full[j * D : j * D + D],
            lambda j, d_up_part: d_ups.append(d_up_part),
        )
        d_up = jnp.concatenate(d_ups, axis=1)
        d_gains = jnp.concatenate(d_gains, axis=0)
        columns = lambda a, width: lax.dynamic_slice(a, (0, own * width), (every, width))
        grad_back = dot_tn(columns(head_act, back_part), d_down)
        grad_in = dot_tn(columns(low, part), d_up)
        grad_out = dot_tn(columns(context_all, part), d_att)
        d_context = after(d_context, grad_back, grad_in, grad_out)
        own_rows = lambda a: lax.dynamic_slice(a, (own * heads, 0), (heads, D))
        d_sum = own_rows(d_sum).reshape(rows, SLOTS, D)
        d_context = own_rows(d_context).reshape(rows, SLOTS, D)

    if links is not None:
        z, y, x = links.at
        where = lambda c, dx, dy: (z + c) % 4 * 4 + (y ^ dy) * 2 + (x ^ dx)
        order = [(c, far, near) for far in range(2) for near in range(2) for c in range(4)]
        source = [[where(c, a, b) for c, a, b in order], [where(c, b, a) for c, a, b in order]]
        source = jnp.stack([jnp.stack(row) for row in source]).astype(jnp.int32)
        sums = [((8, part, D), BF, VMEM)] * 4
        sums[2] = ((9, part, D), BF, VMEM)
    else:
        source = jnp.zeros((2, 1), jnp.int32)
        sums = [((1, D, D), BF, VMEM)] * 2
    outs = launch(
        attend_back,
        [
            (source, SMEM),
            (q_lengths, SMEM),
            (asking, SMEM),
            (inputs, two(SEQ_LEN, D)),
            (query, two(SLOTS, D)),
            (key, two(SEQ_LEN, D)),
            (value, two(D, SEQ_LEN)),
            (d_context, two(SLOTS, D)),
        ],
        [],
        [
            ((rows, WIDE, SEQ_LEN), BF, two(WIDE, SEQ_LEN)),
            ((rows, WIDE, SEQ_LEN), BF, two(WIDE, SEQ_LEN)),
            ((rows, WIDE, D), BF, two(WIDE, D)),
            ((rows, WIDE, D), BF, two(WIDE, D)),
            ((rows, SLOTS, D), BF, two(SLOTS, D)),
        ]
        + sums,
        [
            pltpu.VMEM((2, rows * WIDE, D), BF),
            pltpu.VMEM((2, rows * WIDE, D), BF),
            pltpu.VMEM((D, D), BF),
            pltpu.VMEM((heads, D), F32),
        ],
        room=60,
        grid=(rows // 2,),
        flops=2 * rows * WIDE * D * (5 * SEQ_LEN + 2 * D),
        moved=16 * MIB,
    )
    low_probs, low_score, wide_query, wide_context, d_query = outs[:5]
    (states_grad,) = launch(
        states_back,
        [
            (low_probs, two(WIDE, SEQ_LEN)),
            (low_score, two(WIDE, SEQ_LEN)),
            (wide_query, two(WIDE, D)),
            (wide_context, two(WIDE, D)),
            (d_query, two(SLOTS, D)),
            (d_sum, two(SLOTS, D)),
        ],
        [g_mix],
        [((rows, SEQ_LEN, D), F32, two(SEQ_LEN, D))],
        [pltpu.VMEM((D, 3 * D), BF), sems(g_mix.copies)],
        room=60,
        grid=(rows // 2,),
        flops=2 * rows * WIDE * D * (3 * D + 2 * SEQ_LEN),
        moved=12 * MIB,
    )
    if links is not None:
        keys, vals, keys_away, vals_away = outs[5:]
        key_in, val_in = move(keys_away, links.x), move(vals_away, links.y)
        key_in, val_in = after(key_in, states_grad), after(val_in, states_grad)
        asked = jnp.concatenate([d_query.reshape(heads, D), key_in[8, :heads]])
        keys_away, vals_away = low_sum(keys[4:], key_in[4:8]), low_sum(vals[4:], val_in[4:])
        keys, vals = low_sum(keys[:4], key_in[:4]), low_sum(vals[:4], val_in[:4])
        key_in = move(jnp.concatenate([keys_away, asked[None]]), links.y)
        val_in = move(vals_away, links.x)
        asked = jnp.concatenate([asked, key_in[4]])
        queries = dot_tn(picked_plane, asked).astype(BF).reshape(4, part, D)
        keys, vals = low_sum(keys, key_in[:4]), low_sum(vals, val_in)
        keep = jnp.concatenate([queries, keys, vals], axis=2)
        behind = [keep]
        grad_qkv = keep[0].astype(F32)
        for c in (1, 2, 3):
            grad_qkv = grad_qkv + move(keep[c], links.z[c]).astype(F32)
    else:
        behind = []
        d_query_all = gather_rows(links, d_query.reshape(heads, D))
        sums = jnp.concatenate([outs[5][0], outs[6][0]], axis=1)
        total = lax.psum_scatter(sums, "batch", scatter_dimension=0, tiled=True).astype(F32)
    if links is not None:
        encoded = finish(first, act, behind)
    columns = lambda a, width: lax.dynamic_slice(a, (0, own * width), (every, width))
    if links is None:
        grad_query = dot_tn(columns(picked_all, part), d_query_all)
        grad_qkv = jnp.concatenate([grad_query, total], axis=1)
    gain_own = lax.dynamic_slice(d_gains, (0, own * part), (4, part))
    return (
        loss,
        encoded[None],
        states_grad[None],
        grad_qkv[None],
        grad_out[None],
        grad_in[None],
        grad_back[None],
        gain_own[0:1],
        gain_own[1:2],
        gain_own[2:3],
        gain_own[3:4],
    )


def solution(mesh):
    rows = P("tower", "batch", None, None)
    matrix = P("tower", "batch", None)
    vector = P("tower", "batch")
    return jax.shard_map(
        body,
        mesh=mesh,
        in_specs=(rows, P("batch", None), P(), P("batch"))
        + (matrix,) * 4
        + (vector,) * 4,
        out_specs=(P(), rows, rows) + (matrix,) * 4 + (vector,) * 4,
        check_vma=False,
    )
```

```python
import functools
import math

import jax
import jax.numpy as jnp
from jax import lax
from jax.experimental import pallas as pl
from jax.experimental.pallas import tpu as pltpu
from jax.sharding import PartitionSpec as P

D = 768
HEADS = 12
HEAD = 64
FF = 3072
SEQ_LEN = 256
QLEN = 64
SLOTS = 4
EPS = 1e-05
NEG = -1000000000.0
BF = jnp.bfloat16
F32 = jnp.float32
MIB = 1 << 20
HEAD_SCALE = 1.0 / math.sqrt(HEAD)
LOGIT_SCALE = 2.0 / math.sqrt(D)
CHUNKS = FF // D
VMEM = pl.BlockSpec(memory_space=pltpu.VMEM)
SMEM = pl.BlockSpec(memory_space=pltpu.SMEM)
ANY = pl.BlockSpec(memory_space=pl.ANY)


def dot(a, b):
    return lax.dot_general(a, b, (((1,), (0,)), ((), ())), preferred_element_type=F32)


def dot_nt(a, b):
    return lax.dot_general(a, b, (((1,), (1,)), ((), ())), preferred_element_type=F32)


def dot_tn(a, b):
    return lax.dot_general(a, b, (((0,), (0,)), ((), ())), preferred_element_type=F32)


def iota(shape, axis):
    return lax.broadcasted_iota(jnp.int32, shape, axis)


def normalise(summed):
    center = summed - jnp.mean(summed, axis=-1, keepdims=True)
    spread = jnp.mean(center * center, axis=-1, keepdims=True)
    scale = lax.rsqrt(spread + EPS)
    return center * scale, scale


def normalise_back(grad, hat, scale, gain):
    d_hat = grad * gain
    mean_d = jnp.mean(d_hat, axis=-1, keepdims=True)
    mean_dh = jnp.mean(d_hat * hat, axis=-1, keepdims=True)
    d_gain = jnp.sum(grad * hat, axis=0, keepdims=True)
    d_shift = jnp.sum(grad, axis=0, keepdims=True)
    return scale * (d_hat - mean_d - hat * mean_dh), d_gain, d_shift


def normal_cdf(values):
    return 0.5 * (1.0 + lax.erf(values * math.sqrt(0.5)))


def gelu(values):
    return values * normal_cdf(values)


def gelu_pair(values):
    cdf = normal_cdf(values)
    bell = jnp.exp(-0.5 * values * values) * (1.0 / math.sqrt(2.0 * math.pi))
    return values * cdf, cdf + values * bell


class Links:
    def __init__(self):
        def table(move):
            at = lambda z, y, x: z * 4 + y * 2 + x
            return [
                (at(z, y, x), at(*move(z, y, x)))
                for z in range(4)
                for y in range(2)
                for x in range(2)
            ]

        by_x = table(lambda z, y, x: (z, y, 1 - x))
        by_y = table(lambda z, y, x: (z, 1 - y, x))
        self.z = [table(lambda z, y, x, c=c: ((z + c) % 4, y, x)) for c in range(4)]
        shifted = lambda pairs: [(a + 16, b + 16) for a, b in pairs]
        self.x, self.y = by_x, by_y
        self.first = by_x + shifted(by_y)
        self.second = by_y + shifted(by_x)
        me = lax.axis_index("batch")
        self.at = (me // 4, me // 2 % 2, me % 2)
        self.question = lax.axis_index("tower") == 0

    def place(self, c, first, second):
        z, y, x = self.at
        dx = jnp.where(self.question, first, second)
        dy = jnp.where(self.question, second, first)
        return (z + c + 4) % 4 * 4 + (y ^ dy) * 2 + (x ^ dx)


def move(value, pairs):
    return lax.ppermute(value, "batch", pairs)


def move_plane(value, pairs):
    return lax.ppermute(value, ("tower", "batch"), pairs)


def after(value, *earlier):
    late = sum(other[(0,) * other.ndim].astype(F32) for other in earlier) > 1e30
    return jnp.where(late, jnp.zeros_like(value), value)


def gather_line(links, shard):
    return jnp.stack([move(shard, links.z[c]) for c in (1, 2, 3)])


def gather_plane(links, line):
    near = move_plane(line, links.first)
    side = move_plane(line, links.second)
    return [line, near, side, move_plane(near, links.second)]


CORNERS = ((0, 0), (1, 0), (0, 1), (1, 1))


class Gathered:
    def __init__(self, pieces, place, bases=None, folds=1):
        self.pieces = pieces
        self.place = place
        self.bases = bases or [0] * len(pieces)
        self.folds = folds
        self.copies = place.shape[0] * folds

    def whole(self):
        return self.pieces[0][0]


def gather_whole(shard):
    whole = lax.all_gather(shard, "batch", axis=0, tiled=True)
    return Gathered([whole[None]], jnp.zeros((1,), jnp.int32))


def gather_pieces(links, own, line, base, folds=1):
    order = [(0, f, s) for f, s in CORNERS] + [(-c, f, s) for f, s in CORNERS for c in (1, 2, 3)]
    place = jnp.stack([links.place(*at) for at in order]).astype(jnp.int32)
    return Gathered([piece[None] for piece in own] + line, place, [base] * 4 + [0] * 4, folds)


def gather_rows(links, rows, behind=None):
    if links is None:
        return lax.all_gather(rows, "batch", axis=0, tiled=True)
    z, y, x = links.at
    count, width = rows.shape
    zs = [rows] + [move(rows, links.z[c]) for c in (1, 2, 3)]
    line = jnp.concatenate([zs[3], zs[2], zs[1], zs[0], zs[3], zs[2], zs[1]])
    line = lax.dynamic_slice(line, ((3 - z) * count, 0), (4 * count, width))
    if behind is not None:
        line = after(line, behind)
    line, near, side, far = gather_plane(links, line)
    by_x, by_y = (jnp.where(links.question, *pair) for pair in ((near, side), (side, near)))
    flip = lambda at, a, b: jnp.where(at == 0, jnp.stack([a, b]), jnp.stack([b, a]))
    full = flip(y, flip(x, line, by_x), flip(x, by_y, far))
    return full.reshape(4, 4, count, width).transpose(1, 0, 2, 3).reshape(16 * count, width)


def low_sum(a, b):
    return (a.astype(F32) + b.astype(F32)).astype(BF)


def load(group, target, sems, low=0, start=True):
    place, pieces, weight = group
    width = target.shape[1]
    copies = []
    k = 0
    for piece, base in zip(pieces, weight.bases):
        for c in range(piece.shape[0]):
            unit = piece.shape[1]
            for fold in range(weight.folds):
                row = pl.multiple_of((place[k] * weight.folds + fold) * unit, unit)
                copies.append(
                    pltpu.make_async_copy(
                        piece.at[c, :, pl.ds(base + low + fold * width, width)],
                        target.at[pl.ds(row, unit), :],
                        sems.at[len(copies)],
                    )
                )
            k += 1
    for copy in copies if start else ():
        copy.start()
    return copies


def wait_all(copies):
    for copy in copies:
        copy.wait()


def launch(
    kernel, ins, weights, outs, scratch, room, grid=None, flops=0, moved=0, same=None, behind=()
):
    values = list(ins)
    for weight in weights:
        values += [(weight.place, SMEM)] + [(piece, ANY) for piece in weight.pieces]
    values += [(value, ANY) for value in behind]

    def run(*refs):
        at = len(ins)
        groups = []
        for weight in weights:
            end = at + 1 + len(weight.pieces)
            groups.append((refs[at], refs[at + 1 : end], weight))
            at = end
        at += len(behind)
        kernel(refs[: len(ins)], groups, refs[at : at + len(outs)], refs[at + len(outs) :])

    extra = {} if grid is None else {"grid": grid}
    return pl.pallas_call(
        run,
        name=getattr(kernel, "func", kernel).__name__,
        input_output_aliases=same or {},
        in_specs=[spec for _, spec in values],
        out_specs=[spec for _, _, spec in outs],
        out_shape=[jax.ShapeDtypeStruct(shape, dtype) for shape, dtype, _ in outs],
        scratch_shapes=scratch,
        compiler_params=pltpu.CompilerParams(vmem_limit_bytes=room * MIB),
        cost_estimate=pl.CostEstimate(
            flops=int(flops), bytes_accessed=int(moved), transcendentals=0
        ),
        **extra,
    )(*[value for value, _ in values])


def sems(*shape):
    return pltpu.SemaphoreType.DMA(shape)


def rows_spec(many, *tail, skip=0):
    return pl.BlockSpec((many,) + tail, lambda r: (r + skip,) + (0,) * len(tail))


def open_keys(shape, key_axis, row, slot_of_query, lens, ask):
    key_at = iota(shape, key_axis)
    slot = key_at >> 6
    limit = jnp.zeros(shape, jnp.int32)
    for s in range(SLOTS):
        limit = jnp.where(slot == s, lens[row, s] * ask + QLEN * (1 - ask), limit)
    return ((key_at & (QLEN - 1)) < limit) & (slot_of_query * ask == slot * ask)


def mix(skip, ins, groups, outs, scratch):
    lens, asking, x_ref = ins[:3]
    query_ref, key_ref, value_ref, context_ref = outs[:4]
    w, w_gain, w_turned, sem = scratch
    row = pl.program_id(0) + skip

    @pl.when(pl.program_id(0) == 0)
    def _():
        copies = load(groups[0], w, sem.at[0])
        if len(outs) > 4:
            wait_all(load(groups[0], w_gain, sem.at[1], 4 * D))
            outs[4][...] = w_gain[...].astype(F32).T[:8]
        wait_all(copies)
        for j in range(0, D, 128):
            part = w[:, 2 * D + j : 2 * D + j + 128].astype(F32)
            w_turned[j : j + 128, :] = part.T.astype(BF)

    x = x_ref[0]
    mixed = dot(x, w[:, : 2 * D])
    for s in range(SLOTS):
        query_ref[0, s : s + 1, :] = mixed[s * QLEN : s * QLEN + 1, :D]
    query = (mixed[:, :D] * HEAD_SCALE).astype(BF)
    keyset = mixed[:, D:].astype(BF)
    values = dot_nt(w_turned[...], x).astype(BF)
    key_ref[0] = keyset
    value_ref[0] = values
    shape = (SEQ_LEN, SEQ_LEN)
    closed = jnp.where(open_keys(shape, 0, row, iota(shape, 1) >> 6, lens, asking[0]), 0, 1) == 1
    ones = jnp.ones((16, SEQ_LEN), BF)
    nothing = jnp.zeros((SEQ_LEN, 128), BF)
    half_of = iota((SEQ_LEN, 128), 1) // HEAD
    scores = []
    for head in range(HEADS):
        low = head // 2 * 128
        mine = jnp.where(half_of == head % 2, query[:, low : low + 128], nothing)
        scores.append(dot_nt(keyset[:, low : low + 128], mine))
    expos = []
    for score in scores:
        score = jnp.where(closed, NEG, score)
        expos.append(jnp.exp(score - jnp.max(score, axis=0, keepdims=True)).astype(BF))
    parts = []
    for head, expo in enumerate(expos):
        mine = values[head * HEAD : head * HEAD + HEAD]
        summed = dot(jnp.concatenate([mine, ones], axis=0), expo)
        parts.append(summed[:HEAD] / summed[HEAD : HEAD + 1])
    context_ref[0] = jnp.concatenate(parts, axis=0).T.astype(BF)


def up(ins, groups, outs, scratch):
    x_ref, context_ref, gains = ins
    first_ref, act_ref = outs
    w_out, w_in, sem = scratch

    @pl.when(pl.program_id(0) == 0)
    def _():
        from_out = load(groups[0], w_out, sem.at[0], 3 * D)
        load(groups[1], w_in, sem.at[1])
        wait_all(from_out)

    many = x_ref.shape[0] * SEQ_LEN
    attended = dot(context_ref[...].reshape(many, D), w_out[...])
    summed = x_ref[...].reshape(many, D).astype(F32) + attended
    first = normalise(summed)[0] * gains[0:1] + gains[1:2]
    low = first.astype(BF)
    first_ref[...] = low.reshape(first_ref.shape)

    @pl.when(pl.program_id(0) == 0)
    def _():
        wait_all(load(groups[1], w_in, sem.at[1], start=False))

    for j in range(CHUNKS):
        part = gelu(dot(low, w_in[:, j * D : j * D + D])).astype(BF)
        act_ref[:, :, j * D : j * D + D] = part.reshape(act_ref.shape[0], SEQ_LEN, D)


def down(ins, groups, outs, scratch):
    first_ref, act_ref, gains = ins
    (encoded_ref,) = outs
    w_back, sem = scratch

    @pl.when(pl.program_id(0) == 0)
    def _():
        wait_all(load(groups[0], w_back, sem))

    many = first_ref.shape[0] * SEQ_LEN
    summed = dot(act_ref[...].reshape(many, FF), w_back[...])
    hat = normalise(first_ref[...].reshape(many, D).astype(F32) + summed)[0]
    encoded_ref[...] = (hat * gains[2:3] + gains[3:4]).astype(BF).reshape(encoded_ref.shape)


def head_up_math(context, picked, gains, w_out, w_in, emit):
    hat, scale = normalise(picked.astype(F32) + dot(context, w_out))
    low = (hat * gains[0:1] + gains[1:2]).astype(BF)
    for j in range(CHUNKS):
        act, slope = gelu_pair(dot(low, w_in(j)))
        emit(j, act.astype(BF), slope.astype(BF))
    return hat, scale, low


def head_up(ins, groups, outs, scratch):
    context_ref, picked_ref, gains = ins
    hat_ref, scale_ref, low_ref, act_ref, slope_ref = outs
    w_out, w_in, sem = scratch
    from_out = load(groups[0], w_out, sem.at[0], 3 * D)
    from_in = load(groups[1], w_in, sem.at[1])
    wait_all(from_out)

    def in_part(j):
        if j == 0:
            wait_all(from_in)
        return w_in[:, j * D : j * D + D]

    def emit(j, act, slope):
        act_ref[:, j * D : j * D + D] = act
        slope_ref[:, j * D : j * D + D] = slope

    hat, scale, low = head_up_math(
        context_ref[...],
        picked_ref[...],
        gains[...],
        w_out[...],
        in_part,
        emit,
    )
    hat_ref[...] = hat
    scale_ref[...] = jnp.broadcast_to(scale, scale_ref.shape)
    low_ref[...] = low


def head_down_math(hat, gains, act, w_back):
    hat2, scale2 = normalise(hat * gains[0:1] + gains[1:2] + dot(act, w_back))
    return hat2, scale2, (hat2 * gains[2:3] + gains[3:4]).astype(BF)


def head_down(ins, groups, outs, scratch):
    hat_ref, act_ref, gains = ins
    hat2_ref, scale2_ref, final_ref = outs
    w_back, sem = scratch
    wait_all(load(groups[0], w_back, sem))
    hat2, scale2, final = head_down_math(hat_ref[...], gains[...], act_ref[...], w_back[...])
    hat2_ref[...] = hat2
    scale2_ref[...] = jnp.broadcast_to(scale2, scale2_ref.shape)
    final_ref[...] = final


def logit_back(asked, passages, positives, ids, place_of):
    logits = dot_nt(asked, passages) * LOGIT_SCALE
    chosen = positives == place_of
    asked_data = jnp.sum(jnp.where(chosen, ids, 0.0), axis=1, keepdims=True)
    open_to = (asked_data == ids) & (place_of >= 0)
    masked = jnp.where(open_to, logits, NEG)
    highest = jnp.max(masked, axis=1, keepdims=True)
    expo = jnp.exp(masked - highest)
    total = jnp.sum(expo, axis=1, keepdims=True)
    target = jnp.sum(jnp.where(chosen, logits, 0.0), axis=1, keepdims=True)
    loss = jnp.sum(highest + jnp.log(total) - target, axis=0, keepdims=True) / asked.shape[0]
    d_logits = (expo / total - jnp.where(chosen, 1.0, 0.0)) * (LOGIT_SCALE / asked.shape[0])
    return loss, d_logits


def dot_split(a, b):
    high = a.astype(BF)
    return dot(high, b) + dot((a - high.astype(F32)).astype(BF), b)


def back_math(d_final, hat2, scale2, hat, scale, gains, slope, w_out, w_in, w_back, emit):
    d_second, d_gain2, d_shift2 = normalise_back(d_final, hat2, scale2, gains[2:3])
    d_down = d_second.astype(BF)
    d_first = d_second
    for j in range(CHUNKS):
        d_up = (dot_nt(d_down, w_back(j)) * slope(j).astype(F32)).astype(BF)
        emit(j, d_up)
        d_first = d_first + dot_nt(d_up, w_in(j))
    d_sum, d_gain, d_shift = normalise_back(d_first, hat, scale, gains[0:1])
    d_att = d_sum.astype(BF)
    d_context = None if w_out is None else dot_nt(d_att, w_out())
    return d_down, d_sum, d_att, d_context, (d_gain, d_shift, d_gain2, d_shift2)


def head_back(ins, groups, outs, scratch):
    asking, own, mine_ref, other_ref, positives, ids, place_of, gains = ins[:8]
    hat2_ref, scale2_ref, hat_ref, scale_ref, slope_ref = ins[8:13]
    act_part, low_part, context_part = ins[13:]
    loss_ref, context_ref, sum_ref, gain_ref, grad_out, grad_in, grad_back = outs
    w_out, w_in, w_back, d_ups, keep_sum, keep_context, near, slopes, near_sem, sem = scratch
    from_near = [
        pltpu.make_async_copy(ref, near.at[k, :, pl.ds(0, ref.shape[1])], near_sem.at[k])
        for k, ref in enumerate((hat2_ref, scale2_ref, hat_ref, scale_ref))
    ]
    from_near.append(pltpu.make_async_copy(slope_ref, slopes, near_sem.at[4]))
    for copy in from_near:
        copy.start()
    from_back = load(groups[2], w_back, sem.at[0])
    from_in = load(groups[1], w_in, sem.at[1])
    from_out = load(groups[0], w_out, sem.at[2], 3 * D)
    rows = mine_ref.shape[0]
    is_asking = jnp.full((rows, D), asking[0]) == 1
    mine, other = mine_ref[...], other_ref[...]
    loss, d_logits = logit_back(
        jnp.where(is_asking, mine, other),
        jnp.where(is_asking, other, mine),
        positives[...],
        ids[...],
        place_of[...],
    )
    loss_ref[...] = jnp.broadcast_to(loss, loss_ref.shape)
    square = jnp.full((rows, rows), asking[0]) == 1
    d_final = dot_split(jnp.where(square, d_logits, d_logits.T), other)
    wait_all(from_near + from_back)

    def in_part(j):
        if j == 0:
            wait_all(from_in)
        return w_in[:, j * D : j * D + D]

    def out_whole():
        wait_all(from_out)
        return w_out[...]

    def emit(j, d_up):
        d_ups[:, j * D : j * D + D] = d_up

    d_down, d_sum, d_att, d_context, d_gains = back_math(
        d_final,
        near[0],
        near[1, :, :1],
        near[2],
        near[3, :, :1],
        gains[...],
        lambda j: slopes[:, j * D : j * D + D],
        out_whole,
        in_part,
        lambda j: w_back[j * D : j * D + D, :],
        emit,
    )
    for i, d_gain in enumerate(d_gains):
        gain_ref[i : i + 1, :] = d_gain
    keep_sum[...] = d_sum
    keep_context[...] = d_context
    count = sum_ref.shape[0] * SLOTS
    at = pl.ds(pl.multiple_of(own[0] * count, 8), count)
    own_sum, own_context = keep_sum[at, :], keep_context[at, :]
    for r in range(sum_ref.shape[0]):
        sum_ref[r] = own_sum[r * SLOTS : r * SLOTS + SLOTS]
        context_ref[r] = own_context[r * SLOTS : r * SLOTS + SLOTS]
    grad_back[...] = dot_tn(act_part[...], d_down)
    grad_in[...] = dot_tn(low_part[...], d_ups[...])
    grad_out[...] = dot_tn(context_part[...], d_att)


WIDE = HEADS * SLOTS


def spread_heads(four):
    eight = jnp.concatenate([four, four], axis=0)
    tall = jnp.concatenate([eight] * (HEADS // 2), axis=0)
    return jnp.where(own_head(), tall, 0.0)


def own_head():
    shape = (WIDE, D)
    return iota(shape, 0) // SLOTS == iota(shape, 1) // HEAD


def attend_back(ins, groups, outs, scratch):
    source, lens, asking, x_ref, picked_ref, key_ref, value_ref, context_ref = ins
    probs_ref, score_ref, query_ref, wide_ref, d_query_ref = outs[:5]
    sum_refs = outs[5:]
    seen, full, total, asked = scratch
    step = pl.program_id(0)
    many = x_ref.shape[0]
    shape = (WIDE, SEQ_LEN)
    every = range(many)
    slot_of = iota(shape, 0) & (SLOTS - 1)
    valid = [open_keys(shape, 1, step * many + i, slot_of, lens, asking[0]) for i in every]
    query = [spread_heads(picked_ref[i]).astype(BF) for i in every]
    d_context = [spread_heads(context_ref[i]).astype(BF) for i in every]
    score = [dot_nt(query[i], key_ref[i]) * HEAD_SCALE for i in every]
    d_probs = [dot(d_context[i], value_ref[i]) for i in every]
    probs, d_score = [], []
    for i in every:
        masked = jnp.where(valid[i], score[i], NEG)
        expo = jnp.exp(masked - jnp.max(masked, axis=-1, keepdims=True))
        prob = expo / jnp.sum(expo, axis=-1, keepdims=True)
        spread = jnp.sum(d_probs[i] * prob, axis=-1, keepdims=True)
        probs.append(prob.astype(BF))
        d_score.append((prob * (d_probs[i] - spread)).astype(BF))
    for i in every:
        probs_ref[i] = probs[i]
        score_ref[i] = d_score[i]
        query_ref[i] = query[i]
        wide_ref[i] = d_context[i]
    d_query = [dot(d_score[i], key_ref[i]) * HEAD_SCALE for i in every]
    by_key = [(dot(d_score[i], x_ref[i]) * HEAD_SCALE).astype(BF) for i in every]
    by_val = [dot(probs[i], x_ref[i]).astype(BF) for i in every]
    fours = []
    for i in every:
        kept = jnp.where(own_head(), d_query[i], 0.0)
        eight = kept[0:8]
        for j in range(8, WIDE, 8):
            eight = eight + kept[j : j + 8]
        fours.append(eight[:SLOTS] + eight[SLOTS:])
        d_query_ref[i] = fours[i].astype(BF)
        at = pl.ds(pl.multiple_of((step * many + i) * WIDE, 16), WIDE)
        seen[0, at, :] = by_key[i]
        seen[1, at, :] = by_val[i]
        full[0, at, :] = query[i]
        full[1, at, :] = d_context[i]

    asked[pl.ds(pl.multiple_of(step * 8, 8), 8), :] = jnp.concatenate(fours, axis=0)

    @pl.when(step == pl.num_programs(0) - 1)
    def _():
        for which in range(2):
            total[...] = dot_tn(seen[which], full[which]).astype(BF)
            k = 0
            for out_ref in sum_refs[which::2]:
                blocks, unit = out_ref.shape[0], out_ref.shape[1]
                for i in range(min(blocks, 8)):
                    at = pl.multiple_of(source[which, k] * unit, unit)
                    out_ref[i] = total[pl.ds(at, unit), :]
                    k += 1
        if len(sum_refs) > 2:
            spare = jnp.zeros((sum_refs[2].shape[1] - asked.shape[0], D), F32)
            sum_refs[2][8] = jnp.concatenate([asked[...], spare], axis=0).astype(BF)


def states_back(ins, groups, outs, scratch):
    probs_ref, score_ref, query_ref, wide_ref, d_query_ref, d_sum_ref = ins
    (grad_ref,) = outs
    w, sem = scratch

    @pl.when(pl.program_id(0) == 0)
    def _():
        wait_all(load(groups[0], w, sem))

    many = grad_ref.shape[0]
    every = range(many)
    tall = many * WIDE
    by_key = (dot_nt(query_ref[...].reshape(tall, D), w[:, D : 2 * D]) * HEAD_SCALE).astype(BF)
    by_val = dot_nt(wide_ref[...].reshape(tall, D), w[:, 2 * D :]).astype(BF)
    fours = [d_query_ref[i].astype(F32) for i in every]
    extra = dot_nt(jnp.concatenate(fours, axis=0).astype(BF), w[:, :D])
    for i in every:
        rows = slice(i * WIDE, i * WIDE + WIDE)
        grad_ref[i] = dot_tn(score_ref[i], by_key[rows]) + dot_tn(probs_ref[i], by_val[rows])
        for s in range(SLOTS):
            at = slice(s * QLEN, s * QLEN + 1)
            add = extra[i * SLOTS + s : i * SLOTS + s + 1] + d_sum_ref[i, s : s + 1]
            grad_ref[i, at, :] = grad_ref[i, at, :] + add


def body(
    states,
    q_lengths,
    dataset_ids,
    positives,
    w_qkv,
    w_out,
    w_in,
    w_back,
    gain_first,
    bias_first,
    gain_second,
    bias_second,
):
    devices = lax.axis_size("batch")
    links = Links() if devices == 16 else None
    own = lax.axis_index("batch")
    is_asking = lax.axis_index("tower") == 0
    asking = is_asking.astype(jnp.int32).reshape(1)
    inputs = states[0]
    rows = inputs.shape[0]
    heads = rows * SLOTS
    every = heads * devices
    part = w_qkv.shape[1]
    back_part = w_back.shape[1]

    vectors = jnp.concatenate([gain_first, bias_first, gain_second, bias_second], axis=0)
    vectors = jnp.pad(vectors.T, ((0, 0), (0, 124)))
    first_needed = jnp.concatenate([w_qkv[0], w_out[0], vectors], axis=1)
    if links is not None:
        folded = jnp.concatenate(jnp.split(w_back[0], CHUNKS, axis=0), axis=1)
        mix_line = gather_line(links, first_needed)
        mix_own = gather_plane(links, first_needed)
        later = jnp.concatenate([w_in[0], folded], axis=1)
        later_own = gather_plane(links, after(later, mix_own[1], mix_own[2]))
        mix_pieces = gather_plane(links, mix_line)
        in_line = gather_line(links, after(w_in[0], mix_line))
        in_pieces = gather_plane(links, after(in_line, mix_pieces[3]))
        g_mix = gather_pieces(links, mix_own, mix_pieces, 0)
        g_in = gather_pieces(links, later_own, in_pieces, 0)
    else:
        g_mix, g_in, g_back = (
            gather_whole(weight) for weight in (first_needed, w_in[0], w_back[0])
        )

    two = functools.partial(rows_spec, 2)
    half = rows // 2
    mixed = []
    for skip in (0, half):
        at = functools.partial(rows_spec, 1, skip=skip)
        kept = [
            ((rows, SLOTS, D), F32, at(SLOTS, D)),
            ((rows, SEQ_LEN, D), BF, at(SEQ_LEN, D)),
            ((rows, D, SEQ_LEN), BF, at(D, SEQ_LEN)),
            ((rows, SEQ_LEN, D), BF, at(SEQ_LEN, D)),
        ]
        behind = []
        if links is not None:
            behind = in_pieces[1:3] if skip else []
        if skip:
            mixed, gains = mixed[:4], mixed[4]
            if links is not None:
                back_line = gather_line(links, after(folded, gains))
        mixed = launch(
            functools.partial(mix, skip),
            [(q_lengths, SMEM), (asking, SMEM), (inputs, at(SEQ_LEN, D))]
            + [(value, ANY) for value in mixed],
            [g_mix],
            kept if skip else kept + [((8, D), F32, VMEM)],
            [
                pltpu.VMEM((D, 3 * D), BF),
                pltpu.VMEM((D, 128), BF),
                pltpu.VMEM((D, D), BF),
                sems(2, g_mix.copies),
            ],
            room=60,
            grid=(half,),
            flops=2 * half * SEQ_LEN * D * (3 * D + 4 * SEQ_LEN),
            moved=10 * MIB,
            same={3 + k: k for k in range(4)} if skip else None,
            behind=behind,
        )
    query, key, value, context = mixed
    picked = inputs.reshape(rows, SLOTS, QLEN, D)[:, :, 0].reshape(heads, D)
    context_own = context.reshape(rows, SLOTS, QLEN, D)[:, :, 0].reshape(heads, D)
    index = positives[:, None]
    note = jnp.pad(jnp.concatenate([index // 256, index % 256], axis=1), ((0, 0), (0, 126)))
    parcel = jnp.concatenate([context_own, picked, note.astype(BF)], axis=1)
    if links is not None:
        parcel = after(parcel, in_pieces[3])
        back_pieces = gather_plane(links, after(back_line, context))
        g_back = gather_pieces(links, later_own, back_pieces, FF, CHUNKS)
    shared = gather_rows(links, parcel)
    context_all, picked_all = shared[:, :D], shared[:, D : 2 * D]
    if links is not None:
        z, y, x = links.at
        plane = lax.dynamic_slice(picked_all, (z * 4 * heads, 0), (4 * heads, D))
        plane = plane.reshape(2, 2, heads, D)
        plane = jnp.where(y == 0, plane, plane[::-1])
        plane = jnp.where(x == 0, plane, plane[:, ::-1]).reshape(4 * heads, 4, 4, part)
        plane = lax.dynamic_slice(plane, (0, 0, own % 4, 0), (4 * heads, 4, 1, part))
        plane = jnp.concatenate([plane, plane], axis=1)
        plane = lax.dynamic_slice(plane, (0, z, 0, 0), (4 * heads, 4, 1, part))
        picked_plane = plane.reshape(4 * heads, 4 * part)
    noted = shared[:, 2 * D : 2 * D + 2].astype(jnp.int32)
    positives_all = noted[:, :1] * 256 + noted[:, 1:]

    def finish(first, act, behind):
        (encoded,) = launch(
            down,
            [(first, two(SEQ_LEN, D)), (act, two(SEQ_LEN, FF)), (gains, VMEM)],
            [g_back],
            [((rows, SEQ_LEN, D), BF, two(SEQ_LEN, D))],
            [pltpu.VMEM((FF, D), BF), sems(g_back.copies)],
            room=60,
            grid=(rows // 2,),
            flops=2 * rows * SEQ_LEN * D * FF,
            moved=24 * MIB,
            behind=behind,
        )
        return encoded

    if links is not None:
        first, act = launch(
            up,
            [(inputs, two(SEQ_LEN, D)), (context, two(SEQ_LEN, D)), (gains, VMEM)],
            [g_mix, g_in],
            [
                ((rows, SEQ_LEN, D), BF, two(SEQ_LEN, D)),
                ((rows, SEQ_LEN, FF), BF, two(SEQ_LEN, FF)),
            ],
            [pltpu.VMEM((D, D), BF), pltpu.VMEM((D, FF), BF), sems(2, g_mix.copies)],
            room=40,
            grid=(rows // 2,),
            flops=2 * rows * SEQ_LEN * D * (D + FF),
            moved=30 * MIB,
        )

        hat, scale, low, head_act, slope = launch(
            head_up,
            [(context_all, VMEM), (picked_all, VMEM), (gains, VMEM)],
            [g_mix, g_in],
            [
                ((every, D), F32, VMEM),
                ((every, 128), F32, VMEM),
                ((every, D), BF, VMEM),
                ((every, FF), BF, VMEM),
                ((every, FF), BF, VMEM),
            ],
            [pltpu.VMEM((D, D), BF), pltpu.VMEM((D, FF), BF), sems(2, g_mix.copies)],
            room=36,
            flops=2 * every * D * (D + FF),
            moved=14 * MIB,
            behind=[act],
        )
        hat2, scale2, final = launch(
            head_down,
            [(hat, VMEM), (head_act, VMEM), (gains, VMEM)],
            [g_back],
            [((every, D), F32, VMEM), ((every, 128), F32, VMEM), ((every, D), BF, VMEM)],
            [pltpu.VMEM((FF, D), BF), sems(g_back.copies)],
            room=24,
            flops=2 * every * D * FF,
            moved=10 * MIB,
        )
    else:
        first, act = launch(
            up,
            [(inputs, two(SEQ_LEN, D)), (context, two(SEQ_LEN, D)), (gains, VMEM)],
            [g_mix, g_in],
            [
                ((rows, SEQ_LEN, D), BF, two(SEQ_LEN, D)),
                ((rows, SEQ_LEN, FF), BF, two(SEQ_LEN, FF)),
            ],
            [pltpu.VMEM((D, D), BF), pltpu.VMEM((D, FF), BF), sems(2, g_mix.copies)],
            room=40,
            grid=(rows // 2,),
            flops=2 * rows * SEQ_LEN * D * (D + FF),
            moved=30 * MIB,
        )

        encoded = finish(first, act, [])
        context_all = after(context_all, encoded)
        out_full = g_mix.whole()[:, 3 * D : 4 * D]
        in_full, back_full = g_in.whole(), g_back.whole()
        acts, slopes = [], []

        def emit(j, act_part, slope_part):
            acts.append(act_part)
            slopes.append(slope_part)

        hat, scale, low = head_up_math(
            context_all,
            picked_all,
            gains,
            out_full,
            lambda j: in_full[:, j * D : j * D + D],
            emit,
        )
        head_act = jnp.concatenate(acts, axis=1)
        hat2, scale2, final = head_down_math(hat, gains, head_act, back_full)

    other = lax.ppermute(final, "tower", [(0, 1), (1, 0)])
    if links is not None:
        column = jnp.arange(every, dtype=jnp.int32)[None]
        place_of = jnp.where(column % SLOTS == 0, column // SLOTS, -1)
        ids = jnp.repeat(dataset_ids.astype(F32), SLOTS)[None]
        columns = lambda a, width: lax.dynamic_slice(a, (0, own * width), (every, width))
        loss, d_context, d_sum, d_gains, grad_out, grad_in, grad_back = launch(
            head_back,
            [
                (asking, SMEM),
                (own.astype(jnp.int32).reshape(1), SMEM),
                (final, VMEM),
                (other, VMEM),
                (positives_all, VMEM),
                (ids, VMEM),
                (place_of, VMEM),
                (gains, VMEM),
                (hat2, ANY),
                (scale2, ANY),
                (hat, ANY),
                (scale, ANY),
                (slope, ANY),
                (columns(head_act, back_part), VMEM),
                (columns(low, part), VMEM),
                (columns(context_all, part), VMEM),
            ],
            [g_mix, g_in, g_back],
            [
                ((8, 128), F32, VMEM),
                ((rows, SLOTS, D), F32, VMEM),
                ((rows, SLOTS, D), F32, VMEM),
                ((8, D), F32, VMEM),
                ((part, D), F32, VMEM),
                ((part, FF), F32, VMEM),
                ((back_part, D), F32, VMEM),
            ],
            [
                pltpu.VMEM((D, D), BF),
                pltpu.VMEM((D, FF), BF),
                pltpu.VMEM((FF, D), BF),
                pltpu.VMEM((every, FF), BF),
                pltpu.VMEM((every, D), F32),
                pltpu.VMEM((every, D), F32),
                pltpu.VMEM((4, every, D), F32),
                pltpu.VMEM((every, FF), BF),
                sems(5),
                sems(3, g_back.copies),
            ],
            room=48,
            flops=2 * every * D * (2 * FF + 3 * D),
            moved=20 * MIB,
        )
        loss = loss[0, 0]
    else:
        passages = jnp.where(is_asking, other, final)[::SLOTS]
        asked = jnp.where(is_asking, final, other)
        loss, d_logits = logit_back(
            asked,
            passages,
            positives_all,
            dataset_ids.astype(F32)[None],
            jnp.arange(passages.shape[0], dtype=jnp.int32)[None],
        )
        loss = loss[0, 0]
        d_asked = dot_split(d_logits, passages)
        d_passages = dot_split(d_logits.T, asked)
        spaced = jnp.pad(d_passages[:, None], ((0, 0), (0, SLOTS - 1), (0, 0)))
        d_ups = []
        d_down, d_sum, d_att, d_context, d_gains = back_math(
            jnp.where(is_asking, d_asked, spaced.reshape(every, D)),
            hat2,
            scale2,
            hat,
            scale,
            gains,
            lambda j: slopes[j],
            lambda: out_full,
            lambda j: in_full[:, j * D : j * D + D],
            lambda j: back_full[j * D : j * D + D],
            lambda j, d_up_part: d_ups.append(d_up_part),
        )
        d_up = jnp.concatenate(d_ups, axis=1)
        d_gains = jnp.concatenate(d_gains, axis=0)
        columns = lambda a, width: lax.dynamic_slice(a, (0, own * width), (every, width))
        grad_back = dot_tn(columns(head_act, back_part), d_down)
        grad_in = dot_tn(columns(low, part), d_up)
        grad_out = dot_tn(columns(context_all, part), d_att)
        d_context = after(d_context, grad_back, grad_in, grad_out)
        own_rows = lambda a: lax.dynamic_slice(a, (own * heads, 0), (heads, D))
        d_sum = own_rows(d_sum).reshape(rows, SLOTS, D)
        d_context = own_rows(d_context).reshape(rows, SLOTS, D)

    if links is not None:
        z, y, x = links.at
        where = lambda c, dx, dy: (z + c) % 4 * 4 + (y ^ dy) * 2 + (x ^ dx)
        order = [(c, far, near) for far in range(2) for near in range(2) for c in range(4)]
        source = [[where(c, a, b) for c, a, b in order], [where(c, b, a) for c, a, b in order]]
        source = jnp.stack([jnp.stack(row) for row in source]).astype(jnp.int32)
        sums = [((8, part, D), BF, VMEM)] * 4
        sums[2] = ((9, part, D), BF, VMEM)
    else:
        source = jnp.zeros((2, 1), jnp.int32)
        sums = [((1, D, D), BF, VMEM)] * 2
    outs = launch(
        attend_back,
        [
            (source, SMEM),
            (q_lengths, SMEM),
            (asking, SMEM),
            (inputs, two(SEQ_LEN, D)),
            (query, two(SLOTS, D)),
            (key, two(SEQ_LEN, D)),
            (value, two(D, SEQ_LEN)),
            (d_context, two(SLOTS, D)),
        ],
        [],
        [
            ((rows, WIDE, SEQ_LEN), BF, two(WIDE, SEQ_LEN)),
            ((rows, WIDE, SEQ_LEN), BF, two(WIDE, SEQ_LEN)),
            ((rows, WIDE, D), BF, two(WIDE, D)),
            ((rows, WIDE, D), BF, two(WIDE, D)),
            ((rows, SLOTS, D), BF, two(SLOTS, D)),
        ]
        + sums,
        [
            pltpu.VMEM((2, rows * WIDE, D), BF),
            pltpu.VMEM((2, rows * WIDE, D), BF),
            pltpu.VMEM((D, D), BF),
            pltpu.VMEM((heads, D), F32),
        ],
        room=60,
        grid=(rows // 2,),
        flops=2 * rows * WIDE * D * (5 * SEQ_LEN + 2 * D),
        moved=16 * MIB,
    )
    low_probs, low_score, wide_query, wide_context, d_query = outs[:5]
    (states_grad,) = launch(
        states_back,
        [
            (low_probs, two(WIDE, SEQ_LEN)),
            (low_score, two(WIDE, SEQ_LEN)),
            (wide_query, two(WIDE, D)),
            (wide_context, two(WIDE, D)),
            (d_query, two(SLOTS, D)),
            (d_sum, two(SLOTS, D)),
        ],
        [g_mix],
        [((rows, SEQ_LEN, D), F32, two(SEQ_LEN, D))],
        [pltpu.VMEM((D, 3 * D), BF), sems(g_mix.copies)],
        room=60,
        grid=(rows // 2,),
        flops=2 * rows * WIDE * D * (3 * D + 2 * SEQ_LEN),
        moved=12 * MIB,
    )
    if links is not None:
        keys, vals, keys_away, vals_away = outs[5:]
        key_in, val_in = move(keys_away, links.x), move(vals_away, links.y)
        key_in, val_in = after(key_in, states_grad), after(val_in, states_grad)
        asked = jnp.concatenate([d_query.reshape(heads, D), key_in[8, :heads]])
        keys_away, vals_away = low_sum(keys[4:], key_in[4:8]), low_sum(vals[4:], val_in[4:])
        keys, vals = low_sum(keys[:4], key_in[:4]), low_sum(vals[:4], val_in[:4])
        key_in = move(jnp.concatenate([keys_away, asked[None]]), links.y)
        val_in = move(vals_away, links.x)
        asked = jnp.concatenate([asked, key_in[4]])
        queries = dot_tn(picked_plane, asked).astype(BF).reshape(4, part, D)
        keys, vals = low_sum(keys, key_in[:4]), low_sum(vals, val_in)
        keep = jnp.concatenate([queries, keys, vals], axis=2)
        behind = [keep]
        grad_qkv = keep[0].astype(F32)
        for c in (1, 2, 3):
            grad_qkv = grad_qkv + move(keep[c], links.z[c]).astype(F32)
    else:
        behind = []
        d_query_all = gather_rows(links, d_query.reshape(heads, D))
        sums = jnp.concatenate([outs[5][0], outs[6][0]], axis=1)
        total = lax.psum_scatter(sums, "batch", scatter_dimension=0, tiled=True).astype(F32)
    if links is not None:
        encoded = finish(first, act, behind)
    columns = lambda a, width: lax.dynamic_slice(a, (0, own * width), (every, width))
    if links is None:
        grad_query = dot_tn(columns(picked_all, part), d_query_all)
        grad_qkv = jnp.concatenate([grad_query, total], axis=1)
    gain_own = lax.dynamic_slice(d_gains, (0, own * part), (4, part))
    return (
        loss,
        encoded[None],
        states_grad[None],
        grad_qkv[None],
        grad_out[None],
        grad_in[None],
        grad_back[None],
        gain_own[0:1],
        gain_own[1:2],
        gain_own[2:3],
        gain_own[3:4],
    )


def solution(mesh):
    rows = P("tower", "batch", None, None)
    matrix = P("tower", "batch", None)
    vector = P("tower", "batch")
    return jax.shard_map(
        body,
        mesh=mesh,
        in_specs=(rows, P("batch", None), P(), P("batch"))
        + (matrix,) * 4
        + (vector,) * 4,
        out_specs=(P(), rows, rows) + (matrix,) * 4 + (vector,) * 4,
        check_vma=False,
    )
```
